256 devices in a mesh: row: 8 (over x_lo, y), col: 16 (over z, core), layer: 2 (over x_hi).
Axes of the slice: x: 4 (x_hi: 2, x_lo: 2; x = x_hi * 2 + x_lo), y: 4, z: 8, core: 2. Of those that a mesh axis runs over, the one named last changes fastest.
Arguments:
- density: float32 [4096, 4096], P('row', ('col', 'layer')), may hold values from -1 to 1, as said below
- pattern: int32 [32, 32], replicated, may hold values from 0 to 1, as said below
Outputs:
- purified: float32 [4096, 4096], P('row', ('col', 'layer'))
The draws below stay inside these ranges and needn't reach their ends.
Inputs may be any that keep to these rules, and one draw needn't show every extreme that they name: pattern is symmetric, with ones on its diagonal; its entries are 0 or 1. density is symmetric.
All inputs are finite; a program needn't handle non-finite values.
Results may differ from the reference program's by a relative error of at most 0.00018.
Values sent between devices are 32-bit elements; how exact they have to be, the bound alone decides.
No kernel may reach another device: no remote copies, remote signals or barrier semaphores. Data moves between devices by JAX's collectives and lax.ppermute only.
A program may use at most 64 MiB of HBM per device.

```python
import jax
import jax.numpy as jnp
from jax import lax

BS = 128
ITERS = 2
N = 4096
NB = 32


def draw_pattern(key, part):
    key = jax.random.fold_in(key, 11)
    key_weight, key_cells = jax.random.split(key)
    index_line = jnp.arange(NB, dtype=jnp.int32)
    distance = jnp.abs(index_line[:, None] - index_line[None, :])
    distance = jnp.minimum(distance, NB - distance)
    weights = jax.random.randint(key_weight, (NB,), 1, 5, dtype=jnp.int32)
    base_level = jnp.maximum(30, 700 - 700 * 4 * distance // NB)
    threshold = base_level * (weights[:, None] + weights[None, :]) // 8
    drawn = jax.random.randint(key_cells, (NB, NB), 0, 1000, dtype=jnp.int32)
    upper = (drawn < threshold).astype(jnp.int32)
    symmetric = jnp.where(index_line[:, None] < index_line[None, :], upper, upper.T)
    return jnp.where(distance == 0, 1, symmetric).astype(jnp.int32)


def draw_density(key, part):
    key = jax.random.fold_in(key, 23)
    key_off, key_diag = jax.random.split(key, 2)
    sigma = 0.3 / jnp.sqrt(0.6 * N)
    raw = jax.random.normal(key_off, (N, N), jnp.float32)
    off_part = (raw + raw.T) * sigma
    diagonal = jax.random.uniform(key_diag, (N,), jnp.float32, 0.3, 0.7)
    index_line = jnp.arange(N, dtype=jnp.int32)
    same = index_line[:, None] == index_line[None, :]
    return jnp.clip(jnp.where(same, diagonal[:, None], off_part), -1.0, 1.0).astype(jnp.float32)


def setup_inputs(seed: int = 0) -> dict:
    seeds = jax.random.split(jax.random.key(seed), 3)
    return {
        "density": draw_density(jax.random.fold_in(seeds[2], 71), 0),
        "pattern": draw_pattern(jax.random.fold_in(seeds[2], 71), 0),
    }


def expand(pattern):
    occupied = pattern.astype(jnp.float32)
    return jnp.repeat(jnp.repeat(occupied, BS, axis=0), BS, axis=1)


def reference(density, pattern):
    in_pattern = expand(pattern)
    current = in_pattern * density
    for iteration in range(ITERS):
        squared = in_pattern * jnp.dot(current, current, precision=lax.Precision.HIGHEST, preferred_element_type=jnp.float32)
        cube_term = in_pattern * jnp.dot(current, squared, precision=lax.Precision.HIGHEST, preferred_element_type=jnp.float32)
        current = 3.0 * squared - 2.0 * cube_term
    return current
```

```python
import jax
import jax.numpy as jnp
from jax import lax
from jax.experimental import pallas as pl
from jax.experimental.pallas import tpu as pltpu
from jax.sharding import PartitionSpec as P

BS = 128
ITERS = 2
NB = 32
CAP = 4
NS = NB * CAP
ROUNDS = 8
ZERO = 2 * NS
S_CAP = 104
D_CAP = 80
E_CAP = NB
PAIRS = 256
UNROLL = 4
LIST = 2 * PAIRS + 2 * UNROLL + 8
NZ, NC = 8, 2
NX, NY = 4, 4
SHARD = CAP * BS // 8
PART = SHARD // NC
UNIT = NZ * NC * PART
PANEL = 4 * UNIT
RAW_HALF = 4 * PANEL
WIDE = 40
F32 = jnp.float32
BF16 = jnp.bfloat16


def panel_cols(tile, layers):
    row_count, shard_cols = tile.shape
    gathered = lax.all_gather(tile, "row", axis=0, tiled=True)
    pieces = gathered.reshape(
        gathered.shape[0] // (shard_cols * layers), layers, shard_cols, shard_cols
    )
    arranged = lax.all_to_all(pieces, "layer", split_axis=1, concat_axis=3, tiled=True)
    return arranged.reshape(-1, layers * shard_cols)


def multiply(left_tile, right_panel):
    partial_sum = jnp.dot(
        lax.all_gather(left_tile, "col", axis=1, tiled=True),
        right_panel,
        precision=lax.Precision.HIGHEST,
        preferred_element_type=jnp.float32,
    )
    return lax.psum_scatter(partial_sum, "layer", scatter_dimension=1, tiled=True)


def dense_plan(density, pattern):
    row_index = lax.axis_index("row")
    col_index = lax.axis_index("col")
    layer_index = lax.axis_index("layer")
    layers = lax.axis_size("layer")
    row_count, shard_cols = density.shape
    blocks = pattern.shape[0]
    block_line = jnp.arange(blocks, dtype=jnp.int32)
    row_ids = (row_index * row_count + jnp.arange(row_count, dtype=jnp.int32)) // BS
    col_ids = (
        (col_index * layers + layer_index) * shard_cols + jnp.arange(shard_cols, dtype=jnp.int32)
    ) // BS
    pick_rows = (row_ids[:, None] == block_line[None, :]).astype(jnp.float32)
    pick_cols = (col_ids[:, None] == block_line[None, :]).astype(jnp.float32)
    occupied = pattern.astype(jnp.float32)
    in_pattern = jnp.dot(
        jnp.dot(pick_rows, occupied, precision=lax.Precision.HIGHEST),
        pick_cols.T,
        precision=lax.Precision.HIGHEST,
    )
    current = in_pattern * density
    for iteration in range(ITERS):
        current_panel = panel_cols(current, layers)
        squared = in_pattern * multiply(current, current_panel)
        cube_term = in_pattern * multiply(current, panel_cols(squared, layers))
        current = 3.0 * squared - 2.0 * cube_term
    return current


def here():
    row = lax.axis_index("row").astype(jnp.int32)
    column = lax.axis_index("col") * lax.axis_size("layer") + lax.axis_index("layer")
    return row, column.astype(jnp.int32)


def ring_place(source, at):
    back = (at - source) & 3
    return jnp.where(back == 3, 2, jnp.where(back == 2, 3, back))


def raw_row(column, p, h, j, r):
    px = ring_place((column & 1) * 2 + (p >> 2), (j & 1) * 2 + (r >> 2))
    py = ring_place(p & 3, r & 3)
    near, far = ((px, py), (py, px))[h]
    other = jnp.where(((j >> 1) & 1) == h, 0, 1)
    return other * RAW_HALF + far * PANEL + near * UNIT + (column >> 1) * PART


def pack_kernel(pat_ref, tile_ref, packed_ref, own_ref, own_t_ref, rank_ref):
    r, j = here()
    K = (pat_ref[...] != 0).astype(F32)
    ii = lax.broadcasted_iota(jnp.int32, (NB, NB), 0)
    jj = lax.broadcasted_iota(jnp.int32, (NB, NB), 1)
    diag = (ii == jj).astype(F32)
    left = K * (1.0 - diag)
    own = diag
    own_t = diag
    after = (ii > jj).astype(F32)
    before = (ii < jj).astype(F32)
    for _ in range(ROUNDS):
        fc = (jnp.sum(left, axis=0, keepdims=True) <= CAP - 1).astype(F32)
        fr = (jnp.sum(left, axis=1, keepdims=True) <= CAP - 1).astype(F32)
        own = own + left * fc * ((1.0 - fr) + fr * after)
        own_t = own_t + left * fr * ((1.0 - fc) + fc * before)
        left = left * (1.0 - fc) * (1.0 - fr)
    own = own + left * after
    own_t = own_t + left * before
    rank = jnp.dot(after, own, preferred_element_type=F32)
    own_ref[...] = own
    own_t_ref[...] = own_t
    rank_ref[...] = rank

    for s in range(CAP):
        total = jnp.zeros((BS, BS), F32)
        for a in range(tile_ref.shape[0] // BS):
            at = (ii == r * (tile_ref.shape[0] // BS) + a) & (jj == j)
            pick = at & (own > 0) & (rank == s)
            w = jnp.sum(jnp.where(pick, 1.0, 0.0), axis=(0, 1), keepdims=True)
            total = total + w * tile_ref[a * BS : (a + 1) * BS, :]
        packed_ref[s * BS : (s + 1) * BS, :] = total


def plan_kernel(
    pat_ref, own_ref, own_t_ref, rank_ref,
    cid_ref, nbr_ref, lid_ref, deg_ref, needed_ref, count_ref, r0, r1, r2, r3, ok_ref,
):
    r, j = here()
    K = (pat_ref[...] != 0).astype(F32)
    ii = lax.broadcasted_iota(jnp.int32, (NB, NB), 0)
    jj = lax.broadcasted_iota(jnp.int32, (NB, NB), 1)
    before = (ii < jj).astype(F32)
    own = own_ref[...]
    own_t = own_t_ref[...]
    rank = rank_ref[...]
    rank_t = jnp.dot(own_t, before, preferred_element_type=F32)
    slot = jj * CAP + rank.astype(jnp.int32)
    slot_t = ii * CAP + rank_t.astype(jnp.int32)
    cid = jnp.where(own > 0, slot, jnp.where(own_t > 0, NS + slot_t, ZERO))
    cid_ref[...] = jnp.full(cid_ref.shape, ZERO, jnp.int32)
    cid_ref[:NB, :] = cid
    column = jnp.where(own > 0, jj, ii)
    turn = jnp.where(own > 0, rank, rank_t).astype(jnp.int32)
    for n, row_ref in enumerate((r0, r1, r2, r3)):
        row_ref[...] = raw_row(column, 2 * turn + n // 2, n % 2, j, r)

    common = jnp.dot(K, K, preferred_element_type=F32)
    pairs = K * jnp.floor((common + 1.0) * 0.5)
    s_blocks = jnp.max(jnp.sum(common, axis=1))
    d_blocks = jnp.max(jnp.sum(common * K, axis=1))
    spread = jnp.dot(K, pairs, preferred_element_type=F32)
    s_pairs = jnp.max(jnp.sum(spread, axis=1))
    fits = (
        (jnp.max(jnp.sum(own, axis=0)) <= CAP)
        & (s_blocks <= S_CAP)
        & (d_blocks <= D_CAP)
        & (s_pairs <= PAIRS)
    )
    ok_ref[0] = fits.astype(jnp.int32)

    kj = jnp.sum(jnp.where(jj == j, K, 0.0), axis=1, keepdims=True)
    near = lax.dot_general(K * kj, K, (((0,), (0,)), ((), ())), preferred_element_type=F32)
    wanted = jnp.where((near > 0) & (K > 0), 1.0, 0.0)
    wide = lax.broadcasted_iota(jnp.int32, (NB, WIDE), 1)
    for listed, n_ref, entries in (
        (K, deg_ref, ((jj, NB, nbr_ref), (cid, ZERO, lid_ref))),
        (wanted, count_ref, ((jj, NB, needed_ref),)),
    ):
        place = jnp.dot(listed, before, preferred_element_type=F32).astype(jnp.int32)
        place = jnp.where(listed > 0, place, -1)
        size = jnp.sum(listed, axis=1, keepdims=True).astype(jnp.int32)
        for value, empty, list_ref in entries:
            out = jnp.full((NB, WIDE), empty, jnp.int32)
            for d in range(NB):
                entry = jnp.sum(jnp.where(place == d, value, 0), axis=1, keepdims=True)
                out = jnp.where((wide == d) & (size > d), entry, out)
            list_ref[...] = out
        n_ref[...] = jnp.broadcast_to(size, (NB, NB))


H_S, H_T, H_E, H_F, H_SB, H_DB, H_EB, H_PN, H_PT = range(9)


def table_kernel(
    ok_ref, cid, nbr, lid, deg_in, needed, count_in, r0, r1, r2, r3,
    head_ref, sl, sr, so, tl, tp, to, el, er, eo, fl, fr, fo, ds_ref, fin_ref,
    pn_ref, pt_ref, an_ref, at_ref,
    did, eid,
):
    r, j = here()
    ok = ok_ref[0]

    def lines(i, carry):
        def entry(d, c):
            pn, pt = c
            k = needed[i, d]
            held = cid[i, k]
            rows = [row[i, k] for row in (r0, r1, r2, r3)]
            flipped = (held >= NS).astype(jnp.int32)
            pn_ref[pn] = held
            pt_ref[pt] = held
            for n, row in enumerate(rows):
                an_ref[4 * pn + n] = row
                at_ref[4 * pt + n] = row
            return pn + (1 - flipped), pt + flipped

        return lax.fori_loop(0, count_in[i, 0] * ok, entry, carry)

    pn, pt = lax.fori_loop(0, NB, lines, (0, 0))
    for names, rows, n in ((pn_ref, an_ref, pn), (pt_ref, at_ref, pt)):
        names[n] = ZERO + 1
        for part in range(4):
            rows[4 * n + part] = 0
    head_ref[H_PN] = pn
    head_ref[H_PT] = pt
    nj = deg_in[j, 0] * ok

    def row(a, carry):
        m = nbr[j, a]
        nm = deg_in[m, 0]
        base = carry[1]

        def output(b, c):
            pos, count, dcount, tcount = c
            k = nbr[m, b]

            def four(g, p):
                at = g * 4
                qs = [nbr[m, at + u] for u in range(4)]
                ls = [lid[m, at + u] for u in range(4)]
                rs = [cid[q, k] for q in qs]
                for u in range(4):
                    sl[p] = ls[u]
                    tl[p] = base + at + u
                    sr[p] = rs[u]
                    so[p] = count
                    p = p + (rs[u] != ZERO).astype(jnp.int32)
                return p

            p = lax.fori_loop(0, (nm + 3) // 4, four, pos)
            sl[p] = ZERO
            tl[p] = S_CAP
            sr[p] = ZERO
            so[p] = count
            p = p + (p & 1)

            def reuse(pair, t):
                tp[t] = pair
                to[t] = dcount
                return t + 1

            inside = (cid[k, j] != ZERO).astype(jnp.int32)
            first = pos // 2
            tcount = lax.fori_loop(first, first + inside * (p // 2 - first), reuse, tcount)
            did[m, k] = dcount
            ds_ref[dcount] = count
            return p, count + 1, dcount + inside, tcount

        return lax.fori_loop(0, nm, output, carry)

    pos, count, dcount, tcount = lax.fori_loop(0, nj, row, (0, 0, 0, 0))
    for t in range(2 * UNROLL):
        sl[pos + t] = ZERO
        tl[pos + t] = S_CAP
        sr[pos + t] = ZERO
        so[pos + t] = S_CAP
    for t in range(UNROLL):
        tp[tcount + t] = pos // 2
        to[tcount + t] = D_CAP
    head_ref[H_S] = (pos // 2 + UNROLL - 1) // UNROLL
    head_ref[H_T] = (tcount + UNROLL - 1) // UNROLL
    ds_ref[dcount] = 0
    head_ref[H_SB] = count
    head_ref[H_DB] = dcount

    def finish(refs, pos, lz, rz, dummy):
        L, R, O = refs
        for t in range(2 * UNROLL):
            L[pos + t] = lz
            R[pos + t] = rz
            O[pos + t] = dummy
        return (pos // 2 + UNROLL - 1) // UNROLL

    def gather(refs, pos, k, left, out, lz, rz):
        L, R, O = refs

        def entry(c, p):
            m = nbr[j, c]
            L[p] = left(m)
            R[p] = did[m, k]
            O[p] = out
            return p + (cid[m, k] != ZERO).astype(jnp.int32)

        p = lax.fori_loop(0, nj, entry, pos)
        L[p] = lz
        R[p] = rz
        O[p] = out
        return p + (p & 1)

    def e_out(b, pos):
        k = nbr[j, b]
        eid[k] = b
        return gather((el, er, eo), pos, k, lambda m: did[j, m], b, D_CAP, D_CAP)

    pos = lax.fori_loop(0, nj, e_out, 0)
    head_ref[H_E] = finish((el, er, eo), pos, D_CAP, D_CAP, E_CAP)
    head_ref[H_EB] = nj

    per = NB // 8

    def f_out(a, pos):
        i = r * per + a

        def stored(pos):
            fin_ref[a] = eid[i]
            return gather((fl, fr, fo), pos, i, lambda k: eid[k], a, E_CAP, D_CAP)

        def absent(pos):
            fin_ref[a] = -1
            return pos

        return lax.cond((cid[i, j] != ZERO) & (ok != 0), stored, absent, pos)

    pos = lax.fori_loop(0, per, f_out, 0)
    head_ref[H_F] = finish((fl, fr, fo), pos, E_CAP, D_CAP, per)


def split(x):
    hi = x.astype(BF16)
    return hi, (x - hi.astype(F32)).astype(BF16)


def compute_kernel(
    head_ref, sl, sr, so, tl, tp, to, el, er, eo, fl, fr, fo, ds_ref, fin_ref,
    pn_ref, pt_ref, an_ref, at_ref,
    *rest,
):
    pieces, rest = rest[:-15], rest[-15:]
    out_ref, raw, ch, cl, sa, sh, slo, da, dh, dl, ea, eh, elo, fa, sem = rest
    copies = []
    row = 0
    for n, piece in enumerate(pieces):
        height = piece.shape[0]
        copies.append(pltpu.make_async_copy(piece, raw.at[pl.ds(row, height)], sem.at[n]))
        row += height
    for c in copies:
        c.start()
    zero = jnp.zeros((BS, BS), BF16)
    for hi, lo, at in ((ch, cl, ZERO), (sh, slo, S_CAP), (dh, dl, D_CAP), (eh, elo, E_CAP)):
        hi[at] = zero
        lo[at] = zero

    def clear(ref, n):
        @pl.loop(0, n)
        def _(t):
            ref[t] = jnp.zeros((BS, BS), F32)

    clear(sa, head_ref[H_SB])
    clear(da, head_ref[H_DB])
    clear(ea, head_ref[H_EB])
    clear(fa, fa.shape[0])
    for c in copies:
        c.wait()

    def prepare(n, names, rows, turn):
        @pl.loop(0, (n + 1) // 2)
        def _(t):
            ids = [names[2 * t], names[2 * t + 1]]
            xs = []
            for u in range(2):
                parts = [
                    raw[pl.ds(pl.multiple_of(rows[8 * t + 4 * u + n], PART), PART), :] for n in range(4)
                ]
                xs.append(split(turn(jnp.concatenate(parts, axis=0))))
            for a, (hi, lo) in zip(ids, xs):
                ch[a] = hi
                cl[a] = lo

    prepare(head_ref[H_PN], pn_ref, an_ref, lambda v: v)
    prepare(head_ref[H_PT], pt_ref, at_ref, lambda v: v.T)

    def phase(n, task, left, right, acc):
        lh, ll = left
        rh, rl = right

        @pl.loop(0, n)
        def _(t):
            sums = []
            outs = []
            for u in range(UNROLL):
                a0, a1, b0, b1, out = task(t * UNROLL + u)
                lhs = jnp.concatenate(
                    [
                        jnp.concatenate([lh[a0], lh[a1]], axis=1),
                        jnp.concatenate([ll[a0], ll[a1]], axis=1),
                    ],
                    axis=0,
                )
                rhs = jnp.concatenate(
                    [
                        jnp.concatenate([rh[b0], rl[b0]], axis=1),
                        jnp.concatenate([rh[b1], rl[b1]], axis=1),
                    ],
                    axis=0,
                )
                both = jnp.dot(lhs, rhs, preferred_element_type=F32)
                sums.append(both[:BS, :BS] + (both[:BS, BS:] + both[BS:, :BS]))
                outs.append(out)
            for u in range(UNROLL):
                acc[outs[u]] = acc[outs[u]] + sums[u]

    def plain(L, R, O):
        def task(t):
            return L[2 * t], L[2 * t + 1], R[2 * t], R[2 * t + 1], O[2 * t]

        return task

    def cube(t):
        at = 2 * tp[t]
        return tl[at], tl[at + 1], sr[at], sr[at + 1], to[t]

    phase(head_ref[H_S], plain(sl, sr, so), (ch, cl), (ch, cl), sa)

    @pl.loop(0, (head_ref[H_SB] + 1) // 2)
    def _(t):
        both = [split(sa[2 * t + u]) for u in range(2)]
        for u in range(2):
            sh[2 * t + u], slo[2 * t + u] = both[u]

    phase(head_ref[H_T], cube, (sh, slo), (ch, cl), da)

    @pl.loop(0, (head_ref[H_DB] + 1) // 2)
    def _(t):
        both = [split(3.0 * sa[ds_ref[2 * t + u]] - 2.0 * da[2 * t + u]) for u in range(2)]
        for u in range(2):
            dh[2 * t + u], dl[2 * t + u] = both[u]

    phase(head_ref[H_E], plain(el, er, eo), (dh, dl), (dh, dl), ea)

    @pl.loop(0, head_ref[H_EB])
    def _(t):
        eh[t], elo[t] = split(ea[t])

    phase(head_ref[H_F], plain(fl, fr, fo), (eh, elo), (dh, dl), fa)
    for a in range(out_ref.shape[0] // BS):
        at = fin_ref[a]
        value = 3.0 * ea[jnp.maximum(at, 0)] - 2.0 * fa[a]
        out_ref[a * BS : (a + 1) * BS, :] = jnp.where(at >= 0, value.T, 0.0)


def to_chips_along_z(shard):
    parts = jnp.broadcast_to(shard.reshape(NC, PART, BS), (NZ, NC, PART, BS)).reshape(NZ * NC, PART, BS)
    return lax.all_to_all(parts, "col", split_axis=0, concat_axis=0, tiled=True).reshape(UNIT, BS)


def linear(x, y, z, core):
    return (((x % 2) * NY + y) * (NZ * NC) + z * NC + core) * 2 + x // 2


def send(value, step):
    pairs = [
        (linear(x, y, z, core), linear(*step(x, y, z, core)))
        for x in range(NX)
        for y in range(NY)
        for z in range(NZ)
        for core in range(NC)
    ]
    return lax.ppermute(value, ("row", "col", "layer"), pairs)


def inner(d):
    return lambda x, y, z, core: ((x + d) % NX, y, z, core) if core == 0 else (x, (y + d) % NY, z, core)


def outer(d):
    return lambda x, y, z, core: (x, (y + d) % NY, z, core) if core == 0 else ((x + d) % NX, y, z, core)


def other_core(x, y, z, core):
    return x, y, z, 1 - core


def list_products(ok, *plan):
    smem = pl.BlockSpec(memory_space=pltpu.SMEM)
    i32 = lambda *shape: jax.ShapeDtypeStruct(shape, jnp.int32)
    return pl.pallas_call(
        table_kernel,
        out_shape=[i32(16), *[i32(LIST)] * 12, i32(D_CAP + 1), i32(8), *[i32(2 * NS + 2)] * 2, *[i32(8 * NS + 8)] * 2],
        in_specs=[smem] * 11,
        out_specs=[smem] * 19,
        scratch_shapes=[
            pltpu.SMEM((NB, NB), jnp.int32),
            pltpu.SMEM((NB,), jnp.int32),
        ],
        cost_estimate=pl.CostEstimate(flops=0, bytes_accessed=30_000_000, transcendentals=0),
        name="list_products",
    )(ok, *plan)


def plan_products(pattern, *owners):
    smem = pl.BlockSpec(memory_space=pltpu.SMEM)
    vmem = pl.BlockSpec(memory_space=pltpu.VMEM)
    i32 = lambda *shape: jax.ShapeDtypeStruct(shape, jnp.int32)
    return pl.pallas_call(
        plan_kernel,
        out_shape=(
            i32(WIDE, NB), i32(NB, WIDE), i32(NB, WIDE), i32(NB, NB), i32(NB, WIDE), i32(NB, NB),
            *[i32(NB, NB)] * 4,
            i32(1),
        ),
        in_specs=[vmem] * 4,
        out_specs=(*[vmem] * 10, smem),
        cost_estimate=pl.CostEstimate(flops=0, bytes_accessed=10_000_000, transcendentals=0),
        name="plan_products",
    )(pattern, *owners)


def gather_pieces(shard, pattern, owners):
    own = to_chips_along_z(shard)
    own, owners = lax.optimization_barrier((own, owners))
    line = [own] + [send(own, inner(d)) for d in (1, -1, 2)]
    *plan, ok = plan_products(pattern, *owners)
    line, plan, ok = lax.optimization_barrier((line, plan, ok))

    panel = jnp.concatenate(line, axis=0)
    back, ahead = send(panel, outer(1)), send(panel, outer(-1))
    swapped = [send(panel, other_core)]
    tables = list_products(ok, *plan)
    back, ahead, tables = lax.optimization_barrier((back, ahead, tables))
    far = [send(back[: PANEL // 2], outer(1)), send(ahead[PANEL // 2 :], outer(-1))]
    swapped += [send(value, other_core) for value in (back, ahead)]
    far = lax.optimization_barrier(far)
    swapped += [send(value, other_core) for value in far]
    return ok, tables, [panel, back, ahead, *far, *swapped]


def per_device(density, pattern):
    smem = pl.BlockSpec(memory_space=pltpu.SMEM)
    vmem = pl.BlockSpec(memory_space=pltpu.VMEM)

    square = jax.ShapeDtypeStruct((NB, NB), F32)
    packed, *owners = pl.pallas_call(
        pack_kernel,
        out_shape=(jax.ShapeDtypeStruct((CAP * BS, BS), F32), square, square, square),
        in_specs=[vmem, vmem],
        out_specs=[vmem] * 4,
        name="pack_blocks",
    )(pattern, density)

    rows = lax.axis_size("row")
    pieces = packed.reshape(rows, SHARD, BS)
    shard = jnp.sum(lax.all_to_all(pieces, "row", split_axis=0, concat_axis=0, tiled=True), axis=0)
    ok, tables, gathered = gather_pieces(shard, pattern, owners)

    def sparse(density, pattern, tables, gathered):
        block = lambda n, t: pltpu.VMEM((n, BS, BS), t)
        return pl.pallas_call(
            compute_kernel,
            out_shape=jax.ShapeDtypeStruct(density.shape, F32),
            in_specs=[smem] * len(tables) + [pl.BlockSpec(memory_space=pl.ANY)] * len(gathered),
            out_specs=vmem,
            scratch_shapes=[
                pltpu.VMEM((2 * RAW_HALF, BS), F32),
                block(ZERO + 2, BF16), block(ZERO + 2, BF16),
                block(S_CAP + 1, F32), block(S_CAP + 1, BF16), block(S_CAP + 1, BF16),
                block(D_CAP + 1, F32), block(D_CAP + 1, BF16), block(D_CAP + 1, BF16),
                block(E_CAP + 1, F32), block(E_CAP + 1, BF16), block(E_CAP + 1, BF16),
                block(NB // 8 + 1, F32),
                pltpu.SemaphoreType.DMA((len(gathered),)),
            ],
            compiler_params=pltpu.CompilerParams(vmem_limit_bytes=60 * 2**20),
            name="purify_column",
        )(*tables, *gathered)

    def dense(density, pattern, tables, gathered):
        return dense_plan(density, pattern)

    return lax.cond(ok[0] != 0, sparse, dense, density, pattern, tables, gathered)


def solution(mesh):
    return jax.shard_map(
        per_device,
        mesh=mesh,
        in_specs=(P("row", ("col", "layer")), P()),
        out_specs=P("row", ("col", "layer")),
        check_vma=False,
    )
```

```python
import jax
import jax.numpy as jnp
from jax import lax
from jax.experimental import pallas as pl
from jax.experimental.pallas import tpu as pltpu
from jax.sharding import PartitionSpec as P

BS = 128
ITERS = 2
NB = 32
CAP = 4
NS = NB * CAP
ROUNDS = 8
ZERO = 2 * NS
S_CAP = 104
D_CAP = 80
E_CAP = NB
PAIRS = 256
UNROLL = 4
MANY = 4
LIST = 2 * PAIRS + 2 * UNROLL + 8
NZ, NC = 8, 2
NX, NY = 4, 4
SHARD = CAP * BS // 8
PART = SHARD // NC
UNIT = NZ * NC * PART
PANEL = 4 * UNIT
RAW_HALF = 4 * PANEL
WIDE = 40
WORD = 4096
F32 = jnp.float32
BF16 = jnp.bfloat16


def panel_cols(tile, layers):
    row_count, shard_cols = tile.shape
    gathered = lax.all_gather(tile, "row", axis=0, tiled=True)
    pieces = gathered.reshape(
        gathered.shape[0] // (shard_cols * layers), layers, shard_cols, shard_cols
    )
    arranged = lax.all_to_all(pieces, "layer", split_axis=1, concat_axis=3, tiled=True)
    return arranged.reshape(-1, layers * shard_cols)


def multiply(left_tile, right_panel):
    partial_sum = jnp.dot(
        lax.all_gather(left_tile, "col", axis=1, tiled=True),
        right_panel,
        precision=lax.Precision.HIGHEST,
        preferred_element_type=jnp.float32,
    )
    return lax.psum_scatter(partial_sum, "layer", scatter_dimension=1, tiled=True)


def dense_plan(density, pattern):
    row_index = lax.axis_index("row")
    col_index = lax.axis_index("col")
    layer_index = lax.axis_index("layer")
    layers = lax.axis_size("layer")
    row_count, shard_cols = density.shape
    blocks = pattern.shape[0]
    block_line = jnp.arange(blocks, dtype=jnp.int32)
    row_ids = (row_index * row_count + jnp.arange(row_count, dtype=jnp.int32)) // BS
    col_ids = (
        (col_index * layers + layer_index) * shard_cols + jnp.arange(shard_cols, dtype=jnp.int32)
    ) // BS
    pick_rows = (row_ids[:, None] == block_line[None, :]).astype(jnp.float32)
    pick_cols = (col_ids[:, None] == block_line[None, :]).astype(jnp.float32)
    occupied = pattern.astype(jnp.float32)
    in_pattern = jnp.dot(
        jnp.dot(pick_rows, occupied, precision=lax.Precision.HIGHEST),
        pick_cols.T,
        precision=lax.Precision.HIGHEST,
    )
    current = in_pattern * density
    for iteration in range(ITERS):
        current_panel = panel_cols(current, layers)
        squared = in_pattern * multiply(current, current_panel)
        cube_term = in_pattern * multiply(current, panel_cols(squared, layers))
        current = 3.0 * squared - 2.0 * cube_term
    return current


def here():
    row = lax.axis_index("row").astype(jnp.int32)
    column = lax.axis_index("col") * lax.axis_size("layer") + lax.axis_index("layer")
    return row, column.astype(jnp.int32)


def ring_place(source, at):
    back = (at - source) & 3
    return jnp.where(back == 3, 2, jnp.where(back == 2, 3, back))


def raw_row(column, p, h, j, r):
    px = ring_place((column & 1) * 2 + (p >> 2), (j & 1) * 2 + (r >> 2))
    py = ring_place(p & 3, r & 3)
    near, far = ((px, py), (py, px))[h]
    other = jnp.where(((j >> 1) & 1) == h, 0, 1)
    high = near >> 1
    group = jnp.where(
        (far == 1) | (far == 2),
        2 + jnp.where(far == 1, 2 * high, 3 - 2 * high),
        2 * far + high,
    )
    unit = (((j >> 2) - (column >> 2)) & (NZ - 1)) * SHARD + ((column >> 1) & 1) * PART
    return other * RAW_HALF + group * (PANEL // 2) + (near & 1) * UNIT + unit


def pack_kernel(pat_ref, tile_ref, packed_ref, own_ref, own_t_ref, rank_ref):
    r, j = here()
    K = (pat_ref[...] != 0).astype(F32)
    ii = lax.broadcasted_iota(jnp.int32, (NB, NB), 0)
    jj = lax.broadcasted_iota(jnp.int32, (NB, NB), 1)
    diag = (ii == jj).astype(F32)
    left = K * (1.0 - diag)
    own = diag
    own_t = diag
    after = (ii > jj).astype(F32)
    before = (ii < jj).astype(F32)
    for _ in range(ROUNDS):
        fc = (jnp.sum(left, axis=0, keepdims=True) <= CAP - 1).astype(F32)
        fr = (jnp.sum(left, axis=1, keepdims=True) <= CAP - 1).astype(F32)
        own = own + left * fc * ((1.0 - fr) + fr * after)
        own_t = own_t + left * fr * ((1.0 - fc) + fc * before)
        left = left * (1.0 - fc) * (1.0 - fr)
    own = own + left * after
    own_t = own_t + left * before
    rank = jnp.dot(after, own, preferred_element_type=F32)
    own_ref[...] = own
    own_t_ref[...] = own_t
    rank_ref[...] = rank

    for s in range(CAP):
        total = jnp.zeros((BS, BS), F32)
        for a in range(tile_ref.shape[0] // BS):
            at = (ii == r * (tile_ref.shape[0] // BS) + a) & (jj == j)
            pick = at & (own > 0) & (rank == s)
            w = jnp.sum(jnp.where(pick, 1.0, 0.0), axis=(0, 1), keepdims=True)
            total = total + w * tile_ref[a * BS : (a + 1) * BS, :]
        packed_ref[s * BS : (s + 1) * BS, :] = total


def plan_kernel(
    pat_ref, own_ref, own_t_ref, rank_ref,
    cid_ref, nbr_ref, deg_ref, needed_ref, count_ref, rows_a, rows_b, ok_ref,
):
    r, j = here()
    K = (pat_ref[...] != 0).astype(F32)
    ii = lax.broadcasted_iota(jnp.int32, (NB, NB), 0)
    jj = lax.broadcasted_iota(jnp.int32, (NB, NB), 1)
    before = (ii < jj).astype(F32)
    own = own_ref[...]
    own_t = own_t_ref[...]
    rank = rank_ref[...]
    rank_t = jnp.dot(own_t, before, preferred_element_type=F32)
    slot = jj * CAP + rank.astype(jnp.int32)
    slot_t = ii * CAP + rank_t.astype(jnp.int32)
    cid = jnp.where(own > 0, slot, jnp.where(own_t > 0, NS + slot_t, ZERO))
    cid_ref[...] = jnp.full(cid_ref.shape, ZERO, jnp.int32)
    cid_ref[:NB, :] = cid
    column = jnp.where(own > 0, jj, ii)
    turn = jnp.where(own > 0, rank, rank_t).astype(jnp.int32)
    for n, row_ref in enumerate((rows_a, rows_b)):
        first, second = [raw_row(column, 2 * turn + n, h, j, r) // PART for h in range(2)]
        row_ref[...] = first + second * WORD

    common = jnp.dot(K, K, preferred_element_type=F32)
    pairs = K * jnp.floor((common + 1.0) * 0.5)
    s_blocks = jnp.max(jnp.sum(common, axis=1))
    d_blocks = jnp.max(jnp.sum(common * K, axis=1))
    spread = jnp.dot(K, pairs, preferred_element_type=F32)
    s_pairs = jnp.max(jnp.sum(spread, axis=1))
    fits = (
        (jnp.max(jnp.sum(own, axis=0)) <= CAP)
        & (s_blocks <= S_CAP)
        & (d_blocks <= D_CAP)
        & (s_pairs <= PAIRS)
    )
    ok_ref[0] = fits.astype(jnp.int32)

    kj = jnp.sum(jnp.where(jj == j, K, 0.0), axis=1, keepdims=True)
    near = lax.dot_general(K * kj, K, (((0,), (0,)), ((), ())), preferred_element_type=F32)
    wanted = jnp.where((near > 0) & (K > 0), 1.0, 0.0)
    wide = lax.broadcasted_iota(jnp.int32, (NB, WIDE), 1)
    for listed, n_ref, entries in (
        (K, deg_ref, ((jj + cid * WORD, NB + ZERO * WORD, nbr_ref),)),
        (wanted, count_ref, ((jj, NB, needed_ref),)),
    ):
        place = jnp.dot(listed, before, preferred_element_type=F32).astype(jnp.int32)
        place = jnp.where(listed > 0, place, -1)
        size = jnp.sum(listed, axis=1, keepdims=True).astype(jnp.int32)
        for value, empty, list_ref in entries:
            out = jnp.full((NB, WIDE), empty, jnp.int32)
            for d in range(NB):
                entry = jnp.sum(jnp.where(place == d, value, 0), axis=1, keepdims=True)
                out = jnp.where((wide == d) & (size > d), entry, out)
            list_ref[...] = out
        n_ref[...] = jnp.broadcast_to(size, (NB, NB))


H_S, H_T, H_E, H_F, H_SB, H_DB, H_EB, H_PN, H_PT = range(9)


def table_kernel(
    ok_ref, cid, nbr, deg_in, needed, count_in, rows_a, rows_b,
    head_ref, sl, sr, tt, el, er, fl, fr, ds_ref, fin_ref, pn_ref, pt_ref, an_ref, at_ref,
    did, eid,
):
    r, j = here()
    ok = ok_ref[0]

    def lines(i, carry):
        def entry(d, c):
            pn, pt = c
            k = needed[i, d]
            held = cid[i, k]
            rows = (rows_a[i, k], rows_b[i, k])
            flipped = (held >= NS).astype(jnp.int32)
            pn_ref[pn] = held
            pt_ref[pt] = held
            for n, row in enumerate(rows):
                an_ref[2 * pn + n] = row
                at_ref[2 * pt + n] = row
            return pn + (1 - flipped), pt + flipped

        return lax.fori_loop(0, count_in[i, 0] * ok, entry, carry)

    pn, pt = lax.fori_loop(0, NB, lines, (0, 0))
    for names, rows, n in ((pn_ref, an_ref, pn), (pt_ref, at_ref, pt)):
        for u in range(MANY - 1):
            names[n + u] = ZERO + 1
            for part in range(2):
                rows[2 * (n + u) + part] = 0
    head_ref[H_PN] = pn
    head_ref[H_PT] = pt
    nj = deg_in[j, 0] * ok

    def row(a, carry):
        m = nbr[j, a] & (WORD - 1)
        nm = deg_in[m, 0]
        base = carry[1] * WORD

        def output(b, c):
            pos, count, dcount, tcount = c
            k = nbr[m, b] & (WORD - 1)
            out = count * WORD

            def four(g, p):
                at = g * 4
                words = [nbr[m, at + u] for u in range(4)]
                rs = [cid[w & (WORD - 1), k] for w in words]
                for u in range(4):
                    sl[p] = (words[u] >> 12) + (base + (at + u) * WORD)
                    sr[p] = rs[u] + out
                    p = p + (rs[u] != ZERO).astype(jnp.int32)
                return p

            p = lax.fori_loop(0, (nm + 3) >> 2, four, pos)
            sl[p] = ZERO + S_CAP * WORD
            sr[p] = ZERO + out
            p = p + (p & 1)

            def reuse(pair, t):
                tt[t] = pair + dcount * WORD
                return t + 1

            inside = (cid[k, j] != ZERO).astype(jnp.int32)
            first = pos >> 1
            tcount = lax.fori_loop(first, first + inside * ((p >> 1) - first), reuse, tcount)
            did[m, k] = dcount
            ds_ref[dcount] = count
            return p, count + 1, dcount + inside, tcount

        return lax.fori_loop(0, nm, output, carry)

    pos, count, dcount, tcount = lax.fori_loop(0, nj, row, (0, 0, 0, 0))
    for t in range(2 * UNROLL):
        sl[pos + t] = ZERO + S_CAP * WORD
        sr[pos + t] = ZERO + S_CAP * WORD
    for t in range(UNROLL):
        tt[tcount + t] = (pos >> 1) + D_CAP * WORD
    for u in range(MANY - 1):
        ds_ref[dcount + u] = 0
    head_ref[H_S] = ((pos >> 1) + UNROLL - 1) // UNROLL
    head_ref[H_T] = (tcount + UNROLL - 1) // UNROLL
    head_ref[H_SB] = count
    head_ref[H_DB] = dcount

    def finish(refs, pos, lz, dummy):
        L, R = refs
        for t in range(2 * UNROLL):
            L[pos + t] = lz
            R[pos + t] = D_CAP + dummy * WORD
        return ((pos >> 1) + UNROLL - 1) // UNROLL

    def gather(refs, pos, k, left, out, lz):
        L, R = refs

        def entry(c, p):
            m = nbr[j, c] & (WORD - 1)
            L[p] = left(m)
            R[p] = did[m, k] + out * WORD
            return p + (cid[m, k] != ZERO).astype(jnp.int32)

        p = lax.fori_loop(0, nj, entry, pos)
        L[p] = lz
        R[p] = D_CAP + out * WORD
        return p + (p & 1)

    def e_out(b, pos):
        k = nbr[j, b] & (WORD - 1)
        eid[k] = b
        return gather((el, er), pos, k, lambda m: did[j, m], b, D_CAP)

    pos = lax.fori_loop(0, nj, e_out, 0)
    head_ref[H_E] = finish((el, er), pos, D_CAP, E_CAP)
    head_ref[H_EB] = nj

    per = NB // 8

    def f_out(a, pos):
        i = r * per + a

        def stored(pos):
            fin_ref[a] = eid[i]
            return gather((fl, fr), pos, i, lambda k: eid[k], a, E_CAP)

        def absent(pos):
            fin_ref[a] = -1
            return pos

        return lax.cond((cid[i, j] != ZERO) & (ok != 0), stored, absent, pos)

    pos = lax.fori_loop(0, per, f_out, 0)
    head_ref[H_F] = finish((fl, fr), pos, E_CAP, per)


def split(x):
    hi = x.astype(BF16)
    return hi, (x - hi.astype(F32)).astype(BF16)


def compute_kernel(
    head_ref, sl, sr, tt, el, er, fl, fr, ds_ref, fin_ref, pn_ref, pt_ref, an_ref, at_ref,
    *rest,
):
    pieces, rest = rest[:-15], rest[-15:]
    out_ref, raw, ch, cl, sa, sh, slo, da, dh, dl, ea, eh, elo, fa, sem = rest
    copies = []
    row = 0
    for n, piece in enumerate(pieces):
        height = piece.shape[0]
        copies.append(pltpu.make_async_copy(piece, raw.at[pl.ds(row, height)], sem.at[n]))
        row += height
    for c in copies:
        c.start()
    zero = jnp.zeros((BS, BS), BF16)
    for hi, lo, at in ((ch, cl, ZERO), (sh, slo, S_CAP), (dh, dl, D_CAP), (eh, elo, E_CAP)):
        hi[at] = zero
        lo[at] = zero

    def clear(ref, n):
        @pl.loop(0, n)
        def _(t):
            ref[t] = jnp.zeros((BS, BS), F32)

    clear(sa, head_ref[H_SB])
    clear(da, head_ref[H_DB])
    clear(ea, head_ref[H_EB])
    clear(fa, fa.shape[0])
    for c in copies:
        c.wait()

    def prepare(n, names, rows, turn):
        @pl.loop(0, (n + MANY - 1) // MANY)
        def _(t):
            ids = [names[MANY * t + u] for u in range(MANY)]
            xs = []
            for u in range(MANY):
                words = [rows[2 * (MANY * t + u) + n] for n in range(2)]
                starts = [w & (WORD - 1) if h == 0 else w >> 12 for w in words for h in range(2)]
                parts = [raw[pl.ds(pl.multiple_of(at * PART, PART), PART), :] for at in starts]
                xs.append(split(turn(jnp.concatenate(parts, axis=0))))
            for a, (hi, lo) in zip(ids, xs):
                ch[a] = hi
                cl[a] = lo

    prepare(head_ref[H_PN], pn_ref, an_ref, lambda v: v)
    prepare(head_ref[H_PT], pt_ref, at_ref, lambda v: v.T)

    def phase(n, task, left, right, acc):
        lh, ll = left
        rh, rl = right

        @pl.loop(0, n)
        def _(t):
            sums = []
            outs = []
            for u in range(UNROLL):
                a0, a1, b0, b1, out = task(t * UNROLL + u)
                lhs = jnp.concatenate(
                    [
                        jnp.concatenate([lh[a0], lh[a1]], axis=1),
                        jnp.concatenate([ll[a0], ll[a1]], axis=1),
                    ],
                    axis=0,
                )
                rhs = jnp.concatenate(
                    [
                        jnp.concatenate([rh[b0], rl[b0]], axis=1),
                        jnp.concatenate([rh[b1], rl[b1]], axis=1),
                    ],
                    axis=0,
                )
                both = jnp.dot(lhs, rhs, preferred_element_type=F32)
                sums.append(both[:BS, :BS] + (both[:BS, BS:] + both[BS:, :BS]))
                outs.append(out)
            for u in range(UNROLL):
                acc[outs[u]] = acc[outs[u]] + sums[u]

    def plain(L, R):
        def task(t):
            r0 = R[2 * t]
            low = lambda w: w & (WORD - 1)
            return low(L[2 * t]), low(L[2 * t + 1]), low(r0), low(R[2 * t + 1]), r0 >> 12

        return task

    def cube(t):
        word = tt[t]
        at = 2 * (word & (WORD - 1))
        return sl[at] >> 12, sl[at + 1] >> 12, sr[at] & (WORD - 1), sr[at + 1] & (WORD - 1), word >> 12

    phase(head_ref[H_S], plain(sl, sr), (ch, cl), (ch, cl), sa)

    @pl.loop(0, (head_ref[H_SB] + MANY - 1) // MANY)
    def _(t):
        done = [split(sa[MANY * t + u]) for u in range(MANY)]
        for u in range(MANY):
            sh[MANY * t + u], slo[MANY * t + u] = done[u]

    phase(head_ref[H_T], cube, (sh, slo), (ch, cl), da)

    @pl.loop(0, (head_ref[H_DB] + MANY - 1) // MANY)
    def _(t):
        done = [split(3.0 * sa[ds_ref[MANY * t + u]] - 2.0 * da[MANY * t + u]) for u in range(MANY)]
        for u in range(MANY):
            dh[MANY * t + u], dl[MANY * t + u] = done[u]

    phase(head_ref[H_E], plain(el, er), (dh, dl), (dh, dl), ea)

    @pl.loop(0, head_ref[H_EB])
    def _(t):
        eh[t], elo[t] = split(ea[t])

    phase(head_ref[H_F], plain(fl, fr), (eh, elo), (dh, dl), fa)
    for a in range(out_ref.shape[0] // BS):
        at = fin_ref[a]
        value = 3.0 * ea[jnp.maximum(at, 0)] - 2.0 * fa[a]
        out_ref[a * BS : (a + 1) * BS, :] = jnp.where(at >= 0, value.T, 0.0)


def linear(x, y, z, core):
    return (((x % 2) * NY + y) * (NZ * NC) + z * NC + core) * 2 + x // 2


def send(value, step):
    pairs = [
        (linear(x, y, z, core), linear(*step(x, y, z, core)))
        for x in range(NX)
        for y in range(NY)
        for z in range(NZ)
        for core in range(NC)
    ]
    return lax.ppermute(value, ("row", "col", "layer"), pairs)


def along_z(d):
    return lambda x, y, z, core: (x, y, (z + d) % NZ, core)


def inner(d):
    return lambda x, y, z, core: ((x + d) % NX, y, z, core) if core == 0 else (x, (y + d) % NY, z, core)


def outer(d):
    return lambda x, y, z, core: (x, (y + d) % NY, z, core) if core == 0 else ((x + d) % NX, y, z, core)


def other_core(x, y, z, core):
    return x, y, z, 1 - core


def list_products(ok, *plan):
    smem = pl.BlockSpec(memory_space=pltpu.SMEM)
    i32 = lambda *shape: jax.ShapeDtypeStruct(shape, jnp.int32)
    return pl.pallas_call(
        table_kernel,
        out_shape=[
            i32(16), *[i32(LIST)] * 7, i32(D_CAP + MANY), i32(8),
            *[i32(2 * NS + 8)] * 2, *[i32(4 * NS + 16)] * 2,
        ],
        in_specs=[smem] * 8,
        out_specs=[smem] * 14,
        scratch_shapes=[
            pltpu.SMEM((NB, NB), jnp.int32),
            pltpu.SMEM((NB,), jnp.int32),
        ],
        cost_estimate=pl.CostEstimate(flops=0, bytes_accessed=30_000_000, transcendentals=0),
        name="list_products",
    )(ok, *plan)


def plan_products(pattern, *owners):
    smem = pl.BlockSpec(memory_space=pltpu.SMEM)
    vmem = pl.BlockSpec(memory_space=pltpu.VMEM)
    i32 = lambda *shape: jax.ShapeDtypeStruct(shape, jnp.int32)
    return pl.pallas_call(
        plan_kernel,
        out_shape=(
            i32(WIDE, NB), i32(NB, WIDE), i32(NB, NB), i32(NB, WIDE), i32(NB, NB),
            *[i32(NB, NB)] * 2,
            i32(1),
        ),
        in_specs=[vmem] * 4,
        out_specs=(*[vmem] * 7, smem),
        cost_estimate=pl.CostEstimate(flops=0, bytes_accessed=10_000_000, transcendentals=0),
        name="plan_products",
    )(pattern, *owners)


def gather_pieces(shard, pattern, owners):
    core = lax.axis_index("col") % NC
    halves = shard[:PART], shard[PART:]
    pick = lambda a, b: jnp.where(core == 0, a, b)
    kept, given = pick(*halves), pick(*halves[::-1])
    got = send(given, other_core)
    unit = jnp.concatenate([pick(kept, got), pick(got, kept)], axis=0)
    unit, owners = lax.optimization_barrier((unit, owners))
    by_z = [unit] + [send(unit, along_z(d)) for d in range(1, NZ)]
    *plan, ok = plan_products(pattern, *owners)
    by_z, plan, ok = lax.optimization_barrier((by_z, plan, ok))
    own = jnp.concatenate(by_z, axis=0)
    line = [own] + [send(own, inner(d)) for d in (1, -1, 2)]
    line = lax.optimization_barrier(line)

    own, back, ahead, opposite = line
    low, high = jnp.concatenate([own, back], axis=0), jnp.concatenate([ahead, opposite], axis=0)
    back_low, ahead_high = send(low, outer(1)), send(high, outer(-1))
    back_high, ahead_low = send(high, outer(1)), send(low, outer(-1))
    back_low, ahead_high, plan = lax.optimization_barrier((back_low, ahead_high, plan))
    far_low, far_high = send(back_low, outer(1)), send(ahead_high, outer(-1))
    panel_swapped = send(jnp.concatenate([low, high], axis=0), other_core)
    tables = list_products(ok, *plan)
    rest = [back_low, ahead_high, back_high, ahead_low, far_low, far_high]
    rest, tables = lax.optimization_barrier((rest, tables))
    swapped = [send(value, other_core) for value in rest]
    return ok, tables, [low, high, *rest, panel_swapped, *swapped]


def per_device(density, pattern):
    smem = pl.BlockSpec(memory_space=pltpu.SMEM)
    vmem = pl.BlockSpec(memory_space=pltpu.VMEM)

    square = jax.ShapeDtypeStruct((NB, NB), F32)
    packed, *owners = pl.pallas_call(
        pack_kernel,
        out_shape=(jax.ShapeDtypeStruct((CAP * BS, BS), F32), square, square, square),
        in_specs=[vmem, vmem],
        out_specs=[vmem] * 4,
        name="pack_blocks",
    )(pattern, density)

    rows = lax.axis_size("row")
    pieces = packed.reshape(rows, SHARD, BS)
    shard = jnp.sum(lax.all_to_all(pieces, "row", split_axis=0, concat_axis=0, tiled=True), axis=0)
    ok, tables, gathered = gather_pieces(shard, pattern, owners)

    def sparse(density, pattern, tables, gathered):
        block = lambda n, t: pltpu.VMEM((n, BS, BS), t)
        return pl.pallas_call(
            compute_kernel,
            out_shape=jax.ShapeDtypeStruct(density.shape, F32),
            in_specs=[smem] * len(tables) + [pl.BlockSpec(memory_space=pl.ANY)] * len(gathered),
            out_specs=vmem,
            scratch_shapes=[
                pltpu.VMEM((2 * RAW_HALF, BS), F32),
                block(ZERO + 2, BF16), block(ZERO + 2, BF16),
                block(S_CAP + 1, F32), block(S_CAP + 1, BF16), block(S_CAP + 1, BF16),
                block(D_CAP + 1, F32), block(D_CAP + 1, BF16), block(D_CAP + 1, BF16),
                block(E_CAP + 1, F32), block(E_CAP + 1, BF16), block(E_CAP + 1, BF16),
                block(NB // 8 + 1, F32),
                pltpu.SemaphoreType.DMA((len(gathered),)),
            ],
            compiler_params=pltpu.CompilerParams(vmem_limit_bytes=60 * 2**20),
            name="purify_column",
        )(*tables, *gathered)

    def dense(density, pattern, tables, gathered):
        return dense_plan(density, pattern)

    return lax.cond(ok[0] != 0, sparse, dense, density, pattern, tables, gathered)


def solution(mesh):
    return jax.shard_map(
        per_device,
        mesh=mesh,
        in_specs=(P("row", ("col", "layer")), P()),
        out_specs=P("row", ("col", "layer")),
        check_vma=False,
    )
```

```python
import jax
import jax.numpy as jnp
from jax import lax
from jax.experimental import pallas as pl
from jax.experimental.pallas import tpu as pltpu
from jax.sharding import PartitionSpec as P

BS = 128
ITERS = 2
NB = 32
CAP = 4
NS = NB * CAP
ROUNDS = 8
ZERO = 2 * NS
S_CAP = 104
D_CAP = 80
E_CAP = NB
PAIRS = 256
UNROLL = 4
MANY = 4
LIST = 2 * PAIRS + 2 * UNROLL + 8
NZ, NC = 8, 2
NX, NY = 4, 4
SHARD = CAP * BS // 8
PART = SHARD // NC
UNIT = NZ * NC * PART
PANEL = 4 * UNIT
RAW_HALF = 4 * PANEL
WIDE = 40
WORD = 4096
F32 = jnp.float32
BF16 = jnp.bfloat16


def panel_cols(tile, layers):
    row_count, shard_cols = tile.shape
    gathered = lax.all_gather(tile, "row", axis=0, tiled=True)
    pieces = gathered.reshape(
        gathered.shape[0] // (shard_cols * layers), layers, shard_cols, shard_cols
    )
    arranged = lax.all_to_all(pieces, "layer", split_axis=1, concat_axis=3, tiled=True)
    return arranged.reshape(-1, layers * shard_cols)


def multiply(left_tile, right_panel):
    partial_sum = jnp.dot(
        lax.all_gather(left_tile, "col", axis=1, tiled=True),
        right_panel,
        precision=lax.Precision.HIGHEST,
        preferred_element_type=jnp.float32,
    )
    return lax.psum_scatter(partial_sum, "layer", scatter_dimension=1, tiled=True)


def dense_plan(density, pattern):
    row_index = lax.axis_index("row")
    col_index = lax.axis_index("col")
    layer_index = lax.axis_index("layer")
    layers = lax.axis_size("layer")
    row_count, shard_cols = density.shape
    blocks = pattern.shape[0]
    block_line = jnp.arange(blocks, dtype=jnp.int32)
    row_ids = (row_index * row_count + jnp.arange(row_count, dtype=jnp.int32)) // BS
    col_ids = (
        (col_index * layers + layer_index) * shard_cols + jnp.arange(shard_cols, dtype=jnp.int32)
    ) // BS
    pick_rows = (row_ids[:, None] == block_line[None, :]).astype(jnp.float32)
    pick_cols = (col_ids[:, None] == block_line[None, :]).astype(jnp.float32)
    occupied = pattern.astype(jnp.float32)
    in_pattern = jnp.dot(
        jnp.dot(pick_rows, occupied, precision=lax.Precision.HIGHEST),
        pick_cols.T,
        precision=lax.Precision.HIGHEST,
    )
    current = in_pattern * density
    for iteration in range(ITERS):
        current_panel = panel_cols(current, layers)
        squared = in_pattern * multiply(current, current_panel)
        cube_term = in_pattern * multiply(current, panel_cols(squared, layers))
        current = 3.0 * squared - 2.0 * cube_term
    return current


def here():
    row = lax.axis_index("row").astype(jnp.int32)
    column = lax.axis_index("col") * lax.axis_size("layer") + lax.axis_index("layer")
    return row, column.astype(jnp.int32)


def ring_place(source, at):
    back = (at - source) & 3
    return jnp.where(back == 3, 2, jnp.where(back == 2, 3, back))


def raw_row(column, p, h, j, r):
    px = ring_place((column & 1) * 2 + (p >> 2), (j & 1) * 2 + (r >> 2))
    py = ring_place(p & 3, r & 3)
    near, far = ((px, py), (py, px))[h]
    other = jnp.where(((j >> 1) & 1) == h, 0, 1)
    high = near >> 1
    group = jnp.where(far == 0, high, jnp.where(far == 3, 6 + high, 1 + 2 * high + far))
    return other * RAW_HALF + group * (PANEL // 2) + (near & 1) * UNIT + (column >> 1) * PART


def pack_kernel(pat_ref, tile_ref, packed_ref, own_ref, own_t_ref, rank_ref):
    r, j = here()
    K = (pat_ref[...] != 0).astype(F32)
    ii = lax.broadcasted_iota(jnp.int32, (NB, NB), 0)
    jj = lax.broadcasted_iota(jnp.int32, (NB, NB), 1)
    diag = (ii == jj).astype(F32)
    left = K * (1.0 - diag)
    own = diag
    own_t = diag
    after = (ii > jj).astype(F32)
    before = (ii < jj).astype(F32)
    for _ in range(ROUNDS):
        fc = (jnp.sum(left, axis=0, keepdims=True) <= CAP - 1).astype(F32)
        fr = (jnp.sum(left, axis=1, keepdims=True) <= CAP - 1).astype(F32)
        own = own + left * fc * ((1.0 - fr) + fr * after)
        own_t = own_t + left * fr * ((1.0 - fc) + fc * before)
        left = left * (1.0 - fc) * (1.0 - fr)
    own = own + left * after
    own_t = own_t + left * before
    rank = jnp.dot(after, own, preferred_element_type=F32)
    own_ref[...] = own
    own_t_ref[...] = own_t
    rank_ref[...] = rank

    for s in range(CAP):
        total = jnp.zeros((BS, BS), F32)
        for a in range(tile_ref.shape[0] // BS):
            at = (ii == r * (tile_ref.shape[0] // BS) + a) & (jj == j)
            pick = at & (own > 0) & (rank == s)
            w = jnp.sum(jnp.where(pick, 1.0, 0.0), axis=(0, 1), keepdims=True)
            total = total + w * tile_ref[a * BS : (a + 1) * BS, :]
        packed_ref[s * BS : (s + 1) * BS, :] = total


def plan_kernel(
    pat_ref, own_ref, own_t_ref, rank_ref,
    cid_ref, nbr_ref, deg_ref, needed_ref, count_ref, rows_a, rows_b, ok_ref,
):
    r, j = here()
    K = (pat_ref[...] != 0).astype(F32)
    ii = lax.broadcasted_iota(jnp.int32, (NB, NB), 0)
    jj = lax.broadcasted_iota(jnp.int32, (NB, NB), 1)
    before = (ii < jj).astype(F32)
    own = own_ref[...]
    own_t = own_t_ref[...]
    rank = rank_ref[...]
    rank_t = jnp.dot(own_t, before, preferred_element_type=F32)
    slot = jj * CAP + rank.astype(jnp.int32)
    slot_t = ii * CAP + rank_t.astype(jnp.int32)
    cid = jnp.where(own > 0, slot, jnp.where(own_t > 0, NS + slot_t, ZERO))
    cid_ref[...] = jnp.full(cid_ref.shape, ZERO, jnp.int32)
    cid_ref[:NB, :] = cid
    column = jnp.where(own > 0, jj, ii)
    turn = jnp.where(own > 0, rank, rank_t).astype(jnp.int32)
    for n, row_ref in enumerate((rows_a, rows_b)):
        first, second = [raw_row(column, 2 * turn + n, h, j, r) // PART for h in range(2)]
        row_ref[...] = first + second * WORD

    common = jnp.dot(K, K, preferred_element_type=F32)
    pairs = K * jnp.floor((common + 1.0) * 0.5)
    s_blocks = jnp.max(jnp.sum(common, axis=1))
    d_blocks = jnp.max(jnp.sum(common * K, axis=1))
    spread = jnp.dot(K, pairs, preferred_element_type=F32)
    s_pairs = jnp.max(jnp.sum(spread, axis=1))
    fits = (
        (jnp.max(jnp.sum(own, axis=0)) <= CAP)
        & (s_blocks <= S_CAP)
        & (d_blocks <= D_CAP)
        & (s_pairs <= PAIRS)
    )
    ok_ref[0] = fits.astype(jnp.int32)

    kj = jnp.sum(jnp.where(jj == j, K, 0.0), axis=1, keepdims=True)
    near = lax.dot_general(K * kj, K, (((0,), (0,)), ((), ())), preferred_element_type=F32)
    wanted = jnp.where((near > 0) & (K > 0), 1.0, 0.0)
    wide = lax.broadcasted_iota(jnp.int32, (NB, WIDE), 1)
    for listed, n_ref, entries in (
        (K, deg_ref, ((jj + cid * WORD, NB + ZERO * WORD, nbr_ref),)),
        (wanted, count_ref, ((jj, NB, needed_ref),)),
    ):
        place = jnp.dot(listed, before, preferred_element_type=F32).astype(jnp.int32)
        place = jnp.where(listed > 0, place, -1)
        size = jnp.sum(listed, axis=1, keepdims=True).astype(jnp.int32)
        for value, empty, list_ref in entries:
            out = jnp.full((NB, WIDE), empty, jnp.int32)
            for d in range(NB):
                entry = jnp.sum(jnp.where(place == d, value, 0), axis=1, keepdims=True)
                out = jnp.where((wide == d) & (size > d), entry, out)
            list_ref[...] = out
        n_ref[...] = jnp.broadcast_to(size, (NB, NB))


H_S, H_T, H_E, H_F, H_SB, H_DB, H_EB = range(7)


def block_kernel(ok_ref, cid, needed, count_in, rows_a, rows_b, head_ref, pn_ref, pt_ref, an_ref, at_ref):
    ok = ok_ref[0]

    def lines(i, carry):
        def entry(d, c):
            pn, pt = c
            k = needed[i, d]
            held = cid[i, k]
            rows = (rows_a[i, k], rows_b[i, k])
            flipped = (held >= NS).astype(jnp.int32)
            pn_ref[pn] = held
            pt_ref[pt] = held
            for n, row in enumerate(rows):
                an_ref[2 * pn + n] = row
                at_ref[2 * pt + n] = row
            return pn + (1 - flipped), pt + flipped

        return lax.fori_loop(0, count_in[i, 0] * ok, entry, carry)

    pn, pt = lax.fori_loop(0, NB, lines, (0, 0))
    for names, rows, n in ((pn_ref, an_ref, pn), (pt_ref, at_ref, pt)):
        for u in range(MANY - 1):
            names[n + u] = ZERO + 1
            for part in range(2):
                rows[2 * (n + u) + part] = 0
    head_ref[0] = pn
    head_ref[1] = pt


def table_kernel(
    ok_ref, cid, nbr, deg_in,
    head_ref, sl, sr, tt, el, er, fl, fr, ds_ref, fin_ref,
    did, eid,
):
    r, j = here()
    ok = ok_ref[0]
    nj = deg_in[j, 0] * ok

    def row(a, carry):
        m = nbr[j, a] & (WORD - 1)
        nm = deg_in[m, 0]
        base = carry[1] * WORD

        def output(b, c):
            pos, count, dcount, tcount = c
            k = nbr[m, b] & (WORD - 1)
            out = count * WORD

            def four(g, p):
                at = g * 4
                words = [nbr[m, at + u] for u in range(4)]
                rs = [cid[w & (WORD - 1), k] for w in words]
                for u in range(4):
                    sl[p] = (words[u] >> 12) + (base + (at + u) * WORD)
                    sr[p] = rs[u] + out
                    p = p + (rs[u] != ZERO).astype(jnp.int32)
                return p

            p = lax.fori_loop(0, (nm + 3) >> 2, four, pos)
            sl[p] = ZERO + S_CAP * WORD
            sr[p] = ZERO + out
            p = p + (p & 1)

            def reuse(pair, t):
                tt[t] = pair + dcount * WORD
                return t + 1

            inside = (cid[k, j] != ZERO).astype(jnp.int32)
            first = pos >> 1
            tcount = lax.fori_loop(first, first + inside * ((p >> 1) - first), reuse, tcount)
            did[m, k] = dcount
            ds_ref[dcount] = count
            return p, count + 1, dcount + inside, tcount

        return lax.fori_loop(0, nm, output, carry)

    pos, count, dcount, tcount = lax.fori_loop(0, nj, row, (0, 0, 0, 0))
    for t in range(2 * UNROLL):
        sl[pos + t] = ZERO + S_CAP * WORD
        sr[pos + t] = ZERO + S_CAP * WORD
    for t in range(UNROLL):
        tt[tcount + t] = (pos >> 1) + D_CAP * WORD
    for u in range(MANY - 1):
        ds_ref[dcount + u] = 0
    head_ref[H_S] = ((pos >> 1) + UNROLL - 1) // UNROLL
    head_ref[H_T] = (tcount + UNROLL - 1) // UNROLL
    head_ref[H_SB] = count
    head_ref[H_DB] = dcount

    def finish(refs, pos, lz, dummy):
        L, R = refs
        for t in range(2 * UNROLL):
            L[pos + t] = lz
            R[pos + t] = D_CAP + dummy * WORD
        return ((pos >> 1) + UNROLL - 1) // UNROLL

    def gather(refs, pos, k, left, out, lz):
        L, R = refs

        def entry(c, p):
            m = nbr[j, c] & (WORD - 1)
            L[p] = left(m)
            R[p] = did[m, k] + out * WORD
            return p + (cid[m, k] != ZERO).astype(jnp.int32)

        p = lax.fori_loop(0, nj, entry, pos)
        L[p] = lz
        R[p] = D_CAP + out * WORD
        return p + (p & 1)

    def e_out(b, pos):
        k = nbr[j, b] & (WORD - 1)
        eid[k] = b
        return gather((el, er), pos, k, lambda m: did[j, m], b, D_CAP)

    pos = lax.fori_loop(0, nj, e_out, 0)
    head_ref[H_E] = finish((el, er), pos, D_CAP, E_CAP)
    head_ref[H_EB] = nj

    per = NB // 8

    def f_out(a, pos):
        i = r * per + a

        def stored(pos):
            fin_ref[a] = eid[i]
            return gather((fl, fr), pos, i, lambda k: eid[k], a, E_CAP)

        def absent(pos):
            fin_ref[a] = -1
            return pos

        return lax.cond((cid[i, j] != ZERO) & (ok != 0), stored, absent, pos)

    pos = lax.fori_loop(0, per, f_out, 0)
    head_ref[H_F] = finish((fl, fr), pos, E_CAP, per)


def split(x):
    hi = x.astype(BF16)
    return hi, (x - hi.astype(F32)).astype(BF16)


def compute_kernel(
    blocks_ref, pn_ref, pt_ref, an_ref, at_ref, head_ref, sl, sr, tt, el, er, fl, fr, ds_ref, fin_ref,
    *rest,
):
    pieces, rest = rest[:-15], rest[-15:]
    out_ref, raw, ch, cl, sa, sh, slo, da, dh, dl, ea, eh, elo, fa, sem = rest
    copies = []
    row = 0
    for n, piece in enumerate(pieces):
        height = piece.shape[0]
        copies.append(pltpu.make_async_copy(piece, raw.at[pl.ds(row, height)], sem.at[n]))
        row += height
    for c in copies:
        c.start()
    zero = jnp.zeros((BS, BS), BF16)
    for hi, lo, at in ((ch, cl, ZERO), (sh, slo, S_CAP), (dh, dl, D_CAP), (eh, elo, E_CAP)):
        hi[at] = zero
        lo[at] = zero

    def clear(ref, n):
        @pl.loop(0, n)
        def _(t):
            ref[t] = jnp.zeros((BS, BS), F32)

    clear(sa, head_ref[H_SB])
    clear(da, head_ref[H_DB])
    clear(ea, head_ref[H_EB])
    clear(fa, fa.shape[0])
    for c in copies:
        c.wait()

    def prepare(n, names, rows, turn):
        @pl.loop(0, (n + MANY - 1) // MANY)
        def _(t):
            ids = [names[MANY * t + u] for u in range(MANY)]
            xs = []
            for u in range(MANY):
                words = [rows[2 * (MANY * t + u) + n] for n in range(2)]
                starts = [w & (WORD - 1) if h == 0 else w >> 12 for w in words for h in range(2)]
                parts = [raw[pl.ds(pl.multiple_of(at * PART, PART), PART), :] for at in starts]
                xs.append(split(turn(jnp.concatenate(parts, axis=0))))
            for a, (hi, lo) in zip(ids, xs):
                ch[a] = hi
                cl[a] = lo

    prepare(blocks_ref[0], pn_ref, an_ref, lambda v: v)
    prepare(blocks_ref[1], pt_ref, at_ref, lambda v: v.T)

    def phase(n, task, left, right, acc):
        lh, ll = left
        rh, rl = right

        @pl.loop(0, n)
        def _(t):
            sums = []
            outs = []
            for u in range(UNROLL):
                a0, a1, b0, b1, out = task(t * UNROLL + u)
                lhs = jnp.concatenate(
                    [
                        jnp.concatenate([lh[a0], lh[a1]], axis=1),
                        jnp.concatenate([ll[a0], ll[a1]], axis=1),
                    ],
                    axis=0,
                )
                rhs = jnp.concatenate(
                    [
                        jnp.concatenate([rh[b0], rl[b0]], axis=1),
                        jnp.concatenate([rh[b1], rl[b1]], axis=1),
                    ],
                    axis=0,
                )
                both = jnp.dot(lhs, rhs, preferred_element_type=F32)
                sums.append(both[:BS, :BS] + (both[:BS, BS:] + both[BS:, :BS]))
                outs.append(out)
            for u in range(UNROLL):
                acc[outs[u]] = acc[outs[u]] + sums[u]

    def plain(L, R):
        def task(t):
            r0 = R[2 * t]
            low = lambda w: w & (WORD - 1)
            return low(L[2 * t]), low(L[2 * t + 1]), low(r0), low(R[2 * t + 1]), r0 >> 12

        return task

    def cube(t):
        word = tt[t]
        at = 2 * (word & (WORD - 1))
        return sl[at] >> 12, sl[at + 1] >> 12, sr[at] & (WORD - 1), sr[at + 1] & (WORD - 1), word >> 12

    phase(head_ref[H_S], plain(sl, sr), (ch, cl), (ch, cl), sa)

    @pl.loop(0, (head_ref[H_SB] + MANY - 1) // MANY)
    def _(t):
        done = [split(sa[MANY * t + u]) for u in range(MANY)]
        for u in range(MANY):
            sh[MANY * t + u], slo[MANY * t + u] = done[u]

    phase(head_ref[H_T], cube, (sh, slo), (ch, cl), da)

    @pl.loop(0, (head_ref[H_DB] + MANY - 1) // MANY)
    def _(t):
        done = [split(3.0 * sa[ds_ref[MANY * t + u]] - 2.0 * da[MANY * t + u]) for u in range(MANY)]
        for u in range(MANY):
            dh[MANY * t + u], dl[MANY * t + u] = done[u]

    phase(head_ref[H_E], plain(el, er), (dh, dl), (dh, dl), ea)

    @pl.loop(0, head_ref[H_EB])
    def _(t):
        eh[t], elo[t] = split(ea[t])

    phase(head_ref[H_F], plain(fl, fr), (eh, elo), (dh, dl), fa)
    for a in range(out_ref.shape[0] // BS):
        at = fin_ref[a]
        value = 3.0 * ea[jnp.maximum(at, 0)] - 2.0 * fa[a]
        out_ref[a * BS : (a + 1) * BS, :] = jnp.where(at >= 0, value.T, 0.0)


def linear(x, y, z, core):
    return (((x % 2) * NY + y) * (NZ * NC) + z * NC + core) * 2 + x // 2


def send(value, step):
    pairs = [
        (linear(x, y, z, core), linear(*step(x, y, z, core)))
        for x in range(NX)
        for y in range(NY)
        for z in range(NZ)
        for core in range(NC)
    ]
    return lax.ppermute(value, ("row", "col", "layer"), pairs)


def along_z(d):
    return lambda x, y, z, core: (x, y, (z + d) % NZ, core)


def inner(d):
    return lambda x, y, z, core: ((x + d) % NX, y, z, core) if core == 0 else (x, (y + d) % NY, z, core)


def outer(d):
    return lambda x, y, z, core: (x, (y + d) % NY, z, core) if core == 0 else ((x + d) % NX, y, z, core)


def other_core(x, y, z, core):
    return x, y, z, 1 - core


def list_blocks(ok, *plan):
    smem = pl.BlockSpec(memory_space=pltpu.SMEM)
    i32 = lambda *shape: jax.ShapeDtypeStruct(shape, jnp.int32)
    return pl.pallas_call(
        block_kernel,
        out_shape=[i32(8), *[i32(2 * NS + 8)] * 2, *[i32(4 * NS + 16)] * 2],
        in_specs=[smem] * 6,
        out_specs=[smem] * 5,
        cost_estimate=pl.CostEstimate(flops=0, bytes_accessed=6_000_000, transcendentals=0),
        name="list_blocks",
    )(ok, *plan)


def list_products(ok, *plan):
    smem = pl.BlockSpec(memory_space=pltpu.SMEM)
    i32 = lambda *shape: jax.ShapeDtypeStruct(shape, jnp.int32)
    return pl.pallas_call(
        table_kernel,
        out_shape=[i32(16), *[i32(LIST)] * 7, i32(D_CAP + MANY), i32(8)],
        in_specs=[smem] * 4,
        out_specs=[smem] * 10,
        scratch_shapes=[
            pltpu.SMEM((NB, NB), jnp.int32),
            pltpu.SMEM((NB,), jnp.int32),
        ],
        cost_estimate=pl.CostEstimate(flops=0, bytes_accessed=20_000_000, transcendentals=0),
        name="list_products",
    )(ok, *plan)


def plan_products(pattern, *owners):
    smem = pl.BlockSpec(memory_space=pltpu.SMEM)
    vmem = pl.BlockSpec(memory_space=pltpu.VMEM)
    i32 = lambda *shape: jax.ShapeDtypeStruct(shape, jnp.int32)
    return pl.pallas_call(
        plan_kernel,
        out_shape=(
            i32(WIDE, NB), i32(NB, WIDE), i32(NB, NB), i32(NB, WIDE), i32(NB, NB),
            *[i32(NB, NB)] * 2,
            i32(1),
        ),
        in_specs=[vmem] * 4,
        out_specs=(*[vmem] * 7, smem),
        cost_estimate=pl.CostEstimate(flops=0, bytes_accessed=10_000_000, transcendentals=0),
        name="plan_products",
    )(pattern, *owners)


def to_chips_along_z(shard):
    parts = jnp.broadcast_to(shard.reshape(NC, PART, BS), (NZ, NC, PART, BS)).reshape(NZ * NC, PART, BS)
    return lax.all_to_all(parts, "col", split_axis=0, concat_axis=0, tiled=True).reshape(UNIT, BS)


def gather_pieces(shard, pattern, owners):
    tie = lax.optimization_barrier
    swap = lambda value: send(value, other_core)
    own = to_chips_along_z(shard)
    back, ahead, opposite = [send(own, inner(d)) for d in (1, -1, 2)]

    back, owners = tie((back, owners))
    low = jnp.concatenate([own, back], axis=0)
    back_low, ahead_low = send(low, outer(1)), send(low, outer(-1))
    their_low = swap(low)
    cid, nbr, deg, needed, count, rows_a, rows_b, ok = plan_products(pattern, *owners)
    blocks = list_blocks(ok, cid, needed, count, rows_a, rows_b)
    ahead, opposite, blocks = tie((ahead, opposite, blocks))

    high = jnp.concatenate([ahead, opposite], axis=0)
    back_high, ahead_high = send(high, outer(1)), send(high, outer(-1))
    their_high = swap(high)
    back_low, ahead_low, cid = tie((back_low, ahead_low, cid))
    far_low = send(back_low, outer(1))
    middle = [swap(back_low), swap(ahead_low)]
    tables = list_products(ok, cid, nbr, deg)
    back_high, ahead_high, far_low, tables = tie((back_high, ahead_high, far_low, tables))
    far_high = send(ahead_high, outer(-1))
    last = [swap(back_high), swap(ahead_high), swap(far_low)]
    far_high = tie(far_high)
    mine = [low, high, back_low, ahead_low, back_high, ahead_high, far_low, far_high]
    return ok, [*blocks, *tables], [*mine, their_low, their_high, *middle, *last, swap(far_high)]


def per_device(density, pattern):
    smem = pl.BlockSpec(memory_space=pltpu.SMEM)
    vmem = pl.BlockSpec(memory_space=pltpu.VMEM)

    square = jax.ShapeDtypeStruct((NB, NB), F32)
    packed, *owners = pl.pallas_call(
        pack_kernel,
        out_shape=(jax.ShapeDtypeStruct((CAP * BS, BS), F32), square, square, square),
        in_specs=[vmem, vmem],
        out_specs=[vmem] * 4,
        name="pack_blocks",
    )(pattern, density)

    rows = lax.axis_size("row")
    pieces = packed.reshape(rows, SHARD, BS)
    shard = jnp.sum(lax.all_to_all(pieces, "row", split_axis=0, concat_axis=0, tiled=True), axis=0)
    ok, tables, gathered = gather_pieces(shard, pattern, owners)

    def sparse(density, pattern, tables, gathered):
        block = lambda n, t: pltpu.VMEM((n, BS, BS), t)
        return pl.pallas_call(
            compute_kernel,
            out_shape=jax.ShapeDtypeStruct(density.shape, F32),
            in_specs=[smem] * len(tables) + [pl.BlockSpec(memory_space=pl.ANY)] * len(gathered),
            out_specs=vmem,
            scratch_shapes=[
                pltpu.VMEM((2 * RAW_HALF, BS), F32),
                block(ZERO + 2, BF16), block(ZERO + 2, BF16),
                block(S_CAP + 1, F32), block(S_CAP + 1, BF16), block(S_CAP + 1, BF16),
                block(D_CAP + 1, F32), block(D_CAP + 1, BF16), block(D_CAP + 1, BF16),
                block(E_CAP + 1, F32), block(E_CAP + 1, BF16), block(E_CAP + 1, BF16),
                block(NB // 8 + 1, F32),
                pltpu.SemaphoreType.DMA((len(gathered),)),
            ],
            compiler_params=pltpu.CompilerParams(vmem_limit_bytes=60 * 2**20),
            name="purify_column",
        )(*tables, *gathered)

    def dense(density, pattern, tables, gathered):
        return dense_plan(density, pattern)

    return lax.cond(ok[0] != 0, sparse, dense, density, pattern, tables, gathered)


def solution(mesh):
    return jax.shard_map(
        per_device,
        mesh=mesh,
        in_specs=(P("row", ("col", "layer")), P()),
        out_specs=P("row", ("col", "layer")),
        check_vma=False,
    )
```

```python
import jax
import jax.numpy as jnp
from jax import lax
from jax.experimental import pallas as pl
from jax.experimental.pallas import tpu as pltpu
from jax.sharding import PartitionSpec as P

BS = 128
ITERS = 2
NB = 32
CAP = 4
NS = NB * CAP
ROUNDS = 8
ZERO = 2 * NS
S_CAP = 104
D_CAP = 80
E_CAP = NB
PAIRS = 256
UNROLL = 4
MANY = 4
LIST = 2 * PAIRS + 2 * UNROLL + 8
NZ, NC = 8, 2
NX, NY = 4, 4
SHARD = CAP * BS // 8
PART = SHARD // NC
UNIT = NZ * NC * PART
PANEL = 4 * UNIT
RAW_HALF = 4 * PANEL
WIDE = 40
WORD = 4096
F32 = jnp.float32
BF16 = jnp.bfloat16


def panel_cols(tile, layers):
    row_count, shard_cols = tile.shape
    gathered = lax.all_gather(tile, "row", axis=0, tiled=True)
    pieces = gathered.reshape(
        gathered.shape[0] // (shard_cols * layers), layers, shard_cols, shard_cols
    )
    arranged = lax.all_to_all(pieces, "layer", split_axis=1, concat_axis=3, tiled=True)
    return arranged.reshape(-1, layers * shard_cols)


def multiply(left_tile, right_panel):
    partial_sum = jnp.dot(
        lax.all_gather(left_tile, "col", axis=1, tiled=True),
        right_panel,
        precision=lax.Precision.HIGHEST,
        preferred_element_type=jnp.float32,
    )
    return lax.psum_scatter(partial_sum, "layer", scatter_dimension=1, tiled=True)


def dense_plan(density, pattern):
    row_index = lax.axis_index("row")
    col_index = lax.axis_index("col")
    layer_index = lax.axis_index("layer")
    layers = lax.axis_size("layer")
    row_count, shard_cols = density.shape
    blocks = pattern.shape[0]
    block_line = jnp.arange(blocks, dtype=jnp.int32)
    row_ids = (row_index * row_count + jnp.arange(row_count, dtype=jnp.int32)) // BS
    col_ids = (
        (col_index * layers + layer_index) * shard_cols + jnp.arange(shard_cols, dtype=jnp.int32)
    ) // BS
    pick_rows = (row_ids[:, None] == block_line[None, :]).astype(jnp.float32)
    pick_cols = (col_ids[:, None] == block_line[None, :]).astype(jnp.float32)
    occupied = pattern.astype(jnp.float32)
    in_pattern = jnp.dot(
        jnp.dot(pick_rows, occupied, precision=lax.Precision.HIGHEST),
        pick_cols.T,
        precision=lax.Precision.HIGHEST,
    )
    current = in_pattern * density
    for iteration in range(ITERS):
        current_panel = panel_cols(current, layers)
        squared = in_pattern * multiply(current, current_panel)
        cube_term = in_pattern * multiply(current, panel_cols(squared, layers))
        current = 3.0 * squared - 2.0 * cube_term
    return current


def here():
    row = lax.axis_index("row").astype(jnp.int32)
    column = lax.axis_index("col") * lax.axis_size("layer") + lax.axis_index("layer")
    return row, column.astype(jnp.int32)


def ring_place(source, at):
    back = (at - source) & 3
    return jnp.where(back == 3, 2, jnp.where(back == 2, 3, back))


def raw_row(column, p, h, j, r):
    px = ring_place((column & 1) * 2 + (p >> 2), (j & 1) * 2 + (r >> 2))
    py = ring_place(p & 3, r & 3)
    near, far = ((px, py), (py, px))[h]
    other = jnp.where(((j >> 1) & 1) == h, 0, 1)
    high = near >> 1
    ring = 2 + jnp.where(far == 1, 2 * high, 3 - 2 * high)
    group = jnp.where(far == 0, high, jnp.where(far == 3, 6 + high, ring))
    return other * RAW_HALF + group * (PANEL // 2) + (near & 1) * UNIT + (column >> 1) * PART


def pack_kernel(pat_ref, tile_ref, packed_ref, own_ref, own_t_ref, rank_ref):
    r, j = here()
    K = (pat_ref[...] != 0).astype(F32)
    ii = lax.broadcasted_iota(jnp.int32, (NB, NB), 0)
    jj = lax.broadcasted_iota(jnp.int32, (NB, NB), 1)
    diag = (ii == jj).astype(F32)
    left = K * (1.0 - diag)
    own = diag
    own_t = diag
    after = (ii > jj).astype(F32)
    before = (ii < jj).astype(F32)
    for _ in range(ROUNDS):
        fc = (jnp.sum(left, axis=0, keepdims=True) <= CAP - 1).astype(F32)
        fr = (jnp.sum(left, axis=1, keepdims=True) <= CAP - 1).astype(F32)
        own = own + left * fc * ((1.0 - fr) + fr * after)
        own_t = own_t + left * fr * ((1.0 - fc) + fc * before)
        left = left * (1.0 - fc) * (1.0 - fr)
    own = own + left * after
    own_t = own_t + left * before
    rank = jnp.dot(after, own, preferred_element_type=F32)
    own_ref[...] = own
    own_t_ref[...] = own_t
    rank_ref[...] = rank

    for s in range(CAP):
        total = jnp.zeros((BS, BS), F32)
        for a in range(tile_ref.shape[0] // BS):
            at = (ii == r * (tile_ref.shape[0] // BS) + a) & (jj == j)
            pick = at & (own > 0) & (rank == s)
            w = jnp.sum(jnp.where(pick, 1.0, 0.0), axis=(0, 1), keepdims=True)
            total = total + w * tile_ref[a * BS : (a + 1) * BS, :]
        packed_ref[s * BS : (s + 1) * BS, :] = total


def plan_kernel(
    pat_ref, own_ref, own_t_ref, rank_ref,
    cid_ref, nbr_ref, deg_ref, needed_ref, count_ref, rows_a, rows_b, ok_ref,
):
    r, j = here()
    K = (pat_ref[...] != 0).astype(F32)
    ii = lax.broadcasted_iota(jnp.int32, (NB, NB), 0)
    jj = lax.broadcasted_iota(jnp.int32, (NB, NB), 1)
    before = (ii < jj).astype(F32)
    own = own_ref[...]
    own_t = own_t_ref[...]
    rank = rank_ref[...]
    rank_t = jnp.dot(own_t, before, preferred_element_type=F32)
    slot = jj * CAP + rank.astype(jnp.int32)
    slot_t = ii * CAP + rank_t.astype(jnp.int32)
    cid = jnp.where(own > 0, slot, jnp.where(own_t > 0, NS + slot_t, ZERO))
    cid_ref[...] = jnp.full(cid_ref.shape, ZERO, jnp.int32)
    cid_ref[:NB, :] = cid
    column = jnp.where(own > 0, jj, ii)
    turn = jnp.where(own > 0, rank, rank_t).astype(jnp.int32)
    for n, row_ref in enumerate((rows_a, rows_b)):
        first, second = [raw_row(column, 2 * turn + n, h, j, r) // PART for h in range(2)]
        row_ref[...] = first + second * WORD

    common = jnp.dot(K, K, preferred_element_type=F32)
    pairs = K * jnp.floor((common + 1.0) * 0.5)
    s_blocks = jnp.max(jnp.sum(common, axis=1))
    d_blocks = jnp.max(jnp.sum(common * K, axis=1))
    spread = jnp.dot(K, pairs, preferred_element_type=F32)
    s_pairs = jnp.max(jnp.sum(spread, axis=1))
    fits = (
        (jnp.max(jnp.sum(own, axis=0)) <= CAP)
        & (s_blocks <= S_CAP)
        & (d_blocks <= D_CAP)
        & (s_pairs <= PAIRS)
    )
    ok_ref[0] = fits.astype(jnp.int32)

    kj = jnp.sum(jnp.where(jj == j, K, 0.0), axis=1, keepdims=True)
    near = lax.dot_general(K * kj, K, (((0,), (0,)), ((), ())), preferred_element_type=F32)
    wanted = jnp.where((near > 0) & (K > 0), 1.0, 0.0)
    wide = lax.broadcasted_iota(jnp.int32, (NB, WIDE), 1)
    for listed, n_ref, entries in (
        (K, deg_ref, ((jj + cid * WORD, NB + ZERO * WORD, nbr_ref),)),
        (wanted, count_ref, ((jj, NB, needed_ref),)),
    ):
        place = jnp.dot(listed, before, preferred_element_type=F32).astype(jnp.int32)
        place = jnp.where(listed > 0, place, -1)
        size = jnp.sum(listed, axis=1, keepdims=True).astype(jnp.int32)
        for value, empty, list_ref in entries:
            out = jnp.full((NB, WIDE), empty, jnp.int32)
            for d in range(NB):
                entry = jnp.sum(jnp.where(place == d, value, 0), axis=1, keepdims=True)
                out = jnp.where((wide == d) & (size > d), entry, out)
            list_ref[...] = out
        n_ref[...] = jnp.broadcast_to(size, (NB, NB))


H_S, H_T, H_E, H_F, H_SB, H_DB, H_EB = range(7)


def block_kernel(ok_ref, cid, needed, count_in, rows_a, rows_b, head_ref, pn_ref, pt_ref, an_ref, at_ref):
    ok = ok_ref[0]

    def lines(i, carry):
        def entry(d, c):
            pn, pt = c
            k = needed[i, d]
            held = cid[i, k]
            rows = (rows_a[i, k], rows_b[i, k])
            flipped = (held >= NS).astype(jnp.int32)
            pn_ref[pn] = held
            pt_ref[pt] = held
            for n, row in enumerate(rows):
                an_ref[2 * pn + n] = row
                at_ref[2 * pt + n] = row
            return pn + (1 - flipped), pt + flipped

        return lax.fori_loop(0, count_in[i, 0] * ok, entry, carry)

    pn, pt = lax.fori_loop(0, NB, lines, (0, 0))
    for names, rows, n in ((pn_ref, an_ref, pn), (pt_ref, at_ref, pt)):
        for u in range(MANY - 1):
            names[n + u] = ZERO + 1
            for part in range(2):
                rows[2 * (n + u) + part] = 0
    head_ref[0] = pn
    head_ref[1] = pt


def table_kernel(
    ok_ref, cid, nbr, deg_in,
    head_ref, sl, sr, tt, el, er, fl, fr, ds_ref, fin_ref,
    did, eid,
):
    r, j = here()
    ok = ok_ref[0]
    nj = deg_in[j, 0] * ok

    def row(a, carry):
        m = nbr[j, a] & (WORD - 1)
        nm = deg_in[m, 0]
        base = carry[1] * WORD

        def output(b, c):
            pos, count, dcount, tcount = c
            k = nbr[m, b] & (WORD - 1)
            out = count * WORD

            def four(g, p):
                at = g * 4
                words = [nbr[m, at + u] for u in range(4)]
                rs = [cid[w & (WORD - 1), k] for w in words]
                for u in range(4):
                    sl[p] = (words[u] >> 12) + (base + (at + u) * WORD)
                    sr[p] = rs[u] + out
                    p = p + (rs[u] != ZERO).astype(jnp.int32)
                return p

            p = lax.fori_loop(0, (nm + 3) >> 2, four, pos)
            sl[p] = ZERO + S_CAP * WORD
            sr[p] = ZERO + out
            p = p + (p & 1)

            def reuse(pair, t):
                tt[t] = pair + dcount * WORD
                return t + 1

            inside = (cid[k, j] != ZERO).astype(jnp.int32)
            first = pos >> 1
            tcount = lax.fori_loop(first, first + inside * ((p >> 1) - first), reuse, tcount)
            did[m, k] = dcount
            ds_ref[dcount] = count
            return p, count + 1, dcount + inside, tcount

        return lax.fori_loop(0, nm, output, carry)

    pos, count, dcount, tcount = lax.fori_loop(0, nj, row, (0, 0, 0, 0))
    for t in range(2 * UNROLL):
        sl[pos + t] = ZERO + S_CAP * WORD
        sr[pos + t] = ZERO + S_CAP * WORD
    for t in range(UNROLL):
        tt[tcount + t] = (pos >> 1) + D_CAP * WORD
    for u in range(MANY - 1):
        ds_ref[dcount + u] = 0
    head_ref[H_S] = ((pos >> 1) + UNROLL - 1) // UNROLL
    head_ref[H_T] = (tcount + UNROLL - 1) // UNROLL
    head_ref[H_SB] = count
    head_ref[H_DB] = dcount

    def finish(refs, pos, lz, dummy):
        L, R = refs
        for t in range(2 * UNROLL):
            L[pos + t] = lz
            R[pos + t] = D_CAP + dummy * WORD
        return ((pos >> 1) + UNROLL - 1) // UNROLL

    def gather(refs, pos, k, left, out, lz):
        L, R = refs

        def entry(c, p):
            m = nbr[j, c] & (WORD - 1)
            L[p] = left(m)
            R[p] = did[m, k] + out * WORD
            return p + (cid[m, k] != ZERO).astype(jnp.int32)

        p = lax.fori_loop(0, nj, entry, pos)
        L[p] = lz
        R[p] = D_CAP + out * WORD
        return p + (p & 1)

    def e_out(b, pos):
        k = nbr[j, b] & (WORD - 1)
        eid[k] = b
        return gather((el, er), pos, k, lambda m: did[j, m], b, D_CAP)

    pos = lax.fori_loop(0, nj, e_out, 0)
    head_ref[H_E] = finish((el, er), pos, D_CAP, E_CAP)
    head_ref[H_EB] = nj

    per = NB // 8

    def f_out(a, pos):
        i = r * per + a

        def stored(pos):
            fin_ref[a] = eid[i]
            return gather((fl, fr), pos, i, lambda k: eid[k], a, E_CAP)

        def absent(pos):
            fin_ref[a] = -1
            return pos

        return lax.cond((cid[i, j] != ZERO) & (ok != 0), stored, absent, pos)

    pos = lax.fori_loop(0, per, f_out, 0)
    head_ref[H_F] = finish((fl, fr), pos, E_CAP, per)


def split(x):
    hi = x.astype(BF16)
    return hi, (x - hi.astype(F32)).astype(BF16)


def compute_kernel(
    blocks_ref, pn_ref, pt_ref, an_ref, at_ref, head_ref, sl, sr, tt, el, er, fl, fr, ds_ref, fin_ref,
    *rest,
):
    pieces, rest = rest[:-15], rest[-15:]
    out_ref, raw, ch, cl, sa, sh, slo, da, dh, dl, ea, eh, elo, fa, sem = rest
    copies = []
    row = 0
    for n, piece in enumerate(pieces):
        height = piece.shape[0]
        copies.append(pltpu.make_async_copy(piece, raw.at[pl.ds(row, height)], sem.at[n]))
        row += height
    for c in copies:
        c.start()
    zero = jnp.zeros((BS, BS), BF16)
    for hi, lo, at in ((ch, cl, ZERO), (sh, slo, S_CAP), (dh, dl, D_CAP), (eh, elo, E_CAP)):
        hi[at] = zero
        lo[at] = zero

    def clear(ref, n):
        @pl.loop(0, n)
        def _(t):
            ref[t] = jnp.zeros((BS, BS), F32)

    clear(sa, head_ref[H_SB])
    clear(da, head_ref[H_DB])
    clear(ea, head_ref[H_EB])
    clear(fa, fa.shape[0])
    for c in copies:
        c.wait()

    def prepare(n, names, rows, turn):
        @pl.loop(0, (n + MANY - 1) // MANY)
        def _(t):
            ids = [names[MANY * t + u] for u in range(MANY)]
            xs = []
            for u in range(MANY):
                words = [rows[2 * (MANY * t + u) + n] for n in range(2)]
                starts = [w & (WORD - 1) if h == 0 else w >> 12 for w in words for h in range(2)]
                parts = [raw[pl.ds(pl.multiple_of(at * PART, PART), PART), :] for at in starts]
                xs.append(split(turn(jnp.concatenate(parts, axis=0))))
            for a, (hi, lo) in zip(ids, xs):
                ch[a] = hi
                cl[a] = lo

    prepare(blocks_ref[0], pn_ref, an_ref, lambda v: v)
    prepare(blocks_ref[1], pt_ref, at_ref, lambda v: v.T)

    def phase(n, task, left, right, acc):
        lh, ll = left
        rh, rl = right

        @pl.loop(0, n)
        def _(t):
            sums = []
            outs = []
            for u in range(UNROLL):
                a0, a1, b0, b1, out = task(t * UNROLL + u)
                lhs = jnp.concatenate(
                    [
                        jnp.concatenate([lh[a0], lh[a1]], axis=1),
                        jnp.concatenate([ll[a0], ll[a1]], axis=1),
                    ],
                    axis=0,
                )
                rhs = jnp.concatenate(
                    [
                        jnp.concatenate([rh[b0], rl[b0]], axis=1),
                        jnp.concatenate([rh[b1], rl[b1]], axis=1),
                    ],
                    axis=0,
                )
                both = jnp.dot(lhs, rhs, preferred_element_type=F32)
                sums.append(both[:BS, :BS] + (both[:BS, BS:] + both[BS:, :BS]))
                outs.append(out)
            for u in range(UNROLL):
                acc[outs[u]] = acc[outs[u]] + sums[u]

    def plain(L, R):
        def task(t):
            r0 = R[2 * t]
            low = lambda w: w & (WORD - 1)
            return low(L[2 * t]), low(L[2 * t + 1]), low(r0), low(R[2 * t + 1]), r0 >> 12

        return task

    def cube(t):
        word = tt[t]
        at = 2 * (word & (WORD - 1))
        return sl[at] >> 12, sl[at + 1] >> 12, sr[at] & (WORD - 1), sr[at + 1] & (WORD - 1), word >> 12

    phase(head_ref[H_S], plain(sl, sr), (ch, cl), (ch, cl), sa)

    @pl.loop(0, (head_ref[H_SB] + MANY - 1) // MANY)
    def _(t):
        done = [split(sa[MANY * t + u]) for u in range(MANY)]
        for u in range(MANY):
            sh[MANY * t + u], slo[MANY * t + u] = done[u]

    phase(head_ref[H_T], cube, (sh, slo), (ch, cl), da)

    @pl.loop(0, (head_ref[H_DB] + MANY - 1) // MANY)
    def _(t):
        done = [split(3.0 * sa[ds_ref[MANY * t + u]] - 2.0 * da[MANY * t + u]) for u in range(MANY)]
        for u in range(MANY):
            dh[MANY * t + u], dl[MANY * t + u] = done[u]

    phase(head_ref[H_E], plain(el, er), (dh, dl), (dh, dl), ea)

    @pl.loop(0, head_ref[H_EB])
    def _(t):
        eh[t], elo[t] = split(ea[t])

    phase(head_ref[H_F], plain(fl, fr), (eh, elo), (dh, dl), fa)
    for a in range(out_ref.shape[0] // BS):
        at = fin_ref[a]
        value = 3.0 * ea[jnp.maximum(at, 0)] - 2.0 * fa[a]
        out_ref[a * BS : (a + 1) * BS, :] = jnp.where(at >= 0, value.T, 0.0)


def linear(x, y, z, core):
    return (((x % 2) * NY + y) * (NZ * NC) + z * NC + core) * 2 + x // 2


def send(value, step):
    pairs = [
        (linear(x, y, z, core), linear(*step(x, y, z, core)))
        for x in range(NX)
        for y in range(NY)
        for z in range(NZ)
        for core in range(NC)
    ]
    return lax.ppermute(value, ("row", "col", "layer"), pairs)


def along_z(d):
    return lambda x, y, z, core: (x, y, (z + d) % NZ, core)


def inner(d):
    return lambda x, y, z, core: ((x + d) % NX, y, z, core) if core == 0 else (x, (y + d) % NY, z, core)


def outer(d):
    return lambda x, y, z, core: (x, (y + d) % NY, z, core) if core == 0 else ((x + d) % NX, y, z, core)


def other_core(x, y, z, core):
    return x, y, z, 1 - core


def list_blocks(ok, *plan):
    smem = pl.BlockSpec(memory_space=pltpu.SMEM)
    i32 = lambda *shape: jax.ShapeDtypeStruct(shape, jnp.int32)
    return pl.pallas_call(
        block_kernel,
        out_shape=[i32(8), *[i32(2 * NS + 8)] * 2, *[i32(4 * NS + 16)] * 2],
        in_specs=[smem] * 6,
        out_specs=[smem] * 5,
        cost_estimate=pl.CostEstimate(flops=0, bytes_accessed=6_000_000, transcendentals=0),
        name="list_blocks",
    )(ok, *plan)


def list_products(ok, *plan):
    smem = pl.BlockSpec(memory_space=pltpu.SMEM)
    i32 = lambda *shape: jax.ShapeDtypeStruct(shape, jnp.int32)
    return pl.pallas_call(
        table_kernel,
        out_shape=[i32(16), *[i32(LIST)] * 7, i32(D_CAP + MANY), i32(8)],
        in_specs=[smem] * 4,
        out_specs=[smem] * 10,
        scratch_shapes=[
            pltpu.SMEM((NB, NB), jnp.int32),
            pltpu.SMEM((NB,), jnp.int32),
        ],
        cost_estimate=pl.CostEstimate(flops=0, bytes_accessed=20_000_000, transcendentals=0),
        name="list_products",
    )(ok, *plan)


def plan_products(pattern, *owners):
    smem = pl.BlockSpec(memory_space=pltpu.SMEM)
    vmem = pl.BlockSpec(memory_space=pltpu.VMEM)
    i32 = lambda *shape: jax.ShapeDtypeStruct(shape, jnp.int32)
    return pl.pallas_call(
        plan_kernel,
        out_shape=(
            i32(WIDE, NB), i32(NB, WIDE), i32(NB, NB), i32(NB, WIDE), i32(NB, NB),
            *[i32(NB, NB)] * 2,
            i32(1),
        ),
        in_specs=[vmem] * 4,
        out_specs=(*[vmem] * 7, smem),
        cost_estimate=pl.CostEstimate(flops=0, bytes_accessed=10_000_000, transcendentals=0),
        name="plan_products",
    )(pattern, *owners)


def to_chips_along_z(shard):
    core = lax.axis_index("col") % NC
    pick = lambda a, b: jnp.where(core == 0, a, b)
    halves = shard[:PART], shard[PART:]
    kept, given = pick(*halves), pick(*halves[::-1])
    got = send(given, other_core)
    unit = jnp.concatenate([pick(kept, got), pick(got, kept)], axis=0)
    lines = [[z * NC + c for z in range(NZ)] for c in range(NC)]
    copies = jnp.broadcast_to(unit, (NZ, SHARD, BS))
    return lax.all_to_all(
        copies, "col", split_axis=0, concat_axis=0, tiled=True, axis_index_groups=lines
    ).reshape(UNIT, BS)


def gather_pieces(shard, pattern, owners):
    tie = lax.optimization_barrier
    swap = lambda value: send(value, other_core)
    own = to_chips_along_z(shard)
    own, owners = tie((own, owners))
    line = [own] + [send(own, inner(d)) for d in (1, -1, 2)]
    cid, nbr, deg, needed, count, rows_a, rows_b, ok = plan_products(pattern, *owners)
    blocks = list_blocks(ok, cid, needed, count, rows_a, rows_b)
    line, blocks = tie((line, blocks))

    low, high = jnp.concatenate(line[:2], axis=0), jnp.concatenate(line[2:], axis=0)
    low, high, cid, nbr, deg = tie((low, high, cid, nbr, deg))
    back_low, ahead_high = send(low, outer(1)), send(high, outer(-1))
    back_high, ahead_low = send(high, outer(1)), send(low, outer(-1))
    tables = list_products(ok, cid, nbr, deg)
    back_low, ahead_high, tables = tie((back_low, ahead_high, tables))
    far_low, far_high = send(back_low, outer(1)), send(ahead_high, outer(-1))
    theirs = [swap(jnp.concatenate([low, high], axis=0)), swap(back_low), swap(ahead_high)]
    late = tie([back_high, ahead_low, far_low, far_high])
    theirs += [swap(value) for value in late]
    mine = [low, high, back_low, ahead_high, *late]
    return ok, [*blocks, *tables], [*mine, *theirs]


def per_device(density, pattern):
    smem = pl.BlockSpec(memory_space=pltpu.SMEM)
    vmem = pl.BlockSpec(memory_space=pltpu.VMEM)

    square = jax.ShapeDtypeStruct((NB, NB), F32)
    packed, *owners = pl.pallas_call(
        pack_kernel,
        out_shape=(jax.ShapeDtypeStruct((CAP * BS, BS), F32), square, square, square),
        in_specs=[vmem, vmem],
        out_specs=[vmem] * 4,
        name="pack_blocks",
    )(pattern, density)

    rows = lax.axis_size("row")
    pieces = packed.reshape(rows, SHARD, BS)
    shard = jnp.sum(lax.all_to_all(pieces, "row", split_axis=0, concat_axis=0, tiled=True), axis=0)
    ok, tables, gathered = gather_pieces(shard, pattern, owners)

    def sparse(density, pattern, tables, gathered):
        block = lambda n, t: pltpu.VMEM((n, BS, BS), t)
        return pl.pallas_call(
            compute_kernel,
            out_shape=jax.ShapeDtypeStruct(density.shape, F32),
            in_specs=[smem] * len(tables) + [pl.BlockSpec(memory_space=pl.ANY)] * len(gathered),
            out_specs=vmem,
            scratch_shapes=[
                pltpu.VMEM((2 * RAW_HALF, BS), F32),
                block(ZERO + 2, BF16), block(ZERO + 2, BF16),
                block(S_CAP + 1, F32), block(S_CAP + 1, BF16), block(S_CAP + 1, BF16),
                block(D_CAP + 1, F32), block(D_CAP + 1, BF16), block(D_CAP + 1, BF16),
                block(E_CAP + 1, F32), block(E_CAP + 1, BF16), block(E_CAP + 1, BF16),
                block(NB // 8 + 1, F32),
                pltpu.SemaphoreType.DMA((len(gathered),)),
            ],
            compiler_params=pltpu.CompilerParams(vmem_limit_bytes=60 * 2**20),
            name="purify_column",
        )(*tables, *gathered)

    def dense(density, pattern, tables, gathered):
        return dense_plan(density, pattern)

    return lax.cond(ok[0] != 0, sparse, dense, density, pattern, tables, gathered)


def solution(mesh):
    return jax.shard_map(
        per_device,
        mesh=mesh,
        in_specs=(P("row", ("col", "layer")), P()),
        out_specs=P("row", ("col", "layer")),
        check_vma=False,
    )
```

```python
import jax
import jax.numpy as jnp
from jax import lax
from jax.experimental import pallas as pl
from jax.experimental.pallas import tpu as pltpu
from jax.sharding import PartitionSpec as P

BS = 128
ITERS = 2
NB = 32
CAP = 4
NS = NB * CAP
ROUNDS = 8
ZERO = 2 * NS
S_CAP = 104
D_CAP = 80
E_CAP = NB
PAIRS = 256
UNROLL = 4
MANY = 4
LIST = 2 * PAIRS + 2 * UNROLL + 8
NZ, NC = 8, 2
NX, NY = 4, 4
SHARD = CAP * BS // 8
UNIT = NZ * SHARD
PANEL = 4 * UNIT
RAW_HALF = 4 * PANEL
WIDE = 40
WORD = 4096
F32 = jnp.float32
BF16 = jnp.bfloat16


def panel_cols(tile, layers):
    row_count, shard_cols = tile.shape
    gathered = lax.all_gather(tile, "row", axis=0, tiled=True)
    pieces = gathered.reshape(
        gathered.shape[0] // (shard_cols * layers), layers, shard_cols, shard_cols
    )
    arranged = lax.all_to_all(pieces, "layer", split_axis=1, concat_axis=3, tiled=True)
    return arranged.reshape(-1, layers * shard_cols)


def multiply(left_tile, right_panel):
    partial_sum = jnp.dot(
        lax.all_gather(left_tile, "col", axis=1, tiled=True),
        right_panel,
        precision=lax.Precision.HIGHEST,
        preferred_element_type=jnp.float32,
    )
    return lax.psum_scatter(partial_sum, "layer", scatter_dimension=1, tiled=True)


def dense_plan(density, pattern):
    row_index = lax.axis_index("row")
    col_index = lax.axis_index("col")
    layer_index = lax.axis_index("layer")
    layers = lax.axis_size("layer")
    row_count, shard_cols = density.shape
    blocks = pattern.shape[0]
    block_line = jnp.arange(blocks, dtype=jnp.int32)
    row_ids = (row_index * row_count + jnp.arange(row_count, dtype=jnp.int32)) // BS
    col_ids = (
        (col_index * layers + layer_index) * shard_cols + jnp.arange(shard_cols, dtype=jnp.int32)
    ) // BS
    pick_rows = (row_ids[:, None] == block_line[None, :]).astype(jnp.float32)
    pick_cols = (col_ids[:, None] == block_line[None, :]).astype(jnp.float32)
    occupied = pattern.astype(jnp.float32)
    in_pattern = jnp.dot(
        jnp.dot(pick_rows, occupied, precision=lax.Precision.HIGHEST),
        pick_cols.T,
        precision=lax.Precision.HIGHEST,
    )
    current = in_pattern * density
    for iteration in range(ITERS):
        current_panel = panel_cols(current, layers)
        squared = in_pattern * multiply(current, current_panel)
        cube_term = in_pattern * multiply(current, panel_cols(squared, layers))
        current = 3.0 * squared - 2.0 * cube_term
    return current


def here():
    row = lax.axis_index("row").astype(jnp.int32)
    column = lax.axis_index("col") * lax.axis_size("layer") + lax.axis_index("layer")
    return row, column.astype(jnp.int32)


def ring_place(source, at):
    back = (at - source) & 3
    return jnp.where(back == 3, 2, jnp.where(back == 2, 3, back))


def raw_row(column, p, j, r):
    px = ring_place((column & 1) * 2 + (p >> 2), (j & 1) * 2 + (r >> 2))
    py = ring_place(p & 3, r & 3)
    core = (column >> 1) & 1
    near, far = jnp.where(core == 0, px, py), jnp.where(core == 0, py, px)
    other = jnp.where(((j >> 1) & 1) == core, 0, 1)
    high = near >> 1
    ring = 2 + jnp.where(far == 1, 2 * high, 3 - 2 * high)
    group = jnp.where(far == 0, high, jnp.where(far == 3, 6 + high, ring))
    return other * RAW_HALF + group * (PANEL // 2) + (near & 1) * UNIT + (column >> 2) * SHARD


def pack_kernel(pat_ref, tile_ref, packed_ref, own_ref, own_t_ref, rank_ref):
    r, j = here()
    K = (pat_ref[...] != 0).astype(F32)
    ii = lax.broadcasted_iota(jnp.int32, (NB, NB), 0)
    jj = lax.broadcasted_iota(jnp.int32, (NB, NB), 1)
    diag = (ii == jj).astype(F32)
    left = K * (1.0 - diag)
    own = diag
    own_t = diag
    after = (ii > jj).astype(F32)
    before = (ii < jj).astype(F32)
    for _ in range(ROUNDS):
        fc = (jnp.sum(left, axis=0, keepdims=True) <= CAP - 1).astype(F32)
        fr = (jnp.sum(left, axis=1, keepdims=True) <= CAP - 1).astype(F32)
        own = own + left * fc * ((1.0 - fr) + fr * after)
        own_t = own_t + left * fr * ((1.0 - fc) + fc * before)
        left = left * (1.0 - fc) * (1.0 - fr)
    own = own + left * after
    own_t = own_t + left * before
    rank = jnp.dot(after, own, preferred_element_type=F32)
    own_ref[...] = own
    own_t_ref[...] = own_t
    rank_ref[...] = rank

    for s in range(CAP):
        total = jnp.zeros((BS, BS), F32)
        for a in range(tile_ref.shape[0] // BS):
            at = (ii == r * (tile_ref.shape[0] // BS) + a) & (jj == j)
            pick = at & (own > 0) & (rank == s)
            w = jnp.sum(jnp.where(pick, 1.0, 0.0), axis=(0, 1), keepdims=True)
            total = total + w * tile_ref[a * BS : (a + 1) * BS, :]
        packed_ref[s * BS : (s + 1) * BS, :] = total


def plan_kernel(
    pat_ref, own_ref, own_t_ref, rank_ref,
    cid_ref, nbr_ref, deg_ref, needed_ref, count_ref, rows_ref, ok_ref,
):
    r, j = here()
    K = (pat_ref[...] != 0).astype(F32)
    ii = lax.broadcasted_iota(jnp.int32, (NB, NB), 0)
    jj = lax.broadcasted_iota(jnp.int32, (NB, NB), 1)
    before = (ii < jj).astype(F32)
    own = own_ref[...]
    own_t = own_t_ref[...]
    rank = rank_ref[...]
    rank_t = jnp.dot(own_t, before, preferred_element_type=F32)
    slot = jj * CAP + rank.astype(jnp.int32)
    slot_t = ii * CAP + rank_t.astype(jnp.int32)
    cid = jnp.where(own > 0, slot, jnp.where(own_t > 0, NS + slot_t, ZERO))
    cid_ref[...] = jnp.full(cid_ref.shape, ZERO, jnp.int32)
    cid_ref[:NB, :] = cid
    column = jnp.where(own > 0, jj, ii)
    turn = jnp.where(own > 0, rank, rank_t).astype(jnp.int32)
    first, second = [raw_row(column, 2 * turn + n, j, r) // SHARD for n in range(2)]
    rows_ref[...] = first + second * WORD

    common = jnp.dot(K, K, preferred_element_type=F32)
    pairs = K * jnp.floor((common + 1.0) * 0.5)
    s_blocks = jnp.max(jnp.sum(common, axis=1))
    d_blocks = jnp.max(jnp.sum(common * K, axis=1))
    spread = jnp.dot(K, pairs, preferred_element_type=F32)
    s_pairs = jnp.max(jnp.sum(spread, axis=1))
    fits = (
        (jnp.max(jnp.sum(own, axis=0)) <= CAP)
        & (s_blocks <= S_CAP)
        & (d_blocks <= D_CAP)
        & (s_pairs <= PAIRS)
    )
    ok_ref[0] = fits.astype(jnp.int32)

    kj = jnp.sum(jnp.where(jj == j, K, 0.0), axis=1, keepdims=True)
    near = lax.dot_general(K * kj, K, (((0,), (0,)), ((), ())), preferred_element_type=F32)
    wanted = jnp.where((near > 0) & (K > 0), 1.0, 0.0)
    wide = lax.broadcasted_iota(jnp.int32, (NB, WIDE), 1)
    for listed, n_ref, entries in (
        (K, deg_ref, ((jj + cid * WORD, NB + ZERO * WORD, nbr_ref),)),
        (wanted, count_ref, ((jj, NB, needed_ref),)),
    ):
        place = jnp.dot(listed, before, preferred_element_type=F32).astype(jnp.int32)
        place = jnp.where(listed > 0, place, -1)
        size = jnp.sum(listed, axis=1, keepdims=True).astype(jnp.int32)
        for value, empty, list_ref in entries:
            out = jnp.full((NB, WIDE), empty, jnp.int32)
            for d in range(NB):
                entry = jnp.sum(jnp.where(place == d, value, 0), axis=1, keepdims=True)
                out = jnp.where((wide == d) & (size > d), entry, out)
            list_ref[...] = out
        n_ref[...] = jnp.broadcast_to(size, (NB, NB))


H_S, H_T, H_E, H_F, H_SB, H_DB, H_EB = range(7)


def block_kernel(ok_ref, cid, needed, count_in, rows_in, head_ref, pn_ref, pt_ref, an_ref, at_ref):
    ok = ok_ref[0]

    def lines(i, carry):
        def entry(d, c):
            pn, pt = c
            k = needed[i, d]
            held = cid[i, k]
            row = rows_in[i, k]
            flipped = (held >= NS).astype(jnp.int32)
            pn_ref[pn] = held
            pt_ref[pt] = held
            an_ref[pn] = row
            at_ref[pt] = row
            return pn + (1 - flipped), pt + flipped

        return lax.fori_loop(0, count_in[i, 0] * ok, entry, carry)

    pn, pt = lax.fori_loop(0, NB, lines, (0, 0))
    for names, rows, n in ((pn_ref, an_ref, pn), (pt_ref, at_ref, pt)):
        for u in range(MANY - 1):
            names[n + u] = ZERO + 1
            rows[n + u] = 0
    head_ref[0] = pn
    head_ref[1] = pt


def table_kernel(
    ok_ref, cid, nbr, deg_in,
    head_ref, sl, sr, tt, el, er, fl, fr, ds_ref, fin_ref,
    did, eid,
):
    r, j = here()
    ok = ok_ref[0]
    nj = deg_in[j, 0] * ok

    def row(a, carry):
        m = nbr[j, a] & (WORD - 1)
        nm = deg_in[m, 0]
        base = carry[1] * WORD

        def output(b, c):
            pos, count, dcount, tcount = c
            k = nbr[m, b] & (WORD - 1)
            out = count * WORD

            def four(g, p):
                at = g * 4
                words = [nbr[m, at + u] for u in range(4)]
                rs = [cid[w & (WORD - 1), k] for w in words]
                for u in range(4):
                    sl[p] = (words[u] >> 12) + (base + (at + u) * WORD)
                    sr[p] = rs[u] + out
                    p = p + (rs[u] != ZERO).astype(jnp.int32)
                return p

            p = lax.fori_loop(0, (nm + 3) >> 2, four, pos)
            sl[p] = ZERO + S_CAP * WORD
            sr[p] = ZERO + out
            p = p + (p & 1)

            def reuse(pair, t):
                tt[t] = pair + dcount * WORD
                return t + 1

            inside = (cid[k, j] != ZERO).astype(jnp.int32)
            first = pos >> 1
            tcount = lax.fori_loop(first, first + inside * ((p >> 1) - first), reuse, tcount)
            did[m, k] = dcount
            ds_ref[dcount] = count
            return p, count + 1, dcount + inside, tcount

        return lax.fori_loop(0, nm, output, carry)

    pos, count, dcount, tcount = lax.fori_loop(0, nj, row, (0, 0, 0, 0))
    for t in range(2 * UNROLL):
        sl[pos + t] = ZERO + S_CAP * WORD
        sr[pos + t] = ZERO + S_CAP * WORD
    for t in range(UNROLL):
        tt[tcount + t] = (pos >> 1) + D_CAP * WORD
    for u in range(MANY - 1):
        ds_ref[dcount + u] = 0
    head_ref[H_S] = ((pos >> 1) + UNROLL - 1) // UNROLL
    head_ref[H_T] = (tcount + UNROLL - 1) // UNROLL
    head_ref[H_SB] = count
    head_ref[H_DB] = dcount

    def finish(refs, pos, lz, dummy):
        L, R = refs
        for t in range(2 * UNROLL):
            L[pos + t] = lz
            R[pos + t] = D_CAP + dummy * WORD
        return ((pos >> 1) + UNROLL - 1) // UNROLL

    def gather(refs, pos, k, left, out, lz):
        L, R = refs

        def entry(c, p):
            m = nbr[j, c] & (WORD - 1)
            L[p] = left(m)
            R[p] = did[m, k] + out * WORD
            return p + (cid[m, k] != ZERO).astype(jnp.int32)

        p = lax.fori_loop(0, nj, entry, pos)
        L[p] = lz
        R[p] = D_CAP + out * WORD
        return p + (p & 1)

    def e_out(b, pos):
        k = nbr[j, b] & (WORD - 1)
        eid[k] = b
        return gather((el, er), pos, k, lambda m: did[j, m], b, D_CAP)

    pos = lax.fori_loop(0, nj, e_out, 0)
    head_ref[H_E] = finish((el, er), pos, D_CAP, E_CAP)
    head_ref[H_EB] = nj

    per = NB // 8

    def f_out(a, pos):
        i = r * per + a

        def stored(pos):
            fin_ref[a] = eid[i]
            return gather((fl, fr), pos, i, lambda k: eid[k], a, E_CAP)

        def absent(pos):
            fin_ref[a] = -1
            return pos

        return lax.cond((cid[i, j] != ZERO) & (ok != 0), stored, absent, pos)

    pos = lax.fori_loop(0, per, f_out, 0)
    head_ref[H_F] = finish((fl, fr), pos, E_CAP, per)


def split(x):
    hi = x.astype(BF16)
    return hi, (x - hi.astype(F32)).astype(BF16)


def compute_kernel(
    blocks_ref, pn_ref, pt_ref, an_ref, at_ref, head_ref, sl, sr, tt, el, er, fl, fr, ds_ref, fin_ref,
    *rest,
):
    pieces, rest = rest[:-15], rest[-15:]
    out_ref, raw, ch, cl, sa, sh, slo, da, dh, dl, ea, eh, elo, fa, sem = rest
    copies = []
    row = 0
    for n, piece in enumerate(pieces):
        height = piece.shape[0]
        copies.append(pltpu.make_async_copy(piece, raw.at[pl.ds(row, height)], sem.at[n]))
        row += height
    for c in copies:
        c.start()
    zero = jnp.zeros((BS, BS), BF16)
    for hi, lo, at in ((ch, cl, ZERO), (sh, slo, S_CAP), (dh, dl, D_CAP), (eh, elo, E_CAP)):
        hi[at] = zero
        lo[at] = zero

    def clear(ref, n):
        @pl.loop(0, n)
        def _(t):
            ref[t] = jnp.zeros((BS, BS), F32)

    clear(sa, head_ref[H_SB])
    clear(da, head_ref[H_DB])
    clear(ea, head_ref[H_EB])
    clear(fa, fa.shape[0])
    for c in copies:
        c.wait()

    def prepare(n, names, rows, turn):
        @pl.loop(0, (n + MANY - 1) // MANY)
        def _(t):
            ids = [names[MANY * t + u] for u in range(MANY)]
            xs = []
            for u in range(MANY):
                word = rows[MANY * t + u]
                parts = [
                    raw[pl.ds(pl.multiple_of(at * SHARD, SHARD), SHARD), :] for at in (word & (WORD - 1), word >> 12)
                ]
                xs.append(split(turn(jnp.concatenate(parts, axis=0))))
            for a, (hi, lo) in zip(ids, xs):
                ch[a] = hi
                cl[a] = lo

    prepare(blocks_ref[0], pn_ref, an_ref, lambda v: v)
    prepare(blocks_ref[1], pt_ref, at_ref, lambda v: v.T)

    def phase(n, task, left, right, acc):
        lh, ll = left
        rh, rl = right

        @pl.loop(0, n)
        def _(t):
            sums = []
            outs = []
            for u in range(UNROLL):
                a0, a1, b0, b1, out = task(t * UNROLL + u)
                lhs = jnp.concatenate(
                    [
                        jnp.concatenate([lh[a0], lh[a1]], axis=1),
                        jnp.concatenate([ll[a0], ll[a1]], axis=1),
                    ],
                    axis=0,
                )
                rhs = jnp.concatenate(
                    [
                        jnp.concatenate([rh[b0], rl[b0]], axis=1),
                        jnp.concatenate([rh[b1], rl[b1]], axis=1),
                    ],
                    axis=0,
                )
                both = jnp.dot(lhs, rhs, preferred_element_type=F32)
                sums.append(both[:BS, :BS] + (both[:BS, BS:] + both[BS:, :BS]))
                outs.append(out)
            for u in range(UNROLL):
                acc[outs[u]] = acc[outs[u]] + sums[u]

    def plain(L, R):
        def task(t):
            r0 = R[2 * t]
            low = lambda w: w & (WORD - 1)
            return low(L[2 * t]), low(L[2 * t + 1]), low(r0), low(R[2 * t + 1]), r0 >> 12

        return task

    def cube(t):
        word = tt[t]
        at = 2 * (word & (WORD - 1))
        return sl[at] >> 12, sl[at + 1] >> 12, sr[at] & (WORD - 1), sr[at + 1] & (WORD - 1), word >> 12

    phase(head_ref[H_S], plain(sl, sr), (ch, cl), (ch, cl), sa)

    @pl.loop(0, (head_ref[H_SB] + MANY - 1) // MANY)
    def _(t):
        done = [split(sa[MANY * t + u]) for u in range(MANY)]
        for u in range(MANY):
            sh[MANY * t + u], slo[MANY * t + u] = done[u]

    phase(head_ref[H_T], cube, (sh, slo), (ch, cl), da)

    @pl.loop(0, (head_ref[H_DB] + MANY - 1) // MANY)
    def _(t):
        done = [split(3.0 * sa[ds_ref[MANY * t + u]] - 2.0 * da[MANY * t + u]) for u in range(MANY)]
        for u in range(MANY):
            dh[MANY * t + u], dl[MANY * t + u] = done[u]

    phase(head_ref[H_E], plain(el, er), (dh, dl), (dh, dl), ea)

    @pl.loop(0, head_ref[H_EB])
    def _(t):
        eh[t], elo[t] = split(ea[t])

    phase(head_ref[H_F], plain(fl, fr), (eh, elo), (dh, dl), fa)
    for a in range(out_ref.shape[0] // BS):
        at = fin_ref[a]
        value = 3.0 * ea[jnp.maximum(at, 0)] - 2.0 * fa[a]
        out_ref[a * BS : (a + 1) * BS, :] = jnp.where(at >= 0, value.T, 0.0)


def linear(x, y, z, core):
    return (((x % 2) * NY + y) * (NZ * NC) + z * NC + core) * 2 + x // 2


def send(value, step):
    pairs = [
        (linear(x, y, z, core), linear(*step(x, y, z, core)))
        for x in range(NX)
        for y in range(NY)
        for z in range(NZ)
        for core in range(NC)
    ]
    return lax.ppermute(value, ("row", "col", "layer"), pairs)


def along_z(d):
    return lambda x, y, z, core: (x, y, (z + d) % NZ, core)


def inner(d):
    return lambda x, y, z, core: ((x + d) % NX, y, z, core) if core == 0 else (x, (y + d) % NY, z, core)


def outer(d):
    return lambda x, y, z, core: (x, (y + d) % NY, z, core) if core == 0 else ((x + d) % NX, y, z, core)


def other_core(x, y, z, core):
    return x, y, z, 1 - core


def list_blocks(ok, *plan):
    smem = pl.BlockSpec(memory_space=pltpu.SMEM)
    i32 = lambda *shape: jax.ShapeDtypeStruct(shape, jnp.int32)
    return pl.pallas_call(
        block_kernel,
        out_shape=[i32(8), *[i32(2 * NS + 8)] * 4],
        in_specs=[smem] * 5,
        out_specs=[smem] * 5,
        cost_estimate=pl.CostEstimate(flops=0, bytes_accessed=6_000_000, transcendentals=0),
        name="list_blocks",
    )(ok, *plan)


def list_products(ok, *plan):
    smem = pl.BlockSpec(memory_space=pltpu.SMEM)
    i32 = lambda *shape: jax.ShapeDtypeStruct(shape, jnp.int32)
    return pl.pallas_call(
        table_kernel,
        out_shape=[i32(16), *[i32(LIST)] * 7, i32(D_CAP + MANY), i32(8)],
        in_specs=[smem] * 4,
        out_specs=[smem] * 10,
        scratch_shapes=[
            pltpu.SMEM((NB, NB), jnp.int32),
            pltpu.SMEM((NB,), jnp.int32),
        ],
        cost_estimate=pl.CostEstimate(flops=0, bytes_accessed=20_000_000, transcendentals=0),
        name="list_products",
    )(ok, *plan)


def plan_products(pattern, *owners):
    smem = pl.BlockSpec(memory_space=pltpu.SMEM)
    vmem = pl.BlockSpec(memory_space=pltpu.VMEM)
    i32 = lambda *shape: jax.ShapeDtypeStruct(shape, jnp.int32)
    return pl.pallas_call(
        plan_kernel,
        out_shape=(
            i32(WIDE, NB), i32(NB, WIDE), i32(NB, NB), i32(NB, WIDE), i32(NB, NB),
            i32(NB, NB),
            i32(1),
        ),
        in_specs=[vmem] * 4,
        out_specs=(*[vmem] * 6, smem),
        cost_estimate=pl.CostEstimate(flops=0, bytes_accessed=10_000_000, transcendentals=0),
        name="plan_products",
    )(pattern, *owners)


def to_chips_along_z(shard):
    lines = [[z * NC + c for z in range(NZ)] for c in range(NC)]
    copies = jnp.broadcast_to(shard, (NZ, SHARD, BS))
    return lax.all_to_all(
        copies, "col", split_axis=0, concat_axis=0, tiled=True, axis_index_groups=lines
    ).reshape(UNIT, BS)


def gather_pieces(shard, pattern, owners):
    tie = lax.optimization_barrier
    swap = lambda value: send(value, other_core)
    own = to_chips_along_z(shard)
    own, owners = tie((own, owners))
    line = [own] + [send(own, inner(d)) for d in (1, -1, 2)]
    cid, nbr, deg, needed, count, rows, ok = plan_products(pattern, *owners)
    blocks = list_blocks(ok, cid, needed, count, rows)
    line, blocks = tie((line, blocks))

    low, high = jnp.concatenate(line[:2], axis=0), jnp.concatenate(line[2:], axis=0)
    low, high, cid, nbr, deg = tie((low, high, cid, nbr, deg))
    back_low, ahead_high = send(low, outer(1)), send(high, outer(-1))
    back_high, ahead_low = send(high, outer(1)), send(low, outer(-1))
    tables = list_products(ok, cid, nbr, deg)
    back_low, ahead_high, tables = tie((back_low, ahead_high, tables))
    far_low, far_high = send(back_low, outer(1)), send(ahead_high, outer(-1))
    panel = jnp.concatenate([low, high], axis=0)
    panel, back_low, ahead_high, back_high, ahead_low = tie((panel, back_low, ahead_high, back_high, ahead_low))
    theirs = [swap(value) for value in (panel, back_low, ahead_high, back_high, ahead_low, far_low, far_high)]
    late = [back_high, ahead_low, far_low, far_high]
    mine = [low, high, back_low, ahead_high, *late]
    return ok, [*blocks, *tables], [*mine, *theirs]


def per_device(density, pattern):
    smem = pl.BlockSpec(memory_space=pltpu.SMEM)
    vmem = pl.BlockSpec(memory_space=pltpu.VMEM)

    square = jax.ShapeDtypeStruct((NB, NB), F32)
    packed, *owners = pl.pallas_call(
        pack_kernel,
        out_shape=(jax.ShapeDtypeStruct((CAP * BS, BS), F32), square, square, square),
        in_specs=[vmem, vmem],
        out_specs=[vmem] * 4,
        name="pack_blocks",
    )(pattern, density)

    rows = lax.axis_size("row")
    pieces = packed.reshape(rows, SHARD, BS)
    shard = jnp.sum(lax.all_to_all(pieces, "row", split_axis=0, concat_axis=0, tiled=True), axis=0)
    ok, tables, gathered = gather_pieces(shard, pattern, owners)

    def sparse(density, pattern, tables, gathered):
        block = lambda n, t: pltpu.VMEM((n, BS, BS), t)
        return pl.pallas_call(
            compute_kernel,
            out_shape=jax.ShapeDtypeStruct(density.shape, F32),
            in_specs=[smem] * len(tables) + [pl.BlockSpec(memory_space=pl.ANY)] * len(gathered),
            out_specs=vmem,
            scratch_shapes=[
                pltpu.VMEM((2 * RAW_HALF, BS), F32),
                block(ZERO + 2, BF16), block(ZERO + 2, BF16),
                block(S_CAP + 1, F32), block(S_CAP + 1, BF16), block(S_CAP + 1, BF16),
                block(D_CAP + 1, F32), block(D_CAP + 1, BF16), block(D_CAP + 1, BF16),
                block(E_CAP + 1, F32), block(E_CAP + 1, BF16), block(E_CAP + 1, BF16),
                block(NB // 8 + 1, F32),
                pltpu.SemaphoreType.DMA((len(gathered),)),
            ],
            compiler_params=pltpu.CompilerParams(vmem_limit_bytes=60 * 2**20),
            name="purify_column",
        )(*tables, *gathered)

    def dense(density, pattern, tables, gathered):
        return dense_plan(density, pattern)

    return lax.cond(ok[0] != 0, sparse, dense, density, pattern, tables, gathered)


def solution(mesh):
    return jax.shard_map(
        per_device,
        mesh=mesh,
        in_specs=(P("row", ("col", "layer")), P()),
        out_specs=P("row", ("col", "layer")),
        check_vma=False,
    )
```

```python
import jax
import jax.numpy as jnp
from jax import lax
from jax.experimental import pallas as pl
from jax.experimental.pallas import tpu as pltpu
from jax.sharding import PartitionSpec as P

BS = 128
ITERS = 2
NB = 32
CAP = 4
NS = NB * CAP
ROUNDS = 5
REPAIRS = 24
ZERO = 2 * NS
S_CAP = 104
D_CAP = 80
E_CAP = NB
PAIRS = 256
UNROLL = 8
FEW = 4
MANY = 4
LIST = 2 * PAIRS + 2 * UNROLL + 8
NZ, NC = 8, 2
NX, NY = 4, 4
SHARD = CAP * BS // 8
UNIT = NZ * SHARD
PANEL = 4 * UNIT
RAW_HALF = 4 * PANEL
WIDE = 40
WORD = 4096
HALF_WORD = 256
OK = WIDE - 1
LANES = 128
NEAR = WIDE
NEED = 2 * WIDE
SIZE = WIDE - 1
F32 = jnp.float32
BF16 = jnp.bfloat16


def panel_cols(tile, layers):
    row_count, shard_cols = tile.shape
    gathered = lax.all_gather(tile, "row", axis=0, tiled=True)
    pieces = gathered.reshape(
        gathered.shape[0] // (shard_cols * layers), layers, shard_cols, shard_cols
    )
    arranged = lax.all_to_all(pieces, "layer", split_axis=1, concat_axis=3, tiled=True)
    return arranged.reshape(-1, layers * shard_cols)


def multiply(left_tile, right_panel):
    partial_sum = jnp.dot(
        lax.all_gather(left_tile, "col", axis=1, tiled=True),
        right_panel,
        precision=lax.Precision.HIGHEST,
        preferred_element_type=jnp.float32,
    )
    return lax.psum_scatter(partial_sum, "layer", scatter_dimension=1, tiled=True)


def dense_plan(density, pattern):
    row_index = lax.axis_index("row")
    col_index = lax.axis_index("col")
    layer_index = lax.axis_index("layer")
    layers = lax.axis_size("layer")
    row_count, shard_cols = density.shape
    blocks = pattern.shape[0]
    block_line = jnp.arange(blocks, dtype=jnp.int32)
    row_ids = (row_index * row_count + jnp.arange(row_count, dtype=jnp.int32)) // BS
    col_ids = (
        (col_index * layers + layer_index) * shard_cols + jnp.arange(shard_cols, dtype=jnp.int32)
    ) // BS
    pick_rows = (row_ids[:, None] == block_line[None, :]).astype(jnp.float32)
    pick_cols = (col_ids[:, None] == block_line[None, :]).astype(jnp.float32)
    occupied = pattern.astype(jnp.float32)
    in_pattern = jnp.dot(
        jnp.dot(pick_rows, occupied, precision=lax.Precision.HIGHEST),
        pick_cols.T,
        precision=lax.Precision.HIGHEST,
    )
    current = in_pattern * density
    for iteration in range(ITERS):
        current_panel = panel_cols(current, layers)
        squared = in_pattern * multiply(current, current_panel)
        cube_term = in_pattern * multiply(current, panel_cols(squared, layers))
        current = 3.0 * squared - 2.0 * cube_term
    return current


def here():
    row = lax.axis_index("row").astype(jnp.int32)
    column = lax.axis_index("col") * lax.axis_size("layer") + lax.axis_index("layer")
    return row, column.astype(jnp.int32)


def ring_place(source, at):
    back = (at - source) & 3
    return jnp.where(back == 3, 2, jnp.where(back == 2, 3, back))


def raw_row(column, p, j, r):
    px = ring_place((column & 1) * 2 + (p >> 2), (j & 1) * 2 + (r >> 2))
    py = ring_place(p & 3, r & 3)
    core = (column >> 1) & 1
    near, far = jnp.where(core == 0, px, py), jnp.where(core == 0, py, px)
    other = jnp.where(((j >> 1) & 1) == core, 0, 1)
    high = near >> 1
    ring = 2 + jnp.where(far == 1, 2 * high, 3 - 2 * high)
    group = jnp.where(far == 0, high, jnp.where(far == 3, 6 + high, ring))
    return other * RAW_HALF + group * (PANEL // 2) + (near & 1) * UNIT + (column >> 2) * SHARD


def pack_kernel(pat_ref, tile_ref, packed_ref, own_ref, own_t_ref, rank_ref):
    r, j = here()
    K = (pat_ref[...] != 0).astype(F32)
    ii = lax.broadcasted_iota(jnp.int32, (NB, NB), 0)
    jj = lax.broadcasted_iota(jnp.int32, (NB, NB), 1)
    diag = (ii == jj).astype(F32)
    left = K * (1.0 - diag)
    own = diag
    own_t = diag
    after = (ii > jj).astype(F32)
    before = (ii < jj).astype(F32)
    for _ in range(ROUNDS):
        fc = (jnp.sum(left, axis=0, keepdims=True) <= CAP - 1).astype(F32)
        fr = (jnp.sum(left, axis=1, keepdims=True) <= CAP - 1).astype(F32)
        own = own + left * fc * ((1.0 - fr) + fr * after)
        own_t = own_t + left * fr * ((1.0 - fc) + fc * before)
        left = left * (1.0 - fc) * (1.0 - fr)
    own = own + left * after
    own_t = own_t + left * before

    number = ii * NB + jj
    number_t = jj * NB + ii

    def move(_, held):
        own, own_t = held
        load_row = jnp.sum(own, axis=0, keepdims=True)
        load_col = jnp.sum(own_t, axis=1, keepdims=True)
        source = own * (1.0 - diag) * (load_row > CAP).astype(F32)
        room = source * (load_col < CAP).astype(F32)
        onward = jnp.max(own_t * (1.0 - diag) * (load_row < CAP).astype(F32), axis=1, keepdims=True)
        through = source * onward * (load_col == CAP).astype(F32)
        none = jnp.max(room, axis=(0, 1), keepdims=True) == 0.0
        use = jnp.where(none, through, room)
        first = jnp.min(jnp.where(use > 0, number, NB * NB), axis=(0, 1), keepdims=True)
        flip = (number == first).astype(F32)
        flip_t = (number_t == first).astype(F32)
        return own - flip + flip_t, own_t - flip_t + flip

    crowded = jnp.max(jnp.sum(own, axis=0)) > CAP
    own, own_t = lax.fori_loop(0, jnp.where(crowded, REPAIRS, 0), move, (own, own_t))
    rank = jnp.dot(after, own, preferred_element_type=F32)
    own_ref[...] = own
    own_t_ref[...] = own_t
    rank_ref[...] = rank

    for s in range(CAP):
        total = jnp.zeros((BS, BS), F32)
        for a in range(tile_ref.shape[0] // BS):
            at = (ii == r * (tile_ref.shape[0] // BS) + a) & (jj == j)
            pick = at & (own > 0) & (rank == s)
            w = jnp.sum(jnp.where(pick, 1.0, 0.0), axis=(0, 1), keepdims=True)
            total = total + w * tile_ref[a * BS : (a + 1) * BS, :]
        packed_ref[s * BS : (s + 1) * BS, :] = total


def plan_kernel(
    pat_ref, own_ref, own_t_ref, rank_ref,
    plan_ref, ok_ref,
):
    r, j = here()
    K = (pat_ref[...] != 0).astype(F32)
    ii = lax.broadcasted_iota(jnp.int32, (NB, NB), 0)
    jj = lax.broadcasted_iota(jnp.int32, (NB, NB), 1)
    before = (ii < jj).astype(F32)
    own = own_ref[...]
    own_t = own_t_ref[...]
    rank = rank_ref[...]
    rank_t = jnp.dot(own_t, before, preferred_element_type=F32)
    slot = jj * CAP + rank.astype(jnp.int32)
    slot_t = ii * CAP + rank_t.astype(jnp.int32)
    cid = jnp.where(own > 0, slot, jnp.where(own_t > 0, NS + slot_t, ZERO))
    column = jnp.where(own > 0, jj, ii)
    turn = jnp.where(own > 0, rank, rank_t).astype(jnp.int32)
    first, second = [raw_row(column, 2 * turn + n, j, r) // SHARD for n in range(2)]
    blocks = cid + (first + second * HALF_WORD) * WORD

    common = jnp.dot(K, K, preferred_element_type=F32)
    pairs = K * jnp.floor((common + 1.0) * 0.5)
    s_blocks = jnp.max(jnp.sum(common, axis=1))
    d_blocks = jnp.max(jnp.sum(common * K, axis=1))
    spread = jnp.dot(K, pairs, preferred_element_type=F32)
    s_pairs = jnp.max(jnp.sum(spread, axis=1))
    fits = (
        (jnp.max(jnp.sum(own, axis=0)) <= CAP)
        & (s_blocks <= S_CAP)
        & (d_blocks <= D_CAP)
        & (s_pairs <= PAIRS)
    )
    ok_ref[0] = fits.astype(jnp.int32)
    last = lax.broadcasted_iota(jnp.int32, (WIDE - NB, LANES), 0) == OK - NB
    plan_ref[NB:WIDE, :] = jnp.where(last, fits.astype(jnp.int32), ZERO)

    kj = jnp.sum(jnp.where(jj == j, K, 0.0), axis=1, keepdims=True)
    near = lax.dot_general(K * kj, K, (((0,), (0,)), ((), ())), preferred_element_type=F32)
    wanted = jnp.where((near > 0) & (K > 0), 1.0, 0.0)
    wide = lax.broadcasted_iota(jnp.int32, (NB, LANES), 1)
    out = jnp.where(wide < NEED, NB + ZERO * WORD, NB)
    for listed, value, at in ((K, jj + cid * WORD, NEAR), (wanted, jj, NEED)):
        place = jnp.dot(listed, before, preferred_element_type=F32).astype(jnp.int32)
        place = jnp.where(listed > 0, place, -1)
        size = jnp.sum(listed, axis=1, keepdims=True).astype(jnp.int32)
        out = jnp.where(wide == at + SIZE, size, out)
        for d in range(NB):
            entry = jnp.sum(jnp.where(place == d, value, 0), axis=1, keepdims=True)
            out = jnp.where((wide == at + d) & (size > d), entry, out)
    plan_ref[:NB, :] = out
    plan_ref[:NB, :NB] = blocks


H_OUT, H_IN, H_AGAIN, H_E, H_F, H_SB, H_DB, H_EB, H_TURN = range(9)


class Part:
    def __init__(self, ref, start):
        self.ref, self.start = ref, start

    def __getitem__(self, at):
        return self.ref[self.start + at]

    def __setitem__(self, at, value):
        self.ref[self.start + at] = value


def parts_of(ref, sizes):
    return [Part(ref, sum(sizes[:n])) for n in range(len(sizes))]


BLOCK_SIZES = [8, *[2 * NS + 8] * 4]
SHORT = 160
NOTHING = PAIRS + 4
LIST_SIZES = [16, *[3 * LIST] * 2, *[SHORT] * 4, D_CAP + MANY, D_CAP + MANY, 8]


def block_kernel(plan, blocks_ref):
    head_ref, pn_ref, pt_ref, an_ref, at_ref = parts_of(blocks_ref, BLOCK_SIZES)
    ok = plan[OK, 0]

    def lines(i, carry):
        def entry(d, c):
            pn, pt = c
            word = plan[i, plan[i, NEED + d]]
            held = word & (WORD - 1)
            row = word >> 12
            flipped = (held >= NS).astype(jnp.int32)
            pn_ref[pn] = held
            pt_ref[pt] = held
            an_ref[pn] = row
            at_ref[pt] = row
            return pn + (1 - flipped), pt + flipped

        return lax.fori_loop(0, plan[i, NEED + SIZE] * ok, entry, carry)

    pn, pt = lax.fori_loop(0, NB, lines, (0, 0))
    for names, rows, n in ((pn_ref, an_ref, pn), (pt_ref, at_ref, pt)):
        for u in range(MANY - 1):
            names[n + u] = ZERO + 1
            rows[n + u] = 0
    head_ref[0] = pn
    head_ref[1] = pt


def table_kernel(plan, lists_ref, sid, did, eid):
    head_ref, sl, sr, el, er, fl, fr, ds_ref, turn_ref, fin_ref = parts_of(lists_ref, LIST_SIZES)
    r, j = here()
    ok = plan[OK, 0]

    def cid(q, k):
        return plan[q, k] & (WORD - 1)

    nj = plan[j, NEAR + SIZE] * ok

    def row(a, carry):
        m = plan[j, NEAR + a] & (WORD - 1)
        nm = plan[m, NEAR + SIZE]
        base = carry[3] * WORD

        def output(b, c):
            apart, inner_, again, count, dcount, turns = c
            k = plan[m, NEAR + b] & (WORD - 1)
            inside = cid(k, j) != ZERO
            turned = inside & (k < m)
            start = jnp.where(turned, again, jnp.where(inside, inner_, apart))
            outs = count * WORD
            outd = dcount * WORD

            def eight(g, p):
                at = g * 8
                words = [plan[m, NEAR + at + u] for u in range(8)]
                rs = [cid(w & (WORD - 1), k) for w in words]
                for u in range(8):
                    sl[p] = (words[u] >> 12) + (base + (at + u) * WORD)
                    sr[p] = rs[u] + jnp.where((p & 1) == 1, outd, outs)
                    p = p + (rs[u] != ZERO).astype(jnp.int32)
                return p

            p = lax.fori_loop(0, (nm + 7) >> 3, eight, start)
            sl[p] = ZERO + S_CAP * WORD
            sr[p] = ZERO + outd
            p = p + (p & 1)
            sid[m, k] = count
            did[m, k] = dcount
            ds_ref[dcount] = count
            turn_ref[turns] = jnp.where(turned, sid[k, m], 0) + outs
            return (
                jnp.where(inside, apart, p),
                jnp.where(inside & jnp.logical_not(turned), p, inner_),
                jnp.where(turned, p, again),
                count + 1,
                dcount + inside.astype(jnp.int32),
                turns + turned.astype(jnp.int32),
            )

        return lax.fori_loop(0, nm, output, carry)

    done = lax.fori_loop(0, nj, row, (0, LIST, 2 * LIST, 0, 0, 0))
    apart, inner_, again, count, dcount, turns = done
    for t, out in enumerate((S_CAP, D_CAP)):
        sl[2 * NOTHING + t] = ZERO + S_CAP * WORD
        sr[2 * NOTHING + t] = ZERO + out * WORD
    for u in range(MANY - 1):
        ds_ref[dcount + u] = 0
        turn_ref[turns + u] = S_CAP * WORD
    head_ref[H_OUT] = apart >> 1
    head_ref[H_IN] = (inner_ - LIST) >> 1
    head_ref[H_AGAIN] = (again - 2 * LIST) >> 1
    head_ref[H_TURN] = turns
    head_ref[H_SB] = count
    head_ref[H_DB] = dcount

    def finish(refs, pos, lz, dummy):
        L, R = refs
        for t in range(2 * FEW):
            L[pos + t] = lz
            R[pos + t] = D_CAP + dummy * WORD
        return ((pos >> 1) + FEW - 1) // FEW

    def gather(refs, pos, k, left, out, lz):
        L, R = refs

        def entry(c, p):
            m = plan[j, NEAR + c] & (WORD - 1)
            L[p] = left(m)
            R[p] = did[m, k] + out * WORD
            return p + (cid(m, k) != ZERO).astype(jnp.int32)

        p = lax.fori_loop(0, nj, entry, pos)
        L[p] = lz
        R[p] = D_CAP + out * WORD
        return p + (p & 1)

    def e_out(b, pos):
        k = plan[j, NEAR + b] & (WORD - 1)
        eid[k] = b
        return gather((el, er), pos, k, lambda m: did[j, m], b, D_CAP)

    pos = lax.fori_loop(0, nj, e_out, 0)
    head_ref[H_E] = finish((el, er), pos, D_CAP, E_CAP)
    head_ref[H_EB] = nj

    per = NB // 8

    def f_out(a, pos):
        i = r * per + a

        def stored(pos):
            fin_ref[a] = eid[i]
            return gather((fl, fr), pos, i, lambda k: eid[k], a, E_CAP)

        def absent(pos):
            fin_ref[a] = -1
            return pos

        return lax.cond((cid(i, j) != ZERO) & (ok != 0), stored, absent, pos)

    pos = lax.fori_loop(0, per, f_out, 0)
    head_ref[H_F] = finish((fl, fr), pos, E_CAP, per)


def split(x):
    hi = x.astype(BF16)
    return hi, (x - hi.astype(F32)).astype(BF16)


def compute_kernel(
    blocks_in, lists_in,
    *rest,
):
    blocks_ref, pn_ref, pt_ref, an_ref, at_ref = parts_of(blocks_in, BLOCK_SIZES)
    head_ref, sl, sr, el, er, fl, fr, ds_ref, turn_ref, fin_ref = parts_of(lists_in, LIST_SIZES)
    pieces, rest = rest[:-15], rest[-15:]
    out_ref, raw, ch, cl, sa, sh, slo, da, dh, dl, ea, eh, elo, fa, sem = rest
    copies = []
    row = 0
    for n, piece in enumerate(pieces):
        height = piece.shape[0]
        copies.append(pltpu.make_async_copy(piece, raw.at[pl.ds(row, height)], sem.at[n]))
        row += height
    for c in copies:
        c.start()
    zero = jnp.zeros((BS, BS), BF16)
    for hi, lo, at in ((ch, cl, ZERO), (sh, slo, S_CAP), (dh, dl, D_CAP), (eh, elo, E_CAP)):
        hi[at] = zero
        lo[at] = zero

    def clear(ref, n):
        @pl.loop(0, n)
        def _(t):
            ref[t] = jnp.zeros((BS, BS), F32)

    clear(sa, head_ref[H_SB])
    clear(da, head_ref[H_DB])
    clear(ea, head_ref[H_EB])
    clear(fa, fa.shape[0])
    for c in copies:
        c.wait()

    def prepare(n, names, rows, turn):
        @pl.loop(0, (n + MANY - 1) // MANY)
        def _(t):
            ids = [names[MANY * t + u] for u in range(MANY)]
            xs = []
            for u in range(MANY):
                word = rows[MANY * t + u]
                parts = [
                    raw[pl.ds(pl.multiple_of(at * SHARD, SHARD), SHARD), :] for at in (word & (HALF_WORD - 1), word >> 8)
                ]
                xs.append(split(turn(jnp.concatenate(parts, axis=0))))
            for a, (hi, lo) in zip(ids, xs):
                ch[a] = hi
                cl[a] = lo

    prepare(blocks_ref[0], pn_ref, an_ref, lambda v: v)
    prepare(blocks_ref[1], pt_ref, at_ref, lambda v: v.T)

    def phase(n, task, left, right, acc, many):
        lh, ll = left
        rh, rl = right

        @pl.loop(0, n)
        def _(t):
            for u in range(many):
                a0, a1, b0, b1, out = task(t * many + u)
                lhs = jnp.concatenate(
                    [
                        jnp.concatenate([lh[a0], lh[a1]], axis=1),
                        jnp.concatenate([ll[a0], ll[a1]], axis=1),
                    ],
                    axis=0,
                )
                rhs = jnp.concatenate(
                    [
                        jnp.concatenate([rh[b0], rl[b0]], axis=1),
                        jnp.concatenate([rh[b1], rl[b1]], axis=1),
                    ],
                    axis=0,
                )
                both = jnp.dot(lhs, rhs, preferred_element_type=F32)
                acc[out] = acc[out] + (both[:BS, :BS] + (both[:BS, BS:] + both[BS:, :BS]))

    low = lambda w: w & (WORD - 1)

    def plain(L, R):
        def task(t):
            r0 = R[2 * t]
            return low(L[2 * t]), low(L[2 * t + 1]), low(r0), low(R[2 * t + 1]), r0 >> 12

        return task

    def span(first, n_first, second, n_second):
        return lambda t: jnp.where(
            t < n_first, first + t, jnp.where(t < n_first + n_second, second + t - n_first, NOTHING)
        )

    def square(t):
        at = 2 * square_pair(t)
        r0 = sr[at]
        return low(sl[at]), low(sl[at + 1]), low(r0), low(sr[at + 1]), r0 >> 12

    def cube(t):
        at = 2 * cube_pair(t)
        r1 = sr[at + 1]
        return sl[at] >> 12, sl[at + 1] >> 12, low(sr[at]), low(r1), r1 >> 12

    n_out, n_in, n_again = head_ref[H_OUT], head_ref[H_IN], head_ref[H_AGAIN]
    square_pair = span(0, n_out, LIST // 2, n_in)
    cube_pair = span(LIST // 2, n_in, LIST, n_again)
    phase((n_out + n_in + UNROLL - 1) // UNROLL, square, (ch, cl), (ch, cl), sa, UNROLL)

    @pl.loop(0, (head_ref[H_TURN] + MANY - 1) // MANY)
    def _(t):
        words = [turn_ref[MANY * t + u] for u in range(MANY)]
        done = [sa[w & (WORD - 1)].T for w in words]
        for u in range(MANY):
            sa[words[u] >> 12] = done[u]

    @pl.loop(0, (head_ref[H_SB] + MANY - 1) // MANY)
    def _(t):
        done = [split(sa[MANY * t + u]) for u in range(MANY)]
        for u in range(MANY):
            sh[MANY * t + u], slo[MANY * t + u] = done[u]

    phase((n_in + n_again + UNROLL - 1) // UNROLL, cube, (sh, slo), (ch, cl), da, UNROLL)

    @pl.loop(0, (head_ref[H_DB] + MANY - 1) // MANY)
    def _(t):
        done = [split(3.0 * sa[ds_ref[MANY * t + u]] - 2.0 * da[MANY * t + u]) for u in range(MANY)]
        for u in range(MANY):
            dh[MANY * t + u], dl[MANY * t + u] = done[u]

    phase(head_ref[H_E], plain(el, er), (dh, dl), (dh, dl), ea, FEW)

    @pl.loop(0, head_ref[H_EB])
    def _(t):
        eh[t], elo[t] = split(ea[t])

    phase(head_ref[H_F], plain(fl, fr), (eh, elo), (dh, dl), fa, FEW)
    for a in range(out_ref.shape[0] // BS):
        at = fin_ref[a]
        value = 3.0 * ea[jnp.maximum(at, 0)] - 2.0 * fa[a]
        out_ref[a * BS : (a + 1) * BS, :] = jnp.where(at >= 0, value.T, 0.0)


def linear(x, y, z, core):
    return (((x % 2) * NY + y) * (NZ * NC) + z * NC + core) * 2 + x // 2


def send(value, step):
    pairs = [
        (linear(x, y, z, core), linear(*step(x, y, z, core)))
        for x in range(NX)
        for y in range(NY)
        for z in range(NZ)
        for core in range(NC)
    ]
    return lax.ppermute(value, ("row", "col", "layer"), pairs)


def along_z(d):
    return lambda x, y, z, core: (x, y, (z + d) % NZ, core)


def inner(d):
    return lambda x, y, z, core: ((x + d) % NX, y, z, core) if core == 0 else (x, (y + d) % NY, z, core)


def outer(d):
    return lambda x, y, z, core: (x, (y + d) % NY, z, core) if core == 0 else ((x + d) % NX, y, z, core)


def other_core(x, y, z, core):
    return x, y, z, 1 - core


def list_blocks(plan):
    smem = pl.BlockSpec(memory_space=pltpu.SMEM)
    i32 = lambda *shape: jax.ShapeDtypeStruct(shape, jnp.int32)
    return pl.pallas_call(
        block_kernel,
        out_shape=i32(sum(BLOCK_SIZES)),
        in_specs=[smem],
        out_specs=smem,
        cost_estimate=pl.CostEstimate(flops=0, bytes_accessed=6_000_000, transcendentals=0),
        name="list_blocks",
    )(plan)


def list_products(plan):
    smem = pl.BlockSpec(memory_space=pltpu.SMEM)
    i32 = lambda *shape: jax.ShapeDtypeStruct(shape, jnp.int32)
    return pl.pallas_call(
        table_kernel,
        out_shape=i32(sum(LIST_SIZES)),
        in_specs=[smem],
        out_specs=smem,
        scratch_shapes=[
            pltpu.SMEM((NB, NB), jnp.int32),
            pltpu.SMEM((NB, NB), jnp.int32),
            pltpu.SMEM((NB,), jnp.int32),
        ],
        cost_estimate=pl.CostEstimate(flops=0, bytes_accessed=20_000_000, transcendentals=0),
        name="list_products",
    )(plan)


def plan_products(pattern, *owners):
    smem = pl.BlockSpec(memory_space=pltpu.SMEM)
    vmem = pl.BlockSpec(memory_space=pltpu.VMEM)
    i32 = lambda *shape: jax.ShapeDtypeStruct(shape, jnp.int32)
    return pl.pallas_call(
        plan_kernel,
        out_shape=(i32(WIDE, LANES), i32(1)),
        in_specs=[vmem] * 4,
        out_specs=(vmem, smem),
        cost_estimate=pl.CostEstimate(flops=0, bytes_accessed=10_000_000, transcendentals=0),
        name="plan_products",
    )(pattern, *owners)


def to_chips_along_z(shard):
    lines = [[z * NC + c for z in range(NZ)] for c in range(NC)]
    copies = jnp.broadcast_to(shard, (NZ, SHARD, BS))
    return lax.all_to_all(
        copies, "col", split_axis=0, concat_axis=0, tiled=True, axis_index_groups=lines
    ).reshape(UNIT, BS)


def gather_pieces(shard, pattern, owners):
    tie = lax.optimization_barrier
    swap = lambda value: send(value, other_core)
    own = to_chips_along_z(shard)
    own, owners = tie((own, owners))
    line = [own] + [send(own, inner(d)) for d in (1, -1, 2)]
    plan, ok = plan_products(pattern, *owners)
    blocks = list_blocks(plan)
    line, blocks = tie((line, blocks))

    low, high = jnp.concatenate(line[:2], axis=0), jnp.concatenate(line[2:], axis=0)
    low, high, plan = tie((low, high, plan))
    back_low, ahead_high = send(low, outer(1)), send(high, outer(-1))
    back_high, ahead_low = send(high, outer(1)), send(low, outer(-1))
    tables = list_products(plan)
    back_low, ahead_high, tables = tie((back_low, ahead_high, tables))
    far_low, far_high = send(back_low, outer(1)), send(ahead_high, outer(-1))
    panel = jnp.concatenate([low, high], axis=0)
    panel, back_low, ahead_high, back_high, ahead_low = tie((panel, back_low, ahead_high, back_high, ahead_low))
    theirs = [swap(value) for value in (panel, back_low, ahead_high, back_high, ahead_low, far_low, far_high)]
    mine = [low, high, back_low, ahead_high, back_high, ahead_low, far_low, far_high]
    return ok, [blocks, tables], [*mine, *theirs]


def per_device(density, pattern):
    smem = pl.BlockSpec(memory_space=pltpu.SMEM)
    vmem = pl.BlockSpec(memory_space=pltpu.VMEM)

    square = jax.ShapeDtypeStruct((NB, NB), F32)
    packed, *owners = pl.pallas_call(
        pack_kernel,
        out_shape=(jax.ShapeDtypeStruct((CAP * BS, BS), F32), square, square, square),
        in_specs=[vmem, vmem],
        out_specs=[vmem] * 4,
        name="pack_blocks",
    )(pattern, density)

    rows = lax.axis_size("row")
    pieces = packed.reshape(rows, SHARD, BS)
    shard = jnp.sum(lax.all_to_all(pieces, "row", split_axis=0, concat_axis=0, tiled=True), axis=0)
    ok, tables, gathered = gather_pieces(shard, pattern, owners)

    def sparse(density, pattern, tables, gathered):
        block = lambda n, t: pltpu.VMEM((n, BS, BS), t)
        return pl.pallas_call(
            compute_kernel,
            out_shape=jax.ShapeDtypeStruct(density.shape, F32),
            in_specs=[smem] * len(tables) + [pl.BlockSpec(memory_space=pl.ANY)] * len(gathered),
            out_specs=vmem,
            scratch_shapes=[
                pltpu.VMEM((2 * RAW_HALF, BS), F32),
                block(ZERO + 2, BF16), block(ZERO + 2, BF16),
                block(S_CAP + 1, F32), block(S_CAP + 1, BF16), block(S_CAP + 1, BF16),
                block(D_CAP + 1, F32), block(D_CAP + 1, BF16), block(D_CAP + 1, BF16),
                block(E_CAP + 1, F32), block(E_CAP + 1, BF16), block(E_CAP + 1, BF16),
                block(NB // 8 + 1, F32),
                pltpu.SemaphoreType.DMA((len(gathered),)),
            ],
            compiler_params=pltpu.CompilerParams(vmem_limit_bytes=60 * 2**20),
            name="purify_column",
        )(*tables, *gathered)

    def dense(density, pattern, tables, gathered):
        return dense_plan(density, pattern)

    return lax.cond(ok[0] != 0, sparse, dense, density, pattern, tables, gathered)


def solution(mesh):
    return jax.shard_map(
        per_device,
        mesh=mesh,
        in_specs=(P("row", ("col", "layer")), P()),
        out_specs=P("row", ("col", "layer")),
        check_vma=False,
    )
```

```python
import jax
import jax.numpy as jnp
from jax import lax
from jax.experimental import pallas as pl
from jax.experimental.pallas import tpu as pltpu
from jax.sharding import PartitionSpec as P

BS = 128
ITERS = 2
NB = 32
CAP = 4
NS = NB * CAP
ROUNDS = 5
REPAIRS = 24
ZERO = 2 * NS
S_CAP = 104
D_CAP = 80
E_CAP = 16
PAIRS = 256
UNROLL = 8
FEW = 4
MANY = 4
LIST = 2 * PAIRS + 2 * UNROLL + 8
NZ, NC = 8, 2
NX, NY = 4, 4
SHARD = CAP * BS // 8
UNIT = NZ * SHARD
PANEL = 4 * UNIT
RAW_HALF = 4 * PANEL
WIDE = 40
WORD = 4096
HALF_WORD = 256
OK = WIDE - 1
LANES = 128
NEAR = WIDE
NEED = 2 * WIDE
SIZE = WIDE - 1
F32 = jnp.float32
BF16 = jnp.bfloat16


def panel_cols(tile, layers):
    row_count, shard_cols = tile.shape
    gathered = lax.all_gather(tile, "row", axis=0, tiled=True)
    pieces = gathered.reshape(
        gathered.shape[0] // (shard_cols * layers), layers, shard_cols, shard_cols
    )
    arranged = lax.all_to_all(pieces, "layer", split_axis=1, concat_axis=3, tiled=True)
    return arranged.reshape(-1, layers * shard_cols)


def multiply(left_tile, right_panel):
    partial_sum = jnp.dot(
        lax.all_gather(left_tile, "col", axis=1, tiled=True),
        right_panel,
        precision=lax.Precision.HIGHEST,
        preferred_element_type=jnp.float32,
    )
    return lax.psum_scatter(partial_sum, "layer", scatter_dimension=1, tiled=True)


def dense_plan(density, pattern):
    row_index = lax.axis_index("row")
    col_index = lax.axis_index("col")
    layer_index = lax.axis_index("layer")
    layers = lax.axis_size("layer")
    row_count, shard_cols = density.shape
    blocks = pattern.shape[0]
    block_line = jnp.arange(blocks, dtype=jnp.int32)
    row_ids = (row_index * row_count + jnp.arange(row_count, dtype=jnp.int32)) // BS
    col_ids = (
        (col_index * layers + layer_index) * shard_cols + jnp.arange(shard_cols, dtype=jnp.int32)
    ) // BS
    pick_rows = (row_ids[:, None] == block_line[None, :]).astype(jnp.float32)
    pick_cols = (col_ids[:, None] == block_line[None, :]).astype(jnp.float32)
    occupied = pattern.astype(jnp.float32)
    in_pattern = jnp.dot(
        jnp.dot(pick_rows, occupied, precision=lax.Precision.HIGHEST),
        pick_cols.T,
        precision=lax.Precision.HIGHEST,
    )
    current = in_pattern * density
    for iteration in range(ITERS):
        current_panel = panel_cols(current, layers)
        squared = in_pattern * multiply(current, current_panel)
        cube_term = in_pattern * multiply(current, panel_cols(squared, layers))
        current = 3.0 * squared - 2.0 * cube_term
    return current


def here():
    row = lax.axis_index("row").astype(jnp.int32)
    column = lax.axis_index("col") * lax.axis_size("layer") + lax.axis_index("layer")
    return row, column.astype(jnp.int32)


def ring_place(source, at):
    back = (at - source) & 3
    return jnp.where(back == 3, 2, jnp.where(back == 2, 3, back))


def raw_row(column, p, j, r):
    px = ring_place((column & 1) * 2 + (p >> 2), (j & 1) * 2 + (r >> 2))
    py = ring_place(p & 3, r & 3)
    core = (column >> 1) & 1
    near, far = jnp.where(core == 0, px, py), jnp.where(core == 0, py, px)
    other = jnp.where(((j >> 1) & 1) == core, 0, 1)
    high = near >> 1
    ring = 2 + jnp.where(far == 1, 2 * high, 3 - 2 * high)
    group = jnp.where(far == 0, high, jnp.where(far == 3, 6 + high, ring))
    return other * RAW_HALF + group * (PANEL // 2) + (near & 1) * UNIT + (column >> 2) * SHARD


def pack_kernel(pat_ref, tile_ref, packed_ref, own_ref, own_t_ref, rank_ref):
    r, j = here()
    K = (pat_ref[...] != 0).astype(F32)
    ii = lax.broadcasted_iota(jnp.int32, (NB, NB), 0)
    jj = lax.broadcasted_iota(jnp.int32, (NB, NB), 1)
    diag = (ii == jj).astype(F32)
    left = K * (1.0 - diag)
    own = diag
    own_t = diag
    after = (ii > jj).astype(F32)
    before = (ii < jj).astype(F32)
    for _ in range(ROUNDS):
        fc = (jnp.sum(left, axis=0, keepdims=True) <= CAP - 1).astype(F32)
        fr = (jnp.sum(left, axis=1, keepdims=True) <= CAP - 1).astype(F32)
        own = own + left * fc * ((1.0 - fr) + fr * after)
        own_t = own_t + left * fr * ((1.0 - fc) + fc * before)
        left = left * (1.0 - fc) * (1.0 - fr)
    own = own + left * after
    own_t = own_t + left * before

    number = ii * NB + jj
    number_t = jj * NB + ii

    def move(_, held):
        own, own_t = held
        load_row = jnp.sum(own, axis=0, keepdims=True)
        load_col = jnp.sum(own_t, axis=1, keepdims=True)
        source = own * (1.0 - diag) * (load_row > CAP).astype(F32)
        room = source * (load_col < CAP).astype(F32)
        onward = jnp.max(own_t * (1.0 - diag) * (load_row < CAP).astype(F32), axis=1, keepdims=True)
        through = source * onward * (load_col == CAP).astype(F32)
        none = jnp.max(room, axis=(0, 1), keepdims=True) == 0.0
        use = jnp.where(none, through, room)
        first = jnp.min(jnp.where(use > 0, number, NB * NB), axis=(0, 1), keepdims=True)
        flip = (number == first).astype(F32)
        flip_t = (number_t == first).astype(F32)
        return own - flip + flip_t, own_t - flip_t + flip

    crowded = jnp.max(jnp.sum(own, axis=0)) > CAP
    own, own_t = lax.fori_loop(0, jnp.where(crowded, REPAIRS, 0), move, (own, own_t))
    rank = jnp.dot(after, own, preferred_element_type=F32)
    own_ref[...] = own
    own_t_ref[...] = own_t
    rank_ref[...] = rank

    for s in range(CAP):
        total = jnp.zeros((BS, BS), F32)
        for a in range(tile_ref.shape[0] // BS):
            at = (ii == r * (tile_ref.shape[0] // BS) + a) & (jj == j)
            pick = at & (own > 0) & (rank == s)
            w = jnp.sum(jnp.where(pick, 1.0, 0.0), axis=(0, 1), keepdims=True)
            total = total + w * tile_ref[a * BS : (a + 1) * BS, :]
        packed_ref[s * BS : (s + 1) * BS, :] = total


def plan_kernel(
    pat_ref, own_ref, own_t_ref, rank_ref,
    plan_ref, ok_ref,
):
    r, j = here()
    K = (pat_ref[...] != 0).astype(F32)
    ii = lax.broadcasted_iota(jnp.int32, (NB, NB), 0)
    jj = lax.broadcasted_iota(jnp.int32, (NB, NB), 1)
    before = (ii < jj).astype(F32)
    own = own_ref[...]
    own_t = own_t_ref[...]
    rank = rank_ref[...]
    rank_t = jnp.dot(own_t, before, preferred_element_type=F32)
    slot = jj * CAP + rank.astype(jnp.int32)
    slot_t = ii * CAP + rank_t.astype(jnp.int32)
    cid = jnp.where(own > 0, slot, jnp.where(own_t > 0, NS + slot_t, ZERO))
    column = jnp.where(own > 0, jj, ii)
    turn = jnp.where(own > 0, rank, rank_t).astype(jnp.int32)
    first, second = [raw_row(column, 2 * turn + n, j, r) // SHARD for n in range(2)]
    blocks = cid + (first + second * HALF_WORD) * WORD

    common = jnp.dot(K, K, preferred_element_type=F32)
    pairs = K * jnp.floor((common + 1.0) * 0.5)
    s_blocks = jnp.max(jnp.sum(common, axis=1))
    d_blocks = jnp.max(jnp.sum(common * K, axis=1))
    spread = jnp.dot(K, pairs, preferred_element_type=F32)
    s_pairs = jnp.max(jnp.sum(spread, axis=1))
    fits = (
        (jnp.max(jnp.sum(own, axis=0)) <= CAP)
        & (s_blocks <= S_CAP)
        & (d_blocks <= D_CAP)
        & (s_pairs <= PAIRS)
        & (jnp.max(jnp.sum(K, axis=1)) <= E_CAP)
    )
    ok_ref[0] = fits.astype(jnp.int32)
    last = lax.broadcasted_iota(jnp.int32, (WIDE - NB, LANES), 0) == OK - NB
    plan_ref[NB:WIDE, :] = jnp.where(last, fits.astype(jnp.int32), ZERO)

    kj = jnp.sum(jnp.where(jj == j, K, 0.0), axis=1, keepdims=True)
    near = lax.dot_general(K * kj, K, (((0,), (0,)), ((), ())), preferred_element_type=F32)
    wanted = jnp.where((near > 0) & (K > 0), 1.0, 0.0)
    wide = lax.broadcasted_iota(jnp.int32, (NB, LANES), 1)
    out = jnp.where(wide < NEED, NB + ZERO * WORD, NB)
    for listed, value, at in ((K, jj + cid * WORD, NEAR), (wanted, jj, NEED)):
        place = jnp.dot(listed, before, preferred_element_type=F32).astype(jnp.int32)
        place = jnp.where(listed > 0, place, -1)
        size = jnp.sum(listed, axis=1, keepdims=True).astype(jnp.int32)
        out = jnp.where(wide == at + SIZE, size, out)
        for d in range(NB):
            entry = jnp.sum(jnp.where(place == d, value, 0), axis=1, keepdims=True)
            out = jnp.where((wide == at + d) & (size > d), entry, out)
    plan_ref[:NB, :] = out
    plan_ref[:NB, :NB] = blocks


H_OUT, H_IN, H_AGAIN, H_E, H_F, H_SB, H_DB, H_EB, H_TURN = range(9)


class Part:
    def __init__(self, ref, start):
        self.ref, self.start = ref, start

    def __getitem__(self, at):
        return self.ref[self.start + at]

    def __setitem__(self, at, value):
        self.ref[self.start + at] = value


def parts_of(ref, sizes):
    return [Part(ref, sum(sizes[:n])) for n in range(len(sizes))]


BLOCK_SIZES = [8, *[2 * NS + 8] * 4]
SHORT = 160
NOTHING = PAIRS + 4
LIST_SIZES = [16, *[3 * LIST] * 2, *[SHORT] * 4, D_CAP + MANY, D_CAP + MANY, 8]


def block_kernel(plan, blocks_ref):
    head_ref, pn_ref, pt_ref, an_ref, at_ref = parts_of(blocks_ref, BLOCK_SIZES)
    ok = plan[OK, 0]

    def lines(i, carry):
        def entry(d, c):
            pn, pt = c
            word = plan[i, plan[i, NEED + d]]
            held = word & (WORD - 1)
            row = word >> 12
            flipped = (held >= NS).astype(jnp.int32)
            pn_ref[pn] = held
            pt_ref[pt] = held
            an_ref[pn] = row
            at_ref[pt] = row
            return pn + (1 - flipped), pt + flipped

        return lax.fori_loop(0, plan[i, NEED + SIZE] * ok, entry, carry)

    pn, pt = lax.fori_loop(0, NB, lines, (0, 0))
    for names, rows, n in ((pn_ref, an_ref, pn), (pt_ref, at_ref, pt)):
        for u in range(MANY - 1):
            names[n + u] = ZERO + 1
            rows[n + u] = 0
    head_ref[0] = pn
    head_ref[1] = pt


def table_kernel(plan, lists_ref, sid, did, eid):
    head_ref, sl, sr, el, er, fl, fr, ds_ref, turn_ref, fin_ref = parts_of(lists_ref, LIST_SIZES)
    r, j = here()
    ok = plan[OK, 0]

    def cid(q, k):
        return plan[q, k] & (WORD - 1)

    nj = plan[j, NEAR + SIZE] * ok

    def row(a, carry):
        m = plan[j, NEAR + a] & (WORD - 1)
        nm = plan[m, NEAR + SIZE]
        base = carry[3] * WORD

        def output(b, c):
            apart, inner_, again, count, dcount, turns = c
            k = plan[m, NEAR + b] & (WORD - 1)
            inside = cid(k, j) != ZERO
            turned = inside & (k < m)
            start = jnp.where(turned, again, jnp.where(inside, inner_, apart))
            outs = count * WORD
            outd = dcount * WORD

            def eight(g, p):
                at = g * 8
                words = [plan[m, NEAR + at + u] for u in range(8)]
                rs = [cid(w & (WORD - 1), k) for w in words]
                for u in range(8):
                    sl[p] = (words[u] >> 12) + (base + (at + u) * WORD)
                    sr[p] = rs[u] + jnp.where((p & 1) == 1, outd, outs)
                    p = p + (rs[u] != ZERO).astype(jnp.int32)
                return p

            p = lax.fori_loop(0, (nm + 7) >> 3, eight, start)
            sl[p] = ZERO + S_CAP * WORD
            sr[p] = ZERO + outd
            p = p + (p & 1)
            sid[m, k] = count
            did[m, k] = dcount
            ds_ref[dcount] = count
            turn_ref[turns] = jnp.where(turned, sid[k, m], 0) + outs
            return (
                jnp.where(inside, apart, p),
                jnp.where(inside & jnp.logical_not(turned), p, inner_),
                jnp.where(turned, p, again),
                count + 1,
                dcount + inside.astype(jnp.int32),
                turns + turned.astype(jnp.int32),
            )

        return lax.fori_loop(0, nm, output, carry)

    done = lax.fori_loop(0, nj, row, (0, LIST, 2 * LIST, 0, 0, 0))
    apart, inner_, again, count, dcount, turns = done
    for t, out in enumerate((S_CAP, D_CAP)):
        sl[2 * NOTHING + t] = ZERO + S_CAP * WORD
        sr[2 * NOTHING + t] = ZERO + out * WORD
    for u in range(MANY - 1):
        ds_ref[dcount + u] = 0
        turn_ref[turns + u] = S_CAP * WORD
    head_ref[H_OUT] = apart >> 1
    head_ref[H_IN] = (inner_ - LIST) >> 1
    head_ref[H_AGAIN] = (again - 2 * LIST) >> 1
    head_ref[H_TURN] = turns
    head_ref[H_SB] = count
    head_ref[H_DB] = dcount

    def finish(refs, pos, lz, dummy):
        L, R = refs
        for t in range(2 * FEW):
            L[pos + t] = lz
            R[pos + t] = D_CAP + dummy * WORD
        return ((pos >> 1) + FEW - 1) // FEW

    def gather(refs, pos, k, left, out, lz):
        L, R = refs

        def entry(c, p):
            m = plan[j, NEAR + c] & (WORD - 1)
            L[p] = left(m)
            R[p] = did[m, k] + out * WORD
            return p + (cid(m, k) != ZERO).astype(jnp.int32)

        p = lax.fori_loop(0, nj, entry, pos)
        L[p] = lz
        R[p] = D_CAP + out * WORD
        return p + (p & 1)

    def e_out(b, pos):
        k = plan[j, NEAR + b] & (WORD - 1)
        eid[k] = b
        return gather((el, er), pos, k, lambda m: did[j, m], b, D_CAP)

    pos = lax.fori_loop(0, nj, e_out, 0)
    head_ref[H_E] = finish((el, er), pos, D_CAP, E_CAP)
    head_ref[H_EB] = nj

    per = NB // 8

    def f_out(a, pos):
        i = r * per + a

        def stored(pos):
            fin_ref[a] = eid[i]
            return gather((fl, fr), pos, i, lambda k: eid[k], a, E_CAP)

        def absent(pos):
            fin_ref[a] = -1
            return pos

        return lax.cond((cid(i, j) != ZERO) & (ok != 0), stored, absent, pos)

    pos = lax.fori_loop(0, per, f_out, 0)
    head_ref[H_F] = finish((fl, fr), pos, E_CAP, per)


class Blocks:
    def __init__(self, ref):
        self.ref = ref

    def rows(self, at):
        return pl.ds(pl.multiple_of(at * BS, BS), BS)

    def __getitem__(self, at):
        return self.ref[self.rows(at), :]

    def __setitem__(self, at, value):
        self.ref[self.rows(at), :] = value


def split(x):
    hi = x.astype(BF16)
    return hi, (x - hi.astype(F32)).astype(BF16)


def compute_kernel(
    blocks_in, lists_in,
    *rest,
):
    blocks_ref, pn_ref, pt_ref, an_ref, at_ref = parts_of(blocks_in, BLOCK_SIZES)
    head_ref, sl, sr, el, er, fl, fr, ds_ref, turn_ref, fin_ref = parts_of(lists_in, LIST_SIZES)
    pieces, rest = rest[:-14], rest[-14:]
    out_ref, raw, ch, cl, sh, slo, da, dh, dl, ea, eh, elo, fa, sem = rest
    sa = Blocks(raw)
    copies = []
    row = 0
    for n, piece in enumerate(pieces):
        height = piece.shape[0]
        copies.append(pltpu.make_async_copy(piece, raw.at[pl.ds(row, height)], sem.at[n]))
        row += height
    for c in copies:
        c.start()
    zero = jnp.zeros((BS, BS), BF16)
    for hi, lo, at in ((ch, cl, ZERO), (sh, slo, S_CAP), (dh, dl, D_CAP), (eh, elo, E_CAP)):
        hi[at] = zero
        lo[at] = zero

    def clear(ref, n):
        @pl.loop(0, n)
        def _(t):
            ref[t] = jnp.zeros((BS, BS), F32)

    clear(da, head_ref[H_DB])
    clear(ea, head_ref[H_EB])
    clear(fa, fa.shape[0])
    for c in copies:
        c.wait()

    def prepare(n, names, rows, turn):
        @pl.loop(0, (n + MANY - 1) // MANY)
        def _(t):
            ids = [names[MANY * t + u] for u in range(MANY)]
            xs = []
            for u in range(MANY):
                word = rows[MANY * t + u]
                parts = [
                    raw[pl.ds(pl.multiple_of(at * SHARD, SHARD), SHARD), :] for at in (word & (HALF_WORD - 1), word >> 8)
                ]
                xs.append(split(turn(jnp.concatenate(parts, axis=0))))
            for a, (hi, lo) in zip(ids, xs):
                ch[a] = hi
                cl[a] = lo

    prepare(blocks_ref[0], pn_ref, an_ref, lambda v: v)
    prepare(blocks_ref[1], pt_ref, at_ref, lambda v: v.T)
    clear(sa, head_ref[H_SB])

    def phase(n, task, left, right, acc, many):
        lh, ll = left
        rh, rl = right

        @pl.loop(0, n)
        def _(t):
            for u in range(many):
                a0, a1, b0, b1, out = task(t * many + u)
                lhs = jnp.concatenate(
                    [
                        jnp.concatenate([lh[a0], lh[a1]], axis=1),
                        jnp.concatenate([ll[a0], ll[a1]], axis=1),
                    ],
                    axis=0,
                )
                rhs = jnp.concatenate(
                    [
                        jnp.concatenate([rh[b0], rl[b0]], axis=1),
                        jnp.concatenate([rh[b1], rl[b1]], axis=1),
                    ],
                    axis=0,
                )
                both = jnp.dot(lhs, rhs, preferred_element_type=F32)
                acc[out] = acc[out] + (both[:BS, :BS] + (both[:BS, BS:] + both[BS:, :BS]))

    low = lambda w: w & (WORD - 1)

    def plain(L, R):
        def task(t):
            r0 = R[2 * t]
            return low(L[2 * t]), low(L[2 * t + 1]), low(r0), low(R[2 * t + 1]), r0 >> 12

        return task

    def span(first, n_first, second, n_second):
        return lambda t: jnp.where(
            t < n_first, first + t, jnp.where(t < n_first + n_second, second + t - n_first, NOTHING)
        )

    def square(t):
        at = 2 * square_pair(t)
        r0 = sr[at]
        return low(sl[at]), low(sl[at + 1]), low(r0), low(sr[at + 1]), r0 >> 12

    def cube(t):
        at = 2 * cube_pair(t)
        r1 = sr[at + 1]
        return sl[at] >> 12, sl[at + 1] >> 12, low(sr[at]), low(r1), r1 >> 12

    n_out, n_in, n_again = head_ref[H_OUT], head_ref[H_IN], head_ref[H_AGAIN]
    square_pair = span(0, n_out, LIST // 2, n_in)
    cube_pair = span(LIST // 2, n_in, LIST, n_again)
    phase((n_out + n_in + UNROLL - 1) // UNROLL, square, (ch, cl), (ch, cl), sa, UNROLL)

    @pl.loop(0, (head_ref[H_TURN] + MANY - 1) // MANY)
    def _(t):
        words = [turn_ref[MANY * t + u] for u in range(MANY)]
        done = [sa[w & (WORD - 1)].T for w in words]
        for u in range(MANY):
            sa[words[u] >> 12] = done[u]

    @pl.loop(0, (head_ref[H_SB] + MANY - 1) // MANY)
    def _(t):
        done = [split(sa[MANY * t + u]) for u in range(MANY)]
        for u in range(MANY):
            sh[MANY * t + u], slo[MANY * t + u] = done[u]

    phase((n_in + n_again + UNROLL - 1) // UNROLL, cube, (sh, slo), (ch, cl), da, UNROLL)

    @pl.loop(0, (head_ref[H_DB] + MANY - 1) // MANY)
    def _(t):
        done = [split(3.0 * sa[ds_ref[MANY * t + u]] - 2.0 * da[MANY * t + u]) for u in range(MANY)]
        for u in range(MANY):
            dh[MANY * t + u], dl[MANY * t + u] = done[u]

    phase(head_ref[H_E], plain(el, er), (dh, dl), (dh, dl), ea, FEW)

    @pl.loop(0, head_ref[H_EB])
    def _(t):
        eh[t], elo[t] = split(ea[t])

    phase(head_ref[H_F], plain(fl, fr), (eh, elo), (dh, dl), fa, FEW)
    for a in range(out_ref.shape[0] // BS):
        at = fin_ref[a]
        value = 3.0 * ea[jnp.maximum(at, 0)] - 2.0 * fa[a]
        out_ref[a * BS : (a + 1) * BS, :] = jnp.where(at >= 0, value.T, 0.0)


def linear(x, y, z, core):
    return (((x % 2) * NY + y) * (NZ * NC) + z * NC + core) * 2 + x // 2


def send(value, step):
    pairs = [
        (linear(x, y, z, core), linear(*step(x, y, z, core)))
        for x in range(NX)
        for y in range(NY)
        for z in range(NZ)
        for core in range(NC)
    ]
    return lax.ppermute(value, ("row", "col", "layer"), pairs)


def along_z(d):
    return lambda x, y, z, core: (x, y, (z + d) % NZ, core)


def inner(d):
    return lambda x, y, z, core: ((x + d) % NX, y, z, core) if core == 0 else (x, (y + d) % NY, z, core)


def outer(d):
    return lambda x, y, z, core: (x, (y + d) % NY, z, core) if core == 0 else ((x + d) % NX, y, z, core)


def other_core(x, y, z, core):
    return x, y, z, 1 - core


def list_blocks(plan):
    smem = pl.BlockSpec(memory_space=pltpu.SMEM)
    i32 = lambda *shape: jax.ShapeDtypeStruct(shape, jnp.int32)
    return pl.pallas_call(
        block_kernel,
        out_shape=i32(sum(BLOCK_SIZES)),
        in_specs=[smem],
        out_specs=smem,
        cost_estimate=pl.CostEstimate(flops=0, bytes_accessed=6_000_000, transcendentals=0),
        name="list_blocks",
    )(plan)


def list_products(plan):
    smem = pl.BlockSpec(memory_space=pltpu.SMEM)
    i32 = lambda *shape: jax.ShapeDtypeStruct(shape, jnp.int32)
    return pl.pallas_call(
        table_kernel,
        out_shape=i32(sum(LIST_SIZES)),
        in_specs=[smem],
        out_specs=smem,
        scratch_shapes=[
            pltpu.SMEM((NB, NB), jnp.int32),
            pltpu.SMEM((NB, NB), jnp.int32),
            pltpu.SMEM((NB,), jnp.int32),
        ],
        cost_estimate=pl.CostEstimate(flops=0, bytes_accessed=20_000_000, transcendentals=0),
        name="list_products",
    )(plan)


def plan_products(pattern, *owners):
    smem = pl.BlockSpec(memory_space=pltpu.SMEM)
    vmem = pl.BlockSpec(memory_space=pltpu.VMEM)
    i32 = lambda *shape: jax.ShapeDtypeStruct(shape, jnp.int32)
    return pl.pallas_call(
        plan_kernel,
        out_shape=(i32(WIDE, LANES), i32(1)),
        in_specs=[vmem] * 4,
        out_specs=(vmem, smem),
        cost_estimate=pl.CostEstimate(flops=0, bytes_accessed=10_000_000, transcendentals=0),
        name="plan_products",
    )(pattern, *owners)


def to_chips_along_z(shard):
    lines = [[z * NC + c for z in range(NZ)] for c in range(NC)]
    copies = jnp.broadcast_to(shard, (NZ, SHARD, BS))
    return lax.all_to_all(
        copies, "col", split_axis=0, concat_axis=0, tiled=True, axis_index_groups=lines
    ).reshape(UNIT, BS)


def gather_pieces(shard, pattern, owners):
    tie = lax.optimization_barrier
    swap = lambda value: send(value, other_core)
    own = to_chips_along_z(shard)
    own, owners = tie((own, owners))
    line = [own] + [send(own, inner(d)) for d in (1, -1, 2)]
    plan, ok = plan_products(pattern, *owners)
    blocks = list_blocks(plan)
    line, blocks = tie((line, blocks))

    low, high = jnp.concatenate(line[:2], axis=0), jnp.concatenate(line[2:], axis=0)
    low, high, plan = tie((low, high, plan))
    back_low, ahead_high = send(low, outer(1)), send(high, outer(-1))
    back_high, ahead_low = send(high, outer(1)), send(low, outer(-1))
    tables = list_products(plan)
    back_low, ahead_high, tables = tie((back_low, ahead_high, tables))
    far_low, far_high = send(back_low, outer(1)), send(ahead_high, outer(-1))
    panel = jnp.concatenate([low, high], axis=0)
    panel, back_low, ahead_high, back_high, ahead_low = tie((panel, back_low, ahead_high, back_high, ahead_low))
    theirs = [swap(value) for value in (panel, back_low, ahead_high, back_high, ahead_low, far_low, far_high)]
    mine = [low, high, back_low, ahead_high, back_high, ahead_low, far_low, far_high]
    return ok, [blocks, tables], [*mine, *theirs]


def per_device(density, pattern):
    smem = pl.BlockSpec(memory_space=pltpu.SMEM)
    vmem = pl.BlockSpec(memory_space=pltpu.VMEM)

    square = jax.ShapeDtypeStruct((NB, NB), F32)
    packed, *owners = pl.pallas_call(
        pack_kernel,
        out_shape=(jax.ShapeDtypeStruct((CAP * BS, BS), F32), square, square, square),
        in_specs=[vmem, vmem],
        out_specs=[vmem] * 4,
        name="pack_blocks",
    )(pattern, density)

    rows = lax.axis_size("row")
    pieces = packed.reshape(rows, SHARD, BS)
    shard = jnp.sum(lax.all_to_all(pieces, "row", split_axis=0, concat_axis=0, tiled=True), axis=0)
    ok, tables, gathered = gather_pieces(shard, pattern, owners)

    def sparse(density, pattern, tables, gathered):
        block = lambda n, t: pltpu.VMEM((n, BS, BS), t)
        return pl.pallas_call(
            compute_kernel,
            out_shape=jax.ShapeDtypeStruct(density.shape, F32),
            in_specs=[smem] * len(tables) + [pl.BlockSpec(memory_space=pl.ANY)] * len(gathered),
            out_specs=vmem,
            scratch_shapes=[
                pltpu.VMEM((2 * RAW_HALF, BS), F32),
                block(ZERO + 2, BF16), block(ZERO + 2, BF16),
                block(S_CAP + 1, BF16), block(S_CAP + 1, BF16),
                block(D_CAP + 1, F32), block(D_CAP + 1, BF16), block(D_CAP + 1, BF16),
                block(E_CAP + 1, F32), block(E_CAP + 1, BF16), block(E_CAP + 1, BF16),
                block(NB // 8 + 1, F32),
                pltpu.SemaphoreType.DMA((len(gathered),)),
            ],
            compiler_params=pltpu.CompilerParams(vmem_limit_bytes=48 * 2**20),
            name="purify_column",
        )(*tables, *gathered)

    def dense(density, pattern, tables, gathered):
        return dense_plan(density, pattern)

    return lax.cond(ok[0] != 0, sparse, dense, density, pattern, tables, gathered)


def solution(mesh):
    return jax.shard_map(
        per_device,
        mesh=mesh,
        in_specs=(P("row", ("col", "layer")), P()),
        out_specs=P("row", ("col", "layer")),
        check_vma=False,
    )
```

```python
import jax
import jax.numpy as jnp
from jax import lax
from jax.experimental import pallas as pl
from jax.experimental.pallas import tpu as pltpu
from jax.sharding import PartitionSpec as P

BS = 128
ITERS = 2
NB = 32
CAP = 4
NS = NB * CAP
ROUNDS = 5
REPAIRS = 24
ZERO = 2 * NS
S_CAP = 104
D_CAP = 80
E_CAP = 16
PAIRS = 256
UNROLL = 8
FEW = 4
MANY = 4
LIST = 2 * PAIRS + 2 * UNROLL + 8
NZ, NC = 8, 2
NX, NY = 4, 4
SHARD = CAP * BS // 8
UNIT = NZ * SHARD
PANEL = 4 * UNIT
RAW_HALF = 4 * PANEL
WIDE = 40
WORD = 4096
HALF_WORD = 256
OK = WIDE - 1
LANES = 128
NEAR = WIDE
NEED = 2 * WIDE
SIZE = WIDE - 1
F32 = jnp.float32
BF16 = jnp.bfloat16


def panel_cols(tile, layers):
    row_count, shard_cols = tile.shape
    gathered = lax.all_gather(tile, "row", axis=0, tiled=True)
    pieces = gathered.reshape(
        gathered.shape[0] // (shard_cols * layers), layers, shard_cols, shard_cols
    )
    arranged = lax.all_to_all(pieces, "layer", split_axis=1, concat_axis=3, tiled=True)
    return arranged.reshape(-1, layers * shard_cols)


def multiply(left_tile, right_panel):
    partial_sum = jnp.dot(
        lax.all_gather(left_tile, "col", axis=1, tiled=True),
        right_panel,
        precision=lax.Precision.HIGHEST,
        preferred_element_type=jnp.float32,
    )
    return lax.psum_scatter(partial_sum, "layer", scatter_dimension=1, tiled=True)


def dense_plan(density, pattern):
    row_index = lax.axis_index("row")
    col_index = lax.axis_index("col")
    layer_index = lax.axis_index("layer")
    layers = lax.axis_size("layer")
    row_count, shard_cols = density.shape
    blocks = pattern.shape[0]
    block_line = jnp.arange(blocks, dtype=jnp.int32)
    row_ids = (row_index * row_count + jnp.arange(row_count, dtype=jnp.int32)) // BS
    col_ids = (
        (col_index * layers + layer_index) * shard_cols + jnp.arange(shard_cols, dtype=jnp.int32)
    ) // BS
    pick_rows = (row_ids[:, None] == block_line[None, :]).astype(jnp.float32)
    pick_cols = (col_ids[:, None] == block_line[None, :]).astype(jnp.float32)
    occupied = pattern.astype(jnp.float32)
    in_pattern = jnp.dot(
        jnp.dot(pick_rows, occupied, precision=lax.Precision.HIGHEST),
        pick_cols.T,
        precision=lax.Precision.HIGHEST,
    )
    current = in_pattern * density
    for iteration in range(ITERS):
        current_panel = panel_cols(current, layers)
        squared = in_pattern * multiply(current, current_panel)
        cube_term = in_pattern * multiply(current, panel_cols(squared, layers))
        current = 3.0 * squared - 2.0 * cube_term
    return current


def here():
    row = lax.axis_index("row").astype(jnp.int32)
    column = lax.axis_index("col") * lax.axis_size("layer") + lax.axis_index("layer")
    return row, column.astype(jnp.int32)


def ring_place(source, at):
    back = (at - source) & 3
    return jnp.where(back == 3, 2, jnp.where(back == 2, 3, back))


def raw_row(column, p, j, r):
    px = ring_place((column & 1) * 2 + (p >> 2), (j & 1) * 2 + (r >> 2))
    py = ring_place(p & 3, r & 3)
    core = (column >> 1) & 1
    near, far = jnp.where(core == 0, px, py), jnp.where(core == 0, py, px)
    other = jnp.where(((j >> 1) & 1) == core, 0, 1)
    high = near >> 1
    ring = 2 + jnp.where(far == 1, 2 * high, 3 - 2 * high)
    group = jnp.where(far == 0, high, jnp.where(far == 3, 6 + high, ring))
    return other * RAW_HALF + group * (PANEL // 2) + (near & 1) * UNIT + (column >> 2) * SHARD


def pack_kernel(pat_ref, tile_ref, packed_ref, own_ref, own_t_ref, rank_ref):
    r, j = here()
    K = (pat_ref[...] != 0).astype(F32)
    ii = lax.broadcasted_iota(jnp.int32, (NB, NB), 0)
    jj = lax.broadcasted_iota(jnp.int32, (NB, NB), 1)
    diag = (ii == jj).astype(F32)
    left = K * (1.0 - diag)
    own = diag
    own_t = diag
    after = (ii > jj).astype(F32)
    before = (ii < jj).astype(F32)
    for _ in range(ROUNDS):
        fc = (jnp.sum(left, axis=0, keepdims=True) <= CAP - 1).astype(F32)
        fr = (jnp.sum(left, axis=1, keepdims=True) <= CAP - 1).astype(F32)
        own = own + left * fc * ((1.0 - fr) + fr * after)
        own_t = own_t + left * fr * ((1.0 - fc) + fc * before)
        left = left * (1.0 - fc) * (1.0 - fr)
    own = own + left * after
    own_t = own_t + left * before

    number = ii * NB + jj
    number_t = jj * NB + ii

    def move(_, held):
        own, own_t = held
        load_row = jnp.sum(own, axis=0, keepdims=True)
        load_col = jnp.sum(own_t, axis=1, keepdims=True)
        source = own * (1.0 - diag) * (load_row > CAP).astype(F32)
        room = source * (load_col < CAP).astype(F32)
        onward = jnp.max(own_t * (1.0 - diag) * (load_row < CAP).astype(F32), axis=1, keepdims=True)
        through = source * onward * (load_col == CAP).astype(F32)
        none = jnp.max(room, axis=(0, 1), keepdims=True) == 0.0
        use = jnp.where(none, through, room)
        first = jnp.min(jnp.where(use > 0, number, NB * NB), axis=(0, 1), keepdims=True)
        flip = (number == first).astype(F32)
        flip_t = (number_t == first).astype(F32)
        return own - flip + flip_t, own_t - flip_t + flip

    crowded = jnp.max(jnp.sum(own, axis=0)) > CAP
    own, own_t = lax.fori_loop(0, jnp.where(crowded, REPAIRS, 0), move, (own, own_t))
    rank = jnp.dot(after, own, preferred_element_type=F32)
    own_ref[...] = own
    own_t_ref[...] = own_t
    rank_ref[...] = rank

    for s in range(CAP):
        total = jnp.zeros((BS, BS), F32)
        for a in range(tile_ref.shape[0] // BS):
            at = (ii == r * (tile_ref.shape[0] // BS) + a) & (jj == j)
            pick = at & (own > 0) & (rank == s)
            w = jnp.sum(jnp.where(pick, 1.0, 0.0), axis=(0, 1), keepdims=True)
            total = total + w * tile_ref[a * BS : (a + 1) * BS, :]
        packed_ref[s * BS : (s + 1) * BS, :] = total


def plan_kernel(
    pat_ref, own_ref, own_t_ref, rank_ref,
    plan_ref, ok_ref,
):
    r, j = here()
    K = (pat_ref[...] != 0).astype(F32)
    ii = lax.broadcasted_iota(jnp.int32, (NB, NB), 0)
    jj = lax.broadcasted_iota(jnp.int32, (NB, NB), 1)
    before = (ii < jj).astype(F32)
    own = own_ref[...]
    own_t = own_t_ref[...]
    rank = rank_ref[...]
    rank_t = jnp.dot(own_t, before, preferred_element_type=F32)
    slot = jj * CAP + rank.astype(jnp.int32)
    slot_t = ii * CAP + rank_t.astype(jnp.int32)
    cid = jnp.where(own > 0, slot, jnp.where(own_t > 0, NS + slot_t, ZERO))
    column = jnp.where(own > 0, jj, ii)
    turn = jnp.where(own > 0, rank, rank_t).astype(jnp.int32)
    first, second = [raw_row(column, 2 * turn + n, j, r) // SHARD for n in range(2)]
    blocks = cid + (first + second * HALF_WORD) * WORD

    common = jnp.dot(K, K, preferred_element_type=F32)
    pairs = K * jnp.floor((common + 1.0) * 0.5)
    s_blocks = jnp.max(jnp.sum(common, axis=1))
    d_blocks = jnp.max(jnp.sum(common * K, axis=1))
    spread = jnp.dot(K, pairs, preferred_element_type=F32)
    s_pairs = jnp.max(jnp.sum(spread, axis=1))
    fits = (
        (jnp.max(jnp.sum(own, axis=0)) <= CAP)
        & (s_blocks <= S_CAP)
        & (d_blocks <= D_CAP)
        & (s_pairs <= PAIRS)
        & (jnp.max(jnp.sum(K, axis=1)) <= E_CAP)
    )
    ok_ref[0] = fits.astype(jnp.int32)
    last = lax.broadcasted_iota(jnp.int32, (WIDE - NB, LANES), 0) == OK - NB
    plan_ref[NB:WIDE, :] = jnp.where(last, fits.astype(jnp.int32), ZERO)

    kj = jnp.sum(jnp.where(jj == j, K, 0.0), axis=1, keepdims=True)
    near = lax.dot_general(K * kj, K, (((0,), (0,)), ((), ())), preferred_element_type=F32)
    wanted = jnp.where((near > 0) & (K > 0), 1.0, 0.0)
    wide = lax.broadcasted_iota(jnp.int32, (NB, LANES), 1)
    out = jnp.where(wide < NEED, NB + ZERO * WORD, NB)
    for listed, value, at in ((K, jj + cid * WORD, NEAR), (wanted, jj, NEED)):
        place = jnp.dot(listed, before, preferred_element_type=F32).astype(jnp.int32)
        place = jnp.where(listed > 0, place, -1)
        size = jnp.sum(listed, axis=1, keepdims=True).astype(jnp.int32)
        out = jnp.where(wide == at + SIZE, size, out)
        for d in range(NB):
            entry = jnp.sum(jnp.where(place == d, value, 0), axis=1, keepdims=True)
            out = jnp.where((wide == at + d) & (size > d), entry, out)
    plan_ref[:NB, :] = out
    plan_ref[:NB, :NB] = blocks


H_OUT, H_IN, H_AGAIN, H_E, H_F, H_SB, H_DB, H_EB, H_TURN = range(9)


class Part:
    def __init__(self, ref, start):
        self.ref, self.start = ref, start

    def __getitem__(self, at):
        return self.ref[self.start + at]

    def __setitem__(self, at, value):
        self.ref[self.start + at] = value


def parts_of(ref, sizes):
    return [Part(ref, sum(sizes[:n])) for n in range(len(sizes))]


BLOCK_SIZES = [8, *[2 * NS + 8] * 4]
SHORT = 160
NOTHING = PAIRS + 4
LIST_SIZES = [16, *[3 * LIST] * 2, *[SHORT] * 4, D_CAP + MANY, D_CAP + MANY, 8]


def block_kernel(plan, blocks_ref):
    head_ref, pn_ref, pt_ref, an_ref, at_ref = parts_of(blocks_ref, BLOCK_SIZES)
    ok = plan[OK, 0]

    def lines(i, carry):
        def entry(d, c):
            pn, pt = c
            word = plan[i, plan[i, NEED + d]]
            held = word & (WORD - 1)
            row = word >> 12
            flipped = (held >= NS).astype(jnp.int32)
            pn_ref[pn] = held
            pt_ref[pt] = held
            an_ref[pn] = row
            at_ref[pt] = row
            return pn + (1 - flipped), pt + flipped

        return lax.fori_loop(0, plan[i, NEED + SIZE] * ok, entry, carry)

    pn, pt = lax.fori_loop(0, NB, lines, (0, 0))
    for names, rows, n in ((pn_ref, an_ref, pn), (pt_ref, at_ref, pt)):
        for u in range(MANY - 1):
            names[n + u] = ZERO + 1
            rows[n + u] = 0
    head_ref[0] = pn
    head_ref[1] = pt


def table_kernel(plan, lists_ref, sid, did, eid):
    head_ref, sl, sr, el, er, fl, fr, ds_ref, turn_ref, fin_ref = parts_of(lists_ref, LIST_SIZES)
    r, j = here()
    ok = plan[OK, 0]

    def cid(q, k):
        return plan[q, k] & (WORD - 1)

    nj = plan[j, NEAR + SIZE] * ok

    def row(a, carry):
        m = plan[j, NEAR + a] & (WORD - 1)
        nm = plan[m, NEAR + SIZE]
        base = carry[3] * WORD

        def output(b, c):
            apart, inner_, again, count, dcount, turns = c
            k = plan[m, NEAR + b] & (WORD - 1)
            inside = cid(k, j) != ZERO
            turned = inside & (k < m)
            start = jnp.where(turned, again, jnp.where(inside, inner_, apart))
            outs = count * WORD
            outd = dcount * WORD

            def eight(g, p):
                at = g * 8
                words = [plan[m, NEAR + at + u] for u in range(8)]
                rs = [cid(w & (WORD - 1), k) for w in words]
                for u in range(8):
                    sl[p] = (words[u] >> 12) + (base + (at + u) * WORD)
                    sr[p] = rs[u] + jnp.where((p & 1) == 1, outd, outs)
                    p = p + (rs[u] != ZERO).astype(jnp.int32)
                return p

            p = lax.fori_loop(0, (nm + 7) >> 3, eight, start)
            sl[p] = ZERO + S_CAP * WORD
            sr[p] = ZERO + outd
            p = p + (p & 1)
            sid[m, k] = count
            did[m, k] = dcount
            ds_ref[dcount] = count
            turn_ref[turns] = jnp.where(turned, sid[k, m], 0) + outs
            return (
                jnp.where(inside, apart, p),
                jnp.where(inside & jnp.logical_not(turned), p, inner_),
                jnp.where(turned, p, again),
                count + 1,
                dcount + inside.astype(jnp.int32),
                turns + turned.astype(jnp.int32),
            )

        return lax.fori_loop(0, nm, output, carry)

    done = lax.fori_loop(0, nj, row, (0, LIST, 2 * LIST, 0, 0, 0))
    apart, inner_, again, count, dcount, turns = done
    for t, out in enumerate((S_CAP, D_CAP)):
        sl[2 * NOTHING + t] = ZERO + S_CAP * WORD
        sr[2 * NOTHING + t] = ZERO + out * WORD
    for u in range(MANY - 1):
        ds_ref[dcount + u] = 0
        turn_ref[turns + u] = S_CAP * WORD
    head_ref[H_OUT] = apart >> 1
    head_ref[H_IN] = (inner_ - LIST) >> 1
    head_ref[H_AGAIN] = (again - 2 * LIST) >> 1
    head_ref[H_TURN] = turns
    head_ref[H_SB] = count
    head_ref[H_DB] = dcount

    def finish(refs, pos, lz, dummy, many):
        L, R = refs
        for t in range(2 * many):
            L[pos + t] = lz
            R[pos + t] = D_CAP + dummy * WORD
        return ((pos >> 1) + many - 1) // many

    def gather(refs, pos, k, left, out, lz):
        L, R = refs

        def entry(c, p):
            m = plan[j, NEAR + c] & (WORD - 1)
            L[p] = left(m)
            R[p] = did[m, k] + out * WORD
            return p + (cid(m, k) != ZERO).astype(jnp.int32)

        p = lax.fori_loop(0, nj, entry, pos)
        L[p] = lz
        R[p] = D_CAP + out * WORD
        return p + (p & 1)

    def e_out(b, pos):
        k = plan[j, NEAR + b] & (WORD - 1)
        eid[k] = b
        return gather((el, er), pos, k, lambda m: did[j, m], b, D_CAP)

    pos = lax.fori_loop(0, nj, e_out, 0)
    head_ref[H_E] = finish((el, er), pos, D_CAP, E_CAP, UNROLL)
    head_ref[H_EB] = nj

    per = NB // 8

    def f_out(a, pos):
        i = r * per + a

        def stored(pos):
            fin_ref[a] = eid[i]
            return gather((fl, fr), pos, i, lambda k: eid[k], a, E_CAP)

        def absent(pos):
            fin_ref[a] = -1
            return pos

        return lax.cond((cid(i, j) != ZERO) & (ok != 0), stored, absent, pos)

    pos = lax.fori_loop(0, per, f_out, 0)
    head_ref[H_F] = finish((fl, fr), pos, E_CAP, per, FEW)


class Blocks:
    def __init__(self, ref):
        self.ref = ref

    def rows(self, at):
        return pl.ds(pl.multiple_of(at * BS, BS), BS)

    def __getitem__(self, at):
        return self.ref[self.rows(at), :]

    def __setitem__(self, at, value):
        self.ref[self.rows(at), :] = value


def split(x):
    hi = x.astype(BF16)
    return hi, (x - hi.astype(F32)).astype(BF16)


def compute_kernel(
    blocks_in, lists_in,
    *rest,
):
    blocks_ref, pn_ref, pt_ref, an_ref, at_ref = parts_of(blocks_in, BLOCK_SIZES)
    head_ref, sl, sr, el, er, fl, fr, ds_ref, turn_ref, fin_ref = parts_of(lists_in, LIST_SIZES)
    pieces, rest = rest[:-14], rest[-14:]
    out_ref, raw, ch, cl, sh, slo, da, dh, dl, ea, eh, elo, fa, sem = rest
    sa = Blocks(raw)
    copies = []
    row = 0
    for n, piece in enumerate(pieces):
        height = piece.shape[0]
        copies.append(pltpu.make_async_copy(piece, raw.at[pl.ds(row, height)], sem.at[n]))
        row += height
    for c in copies:
        c.start()
    zero = jnp.zeros((BS, BS), BF16)
    for hi, lo, at in ((ch, cl, ZERO), (sh, slo, S_CAP), (dh, dl, D_CAP), (eh, elo, E_CAP)):
        hi[at] = zero
        lo[at] = zero

    def clear(ref, n):
        @pl.loop(0, (n + MANY - 1) // MANY)
        def _(t):
            for u in range(MANY):
                ref[MANY * t + u] = jnp.zeros((BS, BS), F32)

    clear(da, head_ref[H_DB])
    clear(ea, head_ref[H_EB])
    clear(fa, NB // 8)
    for c in copies:
        c.wait()

    def prepare(n, names, rows, turn):
        @pl.loop(0, (n + MANY - 1) // MANY)
        def _(t):
            ids = [names[MANY * t + u] for u in range(MANY)]
            xs = []
            for u in range(MANY):
                word = rows[MANY * t + u]
                parts = [
                    raw[pl.ds(pl.multiple_of(at * SHARD, SHARD), SHARD), :] for at in (word & (HALF_WORD - 1), word >> 8)
                ]
                xs.append(split(turn(jnp.concatenate(parts, axis=0))))
            for a, (hi, lo) in zip(ids, xs):
                ch[a] = hi
                cl[a] = lo

    prepare(blocks_ref[0], pn_ref, an_ref, lambda v: v)
    prepare(blocks_ref[1], pt_ref, at_ref, lambda v: v.T)
    clear(sa, head_ref[H_SB])

    def phase(n, task, left, right, acc, many):
        lh, ll = left
        rh, rl = right

        @pl.loop(0, n)
        def _(t):
            for u in range(many):
                a0, a1, b0, b1, out = task(t * many + u)
                lhs = jnp.concatenate(
                    [
                        jnp.concatenate([lh[a0], lh[a1]], axis=1),
                        jnp.concatenate([ll[a0], ll[a1]], axis=1),
                    ],
                    axis=0,
                )
                rhs = jnp.concatenate(
                    [
                        jnp.concatenate([rh[b0], rl[b0]], axis=1),
                        jnp.concatenate([rh[b1], rl[b1]], axis=1),
                    ],
                    axis=0,
                )
                both = jnp.dot(lhs, rhs, preferred_element_type=F32)
                acc[out] = acc[out] + (both[:BS, :BS] + (both[:BS, BS:] + both[BS:, :BS]))

    low = lambda w: w & (WORD - 1)

    def plain(L, R):
        def task(t):
            r0 = R[2 * t]
            return low(L[2 * t]), low(L[2 * t + 1]), low(r0), low(R[2 * t + 1]), r0 >> 12

        return task

    def span(first, n_first, second, n_second):
        return lambda t: jnp.where(
            t < n_first, first + t, jnp.where(t < n_first + n_second, second + t - n_first, NOTHING)
        )

    def square(t):
        at = 2 * square_pair(t)
        r0 = sr[at]
        return low(sl[at]), low(sl[at + 1]), low(r0), low(sr[at + 1]), r0 >> 12

    def cube(t):
        at = 2 * cube_pair(t)
        r1 = sr[at + 1]
        return sl[at] >> 12, sl[at + 1] >> 12, low(sr[at]), low(r1), r1 >> 12

    n_out, n_in, n_again = head_ref[H_OUT], head_ref[H_IN], head_ref[H_AGAIN]
    square_pair = span(0, n_out, LIST // 2, n_in)
    cube_pair = span(LIST // 2, n_in, LIST, n_again)
    phase((n_out + n_in + UNROLL - 1) // UNROLL, square, (ch, cl), (ch, cl), sa, UNROLL)

    @pl.loop(0, (head_ref[H_TURN] + MANY - 1) // MANY)
    def _(t):
        words = [turn_ref[MANY * t + u] for u in range(MANY)]
        done = [sa[w & (WORD - 1)].T for w in words]
        for u in range(MANY):
            sa[words[u] >> 12] = done[u]

    @pl.loop(0, (head_ref[H_SB] + MANY - 1) // MANY)
    def _(t):
        done = [split(sa[MANY * t + u]) for u in range(MANY)]
        for u in range(MANY):
            sh[MANY * t + u], slo[MANY * t + u] = done[u]

    phase((n_in + n_again + UNROLL - 1) // UNROLL, cube, (sh, slo), (ch, cl), da, UNROLL)

    @pl.loop(0, (head_ref[H_DB] + MANY - 1) // MANY)
    def _(t):
        done = [split(3.0 * sa[ds_ref[MANY * t + u]] - 2.0 * da[MANY * t + u]) for u in range(MANY)]
        for u in range(MANY):
            dh[MANY * t + u], dl[MANY * t + u] = done[u]

    phase(head_ref[H_E], plain(el, er), (dh, dl), (dh, dl), ea, UNROLL)

    @pl.loop(0, head_ref[H_EB])
    def _(t):
        eh[t], elo[t] = split(ea[t])

    phase(head_ref[H_F], plain(fl, fr), (eh, elo), (dh, dl), fa, FEW)
    for a in range(out_ref.shape[0] // BS):
        at = fin_ref[a]
        value = 3.0 * ea[jnp.maximum(at, 0)] - 2.0 * fa[a]
        out_ref[a * BS : (a + 1) * BS, :] = jnp.where(at >= 0, value.T, 0.0)


def linear(x, y, z, core):
    return (((x % 2) * NY + y) * (NZ * NC) + z * NC + core) * 2 + x // 2


def send(value, step):
    pairs = [
        (linear(x, y, z, core), linear(*step(x, y, z, core)))
        for x in range(NX)
        for y in range(NY)
        for z in range(NZ)
        for core in range(NC)
    ]
    return lax.ppermute(value, ("row", "col", "layer"), pairs)


def along_z(d):
    return lambda x, y, z, core: (x, y, (z + d) % NZ, core)


def inner(d):
    return lambda x, y, z, core: ((x + d) % NX, y, z, core) if core == 0 else (x, (y + d) % NY, z, core)


def outer(d):
    return lambda x, y, z, core: (x, (y + d) % NY, z, core) if core == 0 else ((x + d) % NX, y, z, core)


def other_core(x, y, z, core):
    return x, y, z, 1 - core


def list_blocks(plan):
    smem = pl.BlockSpec(memory_space=pltpu.SMEM)
    i32 = lambda *shape: jax.ShapeDtypeStruct(shape, jnp.int32)
    return pl.pallas_call(
        block_kernel,
        out_shape=i32(sum(BLOCK_SIZES)),
        in_specs=[smem],
        out_specs=smem,
        cost_estimate=pl.CostEstimate(flops=0, bytes_accessed=6_000_000, transcendentals=0),
        name="list_blocks",
    )(plan)


def list_products(plan):
    smem = pl.BlockSpec(memory_space=pltpu.SMEM)
    i32 = lambda *shape: jax.ShapeDtypeStruct(shape, jnp.int32)
    return pl.pallas_call(
        table_kernel,
        out_shape=i32(sum(LIST_SIZES)),
        in_specs=[smem],
        out_specs=smem,
        scratch_shapes=[
            pltpu.SMEM((NB, NB), jnp.int32),
            pltpu.SMEM((NB, NB), jnp.int32),
            pltpu.SMEM((NB,), jnp.int32),
        ],
        cost_estimate=pl.CostEstimate(flops=0, bytes_accessed=20_000_000, transcendentals=0),
        name="list_products",
    )(plan)


def plan_products(pattern, *owners):
    smem = pl.BlockSpec(memory_space=pltpu.SMEM)
    vmem = pl.BlockSpec(memory_space=pltpu.VMEM)
    i32 = lambda *shape: jax.ShapeDtypeStruct(shape, jnp.int32)
    return pl.pallas_call(
        plan_kernel,
        out_shape=(i32(WIDE, LANES), i32(1)),
        in_specs=[vmem] * 4,
        out_specs=(vmem, smem),
        cost_estimate=pl.CostEstimate(flops=0, bytes_accessed=10_000_000, transcendentals=0),
        name="plan_products",
    )(pattern, *owners)


def to_chips_along_z(shard):
    lines = [[z * NC + c for z in range(NZ)] for c in range(NC)]
    copies = jnp.broadcast_to(shard, (NZ, SHARD, BS))
    return lax.all_to_all(
        copies, "col", split_axis=0, concat_axis=0, tiled=True, axis_index_groups=lines
    ).reshape(UNIT, BS)


def gather_pieces(shard, pattern, owners):
    tie = lax.optimization_barrier
    swap = lambda value: send(value, other_core)
    own = to_chips_along_z(shard)
    own, owners = tie((own, owners))
    line = [own] + [send(own, inner(d)) for d in (1, -1, 2)]
    plan, ok = plan_products(pattern, *owners)
    blocks = list_blocks(plan)
    line, blocks = tie((line, blocks))

    low, high = jnp.concatenate(line[:2], axis=0), jnp.concatenate(line[2:], axis=0)
    low, high, plan = tie((low, high, plan))
    back_low, ahead_high = send(low, outer(1)), send(high, outer(-1))
    back_high, ahead_low = send(high, outer(1)), send(low, outer(-1))
    tables = list_products(plan)
    back_low, ahead_high, tables = tie((back_low, ahead_high, tables))
    far_low, far_high = send(back_low, outer(1)), send(ahead_high, outer(-1))
    panel = jnp.concatenate([low, high], axis=0)
    panel, back_low, ahead_high, back_high, ahead_low = tie((panel, back_low, ahead_high, back_high, ahead_low))
    first = jnp.concatenate([back_low, ahead_high], axis=0)
    second = jnp.concatenate([back_high, ahead_low], axis=0)
    theirs = [swap(value) for value in (panel, first, second, far_low, far_high)]
    mine = [low, high, back_low, ahead_high, back_high, ahead_low, far_low, far_high]
    return ok, [blocks, tables], [*mine, *theirs]


def per_device(density, pattern):
    smem = pl.BlockSpec(memory_space=pltpu.SMEM)
    vmem = pl.BlockSpec(memory_space=pltpu.VMEM)

    square = jax.ShapeDtypeStruct((NB, NB), F32)
    packed, *owners = pl.pallas_call(
        pack_kernel,
        out_shape=(jax.ShapeDtypeStruct((CAP * BS, BS), F32), square, square, square),
        in_specs=[vmem, vmem],
        out_specs=[vmem] * 4,
        name="pack_blocks",
    )(pattern, density)

    rows = lax.axis_size("row")
    pieces = packed.reshape(rows, SHARD, BS)
    shard = jnp.sum(lax.all_to_all(pieces, "row", split_axis=0, concat_axis=0, tiled=True), axis=0)
    ok, tables, gathered = gather_pieces(shard, pattern, owners)

    def sparse(density, pattern, tables, gathered):
        block = lambda n, t: pltpu.VMEM((n, BS, BS), t)
        return pl.pallas_call(
            compute_kernel,
            out_shape=jax.ShapeDtypeStruct(density.shape, F32),
            in_specs=[smem] * len(tables) + [pl.BlockSpec(memory_space=pl.ANY)] * len(gathered),
            out_specs=vmem,
            scratch_shapes=[
                pltpu.VMEM((2 * RAW_HALF, BS), F32),
                block(ZERO + 2, BF16), block(ZERO + 2, BF16),
                block(S_CAP + 1, BF16), block(S_CAP + 1, BF16),
                block(D_CAP + 1, F32), block(D_CAP + 1, BF16), block(D_CAP + 1, BF16),
                block(E_CAP + 1, F32), block(E_CAP + 1, BF16), block(E_CAP + 1, BF16),
                block(NB // 8 + 1, F32),
                pltpu.SemaphoreType.DMA((len(gathered),)),
            ],
            compiler_params=pltpu.CompilerParams(vmem_limit_bytes=48 * 2**20),
            name="purify_column",
        )(*tables, *gathered)

    def dense(density, pattern, tables, gathered):
        return dense_plan(density, pattern)

    return lax.cond(ok[0] != 0, sparse, dense, density, pattern, tables, gathered)


def solution(mesh):
    return jax.shard_map(
        per_device,
        mesh=mesh,
        in_specs=(P("row", ("col", "layer")), P()),
        out_specs=P("row", ("col", "layer")),
        check_vma=False,
    )
```

```python
import jax
import jax.numpy as jnp
from jax import lax
from jax.experimental import pallas as pl
from jax.experimental.pallas import tpu as pltpu
from jax.sharding import PartitionSpec as P

BS = 128
ITERS = 2
NB = 32
CAP = 4
NS = NB * CAP
ROUNDS = 5
REPAIRS = 24
ZERO = 2 * NS
S_CAP = 104
D_CAP = 80
E_CAP = 16
PAIRS = 256
UNROLL = 8
FEW = 4
MANY = 4
LIST = 2 * PAIRS + 2 * UNROLL + 8
NZ, NC = 8, 2
NX, NY = 4, 4
SHARD = CAP * BS // 8
UNIT = NZ * SHARD
PANEL = 4 * UNIT
RAW_HALF = 4 * PANEL
WIDE = 40
WORD = 4096
HALF_WORD = 256
OK = WIDE - 1
LANES = 128
NEAR = WIDE
NEED = 2 * WIDE
SIZE = WIDE - 1
F32 = jnp.float32
BF16 = jnp.bfloat16


def panel_cols(tile, layers):
    row_count, shard_cols = tile.shape
    gathered = lax.all_gather(tile, "row", axis=0, tiled=True)
    pieces = gathered.reshape(
        gathered.shape[0] // (shard_cols * layers), layers, shard_cols, shard_cols
    )
    arranged = lax.all_to_all(pieces, "layer", split_axis=1, concat_axis=3, tiled=True)
    return arranged.reshape(-1, layers * shard_cols)


def multiply(left_tile, right_panel):
    partial_sum = jnp.dot(
        lax.all_gather(left_tile, "col", axis=1, tiled=True),
        right_panel,
        precision=lax.Precision.HIGHEST,
        preferred_element_type=jnp.float32,
    )
    return lax.psum_scatter(partial_sum, "layer", scatter_dimension=1, tiled=True)


def dense_plan(density, pattern):
    row_index = lax.axis_index("row")
    col_index = lax.axis_index("col")
    layer_index = lax.axis_index("layer")
    layers = lax.axis_size("layer")
    row_count, shard_cols = density.shape
    blocks = pattern.shape[0]
    block_line = jnp.arange(blocks, dtype=jnp.int32)
    row_ids = (row_index * row_count + jnp.arange(row_count, dtype=jnp.int32)) // BS
    col_ids = (
        (col_index * layers + layer_index) * shard_cols + jnp.arange(shard_cols, dtype=jnp.int32)
    ) // BS
    pick_rows = (row_ids[:, None] == block_line[None, :]).astype(jnp.float32)
    pick_cols = (col_ids[:, None] == block_line[None, :]).astype(jnp.float32)
    occupied = pattern.astype(jnp.float32)
    in_pattern = jnp.dot(
        jnp.dot(pick_rows, occupied, precision=lax.Precision.HIGHEST),
        pick_cols.T,
        precision=lax.Precision.HIGHEST,
    )
    current = in_pattern * density
    for iteration in range(ITERS):
        current_panel = panel_cols(current, layers)
        squared = in_pattern * multiply(current, current_panel)
        cube_term = in_pattern * multiply(current, panel_cols(squared, layers))
        current = 3.0 * squared - 2.0 * cube_term
    return current


def here():
    row = lax.axis_index("row").astype(jnp.int32)
    column = lax.axis_index("col") * lax.axis_size("layer") + lax.axis_index("layer")
    return row, column.astype(jnp.int32)


def ring_place(source, at):
    back = (at - source) & 3
    return jnp.where(back == 3, 2, jnp.where(back == 2, 3, back))


def raw_row(column, p, j, r):
    px = ring_place((column & 1) * 2 + (p >> 2), (j & 1) * 2 + (r >> 2))
    py = ring_place(p & 3, r & 3)
    core = (column >> 1) & 1
    near, far = jnp.where(core == 0, px, py), jnp.where(core == 0, py, px)
    other = jnp.where(((j >> 1) & 1) == core, 0, 1)
    high = near >> 1
    ring = 2 + jnp.where(far == 1, 2 * high, 3 - 2 * high)
    group = jnp.where(far == 0, high, jnp.where(far == 3, 6 + high, ring))
    return other * RAW_HALF + group * (PANEL // 2) + (near & 1) * UNIT + (column >> 2) * SHARD


def pack_kernel(pat_ref, tile_ref, packed_ref, own_ref, own_t_ref, rank_ref):
    r, j = here()
    K = (pat_ref[...] != 0).astype(F32)
    ii = lax.broadcasted_iota(jnp.int32, (NB, NB), 0)
    jj = lax.broadcasted_iota(jnp.int32, (NB, NB), 1)
    diag = (ii == jj).astype(F32)
    left = K * (1.0 - diag)
    own = diag
    own_t = diag
    after = (ii > jj).astype(F32)
    before = (ii < jj).astype(F32)
    for _ in range(ROUNDS):
        fc = (jnp.sum(left, axis=0, keepdims=True) <= CAP - 1).astype(F32)
        fr = (jnp.sum(left, axis=1, keepdims=True) <= CAP - 1).astype(F32)
        own = own + left * fc * ((1.0 - fr) + fr * after)
        own_t = own_t + left * fr * ((1.0 - fc) + fc * before)
        left = left * (1.0 - fc) * (1.0 - fr)
    own = own + left * after
    own_t = own_t + left * before

    number = ii * NB + jj
    number_t = jj * NB + ii

    def move(_, held):
        own, own_t = held
        load_row = jnp.sum(own, axis=0, keepdims=True)
        load_col = jnp.sum(own_t, axis=1, keepdims=True)
        source = own * (1.0 - diag) * (load_row > CAP).astype(F32)
        room = source * (load_col < CAP).astype(F32)
        onward = jnp.max(own_t * (1.0 - diag) * (load_row < CAP).astype(F32), axis=1, keepdims=True)
        through = source * onward * (load_col == CAP).astype(F32)
        none = jnp.max(room, axis=(0, 1), keepdims=True) == 0.0
        use = jnp.where(none, through, room)
        first = jnp.min(jnp.where(use > 0, number, NB * NB), axis=(0, 1), keepdims=True)
        flip = (number == first).astype(F32)
        flip_t = (number_t == first).astype(F32)
        return own - flip + flip_t, own_t - flip_t + flip

    crowded = jnp.max(jnp.sum(own, axis=0)) > CAP
    own, own_t = lax.fori_loop(0, jnp.where(crowded, REPAIRS, 0), move, (own, own_t))
    rank = jnp.dot(after, own, preferred_element_type=F32)
    own_ref[...] = own
    own_t_ref[...] = own_t
    rank_ref[...] = rank

    for s in range(CAP):
        total = jnp.zeros((BS, BS), F32)
        for a in range(tile_ref.shape[0] // BS):
            at = (ii == r * (tile_ref.shape[0] // BS) + a) & (jj == j)
            pick = at & (own > 0) & (rank == s)
            w = jnp.sum(jnp.where(pick, 1.0, 0.0), axis=(0, 1), keepdims=True)
            total = total + w * tile_ref[a * BS : (a + 1) * BS, :]
        packed_ref[s * BS : (s + 1) * BS, :] = total


def plan_kernel(
    pat_ref, own_ref, own_t_ref, rank_ref,
    plan_ref, ok_ref,
):
    r, j = here()
    K = (pat_ref[...] != 0).astype(F32)
    ii = lax.broadcasted_iota(jnp.int32, (NB, NB), 0)
    jj = lax.broadcasted_iota(jnp.int32, (NB, NB), 1)
    before = (ii < jj).astype(F32)
    own = own_ref[...]
    own_t = own_t_ref[...]
    rank = rank_ref[...]
    rank_t = jnp.dot(own_t, before, preferred_element_type=F32)
    slot = jj * CAP + rank.astype(jnp.int32)
    slot_t = ii * CAP + rank_t.astype(jnp.int32)
    cid = jnp.where(own > 0, slot, jnp.where(own_t > 0, NS + slot_t, ZERO))
    column = jnp.where(own > 0, jj, ii)
    turn = jnp.where(own > 0, rank, rank_t).astype(jnp.int32)
    first, second = [raw_row(column, 2 * turn + n, j, r) // SHARD for n in range(2)]
    blocks = cid + (first + second * HALF_WORD) * WORD

    common = jnp.dot(K, K, preferred_element_type=F32)
    pairs = K * jnp.floor((common + 1.0) * 0.5)
    s_blocks = jnp.max(jnp.sum(common, axis=1))
    d_blocks = jnp.max(jnp.sum(common * K, axis=1))
    spread = jnp.dot(K, pairs, preferred_element_type=F32)
    s_pairs = jnp.max(jnp.sum(spread, axis=1))
    fits = (
        (jnp.max(jnp.sum(own, axis=0)) <= CAP)
        & (s_blocks <= S_CAP)
        & (d_blocks <= D_CAP)
        & (s_pairs <= PAIRS)
        & (jnp.max(jnp.sum(K, axis=1)) <= E_CAP)
    )
    ok_ref[0] = fits.astype(jnp.int32)
    last = lax.broadcasted_iota(jnp.int32, (WIDE - NB, LANES), 0) == OK - NB
    plan_ref[NB:WIDE, :] = jnp.where(last, fits.astype(jnp.int32), ZERO)

    kj = jnp.sum(jnp.where(jj == j, K, 0.0), axis=1, keepdims=True)
    near = lax.dot_general(K * kj, K, (((0,), (0,)), ((), ())), preferred_element_type=F32)
    wanted = jnp.where((near > 0) & (K > 0), 1.0, 0.0)
    wide = lax.broadcasted_iota(jnp.int32, (NB, LANES), 1)
    out = jnp.where(wide < NEED, NB + ZERO * WORD, NB)
    for listed, value, at in ((K, jj + cid * WORD, NEAR), (wanted, jj, NEED)):
        place = jnp.dot(listed, before, preferred_element_type=F32).astype(jnp.int32)
        place = jnp.where(listed > 0, place, -1)
        size = jnp.sum(listed, axis=1, keepdims=True).astype(jnp.int32)
        out = jnp.where(wide == at + SIZE, size, out)
        for d in range(NB):
            entry = jnp.sum(jnp.where(place == d, value, 0), axis=1, keepdims=True)
            out = jnp.where((wide == at + d) & (size > d), entry, out)
    plan_ref[:NB, :] = out
    plan_ref[:NB, :NB] = blocks


H_OUT, H_IN, H_AGAIN, H_E, H_F, H_SB, H_DB, H_EB, H_TURN = range(9)


class Part:
    def __init__(self, ref, start):
        self.ref, self.start = ref, start

    def __getitem__(self, at):
        return self.ref[self.start + at]

    def __setitem__(self, at, value):
        self.ref[self.start + at] = value


def parts_of(ref, sizes):
    return [Part(ref, sum(sizes[:n])) for n in range(len(sizes))]


BLOCK_SIZES = [8, *[2 * NS + 8] * 4]
SHORT = 160
NOTHING = PAIRS + 4
LIST_SIZES = [16, *[3 * LIST] * 2, *[SHORT] * 4, D_CAP + MANY, D_CAP + MANY, 8]


def block_kernel(plan, blocks_ref):
    head_ref, pn_ref, pt_ref, an_ref, at_ref = parts_of(blocks_ref, BLOCK_SIZES)
    ok = plan[OK, 0]

    def lines(i, carry):
        def entry(d, c):
            pn, pt = c
            word = plan[i, plan[i, NEED + d]]
            held = word & (WORD - 1)
            row = word >> 12
            flipped = (held >= NS).astype(jnp.int32)
            pn_ref[pn] = held
            pt_ref[pt] = held
            an_ref[pn] = row
            at_ref[pt] = row
            return pn + (1 - flipped), pt + flipped

        return lax.fori_loop(0, plan[i, NEED + SIZE] * ok, entry, carry)

    pn, pt = lax.fori_loop(0, NB, lines, (0, 0))
    for names, rows, n in ((pn_ref, an_ref, pn), (pt_ref, at_ref, pt)):
        for u in range(MANY - 1):
            names[n + u] = ZERO + 1
            rows[n + u] = 0
    head_ref[0] = pn
    head_ref[1] = pt


def table_kernel(plan, lists_ref, sid, did, eid):
    head_ref, sl, sr, el, er, fl, fr, ds_ref, turn_ref, fin_ref = parts_of(lists_ref, LIST_SIZES)
    r, j = here()
    ok = plan[OK, 0]

    def cid(q, k):
        return plan[q, k] & (WORD - 1)

    nj = plan[j, NEAR + SIZE] * ok

    def row(a, carry):
        m = plan[j, NEAR + a] & (WORD - 1)
        nm = plan[m, NEAR + SIZE]
        base = carry[3] * WORD

        def output(b, c):
            apart, inner_, again, count, dcount, turns = c
            k = plan[m, NEAR + b] & (WORD - 1)
            inside = cid(k, j) != ZERO
            turned = inside & (k < m)
            start = jnp.where(turned, again, jnp.where(inside, inner_, apart))
            outs = count * WORD
            outd = dcount * WORD

            def eight(g, p):
                at = g * 8
                words = [plan[m, NEAR + at + u] for u in range(8)]
                rs = [cid(w & (WORD - 1), k) for w in words]
                for u in range(8):
                    sl[p] = (words[u] >> 12) + (base + (at + u) * WORD)
                    sr[p] = rs[u] + jnp.where((p & 1) == 1, outd, outs)
                    p = p + (rs[u] != ZERO).astype(jnp.int32)
                return p

            p = lax.fori_loop(0, (nm + 7) >> 3, eight, start)
            sl[p] = ZERO + S_CAP * WORD
            sr[p] = ZERO + outd
            p = p + (p & 1)
            sid[m, k] = count
            did[m, k] = dcount
            ds_ref[dcount] = count
            turn_ref[turns] = jnp.where(turned, sid[k, m], 0) + outs
            return (
                jnp.where(inside, apart, p),
                jnp.where(inside & jnp.logical_not(turned), p, inner_),
                jnp.where(turned, p, again),
                count + 1,
                dcount + inside.astype(jnp.int32),
                turns + turned.astype(jnp.int32),
            )

        return lax.fori_loop(0, nm, output, carry)

    done = lax.fori_loop(0, nj, row, (0, LIST, 2 * LIST, 0, 0, 0))
    apart, inner_, again, count, dcount, turns = done
    for t, out in enumerate((S_CAP, D_CAP)):
        sl[2 * NOTHING + t] = ZERO + S_CAP * WORD
        sr[2 * NOTHING + t] = ZERO + out * WORD
    for u in range(MANY - 1):
        ds_ref[dcount + u] = 0
        turn_ref[turns + u] = S_CAP * WORD
    head_ref[H_OUT] = apart >> 1
    head_ref[H_IN] = (inner_ - LIST) >> 1
    head_ref[H_AGAIN] = (again - 2 * LIST) >> 1
    head_ref[H_TURN] = turns
    head_ref[H_SB] = count
    head_ref[H_DB] = dcount

    def finish(refs, pos, lz, dummy, many):
        L, R = refs
        for t in range(2 * many):
            L[pos + t] = lz
            R[pos + t] = D_CAP + dummy * WORD
        return ((pos >> 1) + many - 1) // many

    def gather(refs, pos, k, left, out, lz):
        L, R = refs

        def entry(c, p):
            m = plan[j, NEAR + c] & (WORD - 1)
            L[p] = left(m)
            R[p] = did[m, k] + out * WORD
            return p + (cid(m, k) != ZERO).astype(jnp.int32)

        p = lax.fori_loop(0, nj, entry, pos)
        L[p] = lz
        R[p] = D_CAP + out * WORD
        return p + (p & 1)

    def e_out(b, pos):
        k = plan[j, NEAR + b] & (WORD - 1)
        eid[k] = b
        return gather((el, er), pos, k, lambda m: did[j, m], b, D_CAP)

    pos = lax.fori_loop(0, nj, e_out, 0)
    head_ref[H_E] = finish((el, er), pos, D_CAP, E_CAP, UNROLL)
    head_ref[H_EB] = nj

    per = NB // 8

    def f_out(a, pos):
        i = r * per + a

        def stored(pos):
            fin_ref[a] = eid[i]
            return gather((fl, fr), pos, i, lambda k: eid[k], a, E_CAP)

        def absent(pos):
            fin_ref[a] = -1
            return pos

        return lax.cond((cid(i, j) != ZERO) & (ok != 0), stored, absent, pos)

    pos = lax.fori_loop(0, per, f_out, 0)
    head_ref[H_F] = finish((fl, fr), pos, E_CAP, per, FEW)


class Blocks:
    def __init__(self, ref):
        self.ref = ref

    def rows(self, at):
        return pl.ds(pl.multiple_of(at * BS, BS), BS)

    def __getitem__(self, at):
        return self.ref[self.rows(at), :]

    def __setitem__(self, at, value):
        self.ref[self.rows(at), :] = value


def split(x):
    hi = x.astype(BF16)
    return hi, (x - hi.astype(F32)).astype(BF16)


def compute_kernel(
    blocks_in, lists_in,
    *rest,
):
    blocks_ref, pn_ref, pt_ref, an_ref, at_ref = parts_of(blocks_in, BLOCK_SIZES)
    head_ref, sl, sr, el, er, fl, fr, ds_ref, turn_ref, fin_ref = parts_of(lists_in, LIST_SIZES)
    pieces, rest = rest[:-14], rest[-14:]
    out_ref, raw, ch, cl, sh, slo, da, dh, dl, ea, eh, elo, fa, sem = rest
    sa = Blocks(raw)
    copies = []
    row = 0
    for n, piece in enumerate(pieces):
        height = piece.shape[0]
        copies.append(pltpu.make_async_copy(piece, raw.at[pl.ds(row, height)], sem.at[n]))
        row += height
    for c in copies:
        c.start()
    zero = jnp.zeros((BS, BS), BF16)
    for hi, lo, at in ((ch, cl, ZERO), (sh, slo, S_CAP), (dh, dl, D_CAP), (eh, elo, E_CAP)):
        hi[at] = zero
        lo[at] = zero

    def clear(ref, n):
        @pl.loop(0, (n + MANY - 1) // MANY)
        def _(t):
            for u in range(MANY):
                ref[MANY * t + u] = jnp.zeros((BS, BS), F32)

    clear(da, head_ref[H_DB])
    clear(ea, head_ref[H_EB])
    clear(fa, NB // 8)
    for c in copies:
        c.wait()

    def prepare(n, names, rows, turn):
        @pl.loop(0, (n + MANY - 1) // MANY)
        def _(t):
            ids = [names[MANY * t + u] for u in range(MANY)]
            xs = []
            for u in range(MANY):
                word = rows[MANY * t + u]
                parts = [
                    raw[pl.ds(pl.multiple_of(at * SHARD, SHARD), SHARD), :] for at in (word & (HALF_WORD - 1), word >> 8)
                ]
                xs.append(split(turn(jnp.concatenate(parts, axis=0))))
            for a, (hi, lo) in zip(ids, xs):
                ch[a] = hi
                cl[a] = lo

    prepare(blocks_ref[0], pn_ref, an_ref, lambda v: v)
    prepare(blocks_ref[1], pt_ref, at_ref, lambda v: v.T)
    clear(sa, head_ref[H_SB])

    def phase(n, task, left, right, acc, many):
        lh, ll = left
        rh, rl = right

        @pl.loop(0, n)
        def _(t):
            for u in range(many):
                a0, a1, b0, b1, out = task(t * many + u)
                lhs = jnp.concatenate(
                    [
                        jnp.concatenate([lh[a0], lh[a1]], axis=1),
                        jnp.concatenate([ll[a0], ll[a1]], axis=1),
                    ],
                    axis=0,
                )
                rhs = jnp.concatenate(
                    [
                        jnp.concatenate([rh[b0], rl[b0]], axis=1),
                        jnp.concatenate([rh[b1], rl[b1]], axis=1),
                    ],
                    axis=0,
                )
                both = jnp.dot(lhs, rhs, preferred_element_type=F32)
                acc[out] = acc[out] + (both[:BS, :BS] + (both[:BS, BS:] + both[BS:, :BS]))

    low = lambda w: w & (WORD - 1)

    def plain(L, R):
        def task(t):
            r0 = R[2 * t]
            return low(L[2 * t]), low(L[2 * t + 1]), low(r0), low(R[2 * t + 1]), r0 >> 12

        return task

    def span(first, n_first, second, n_second):
        return lambda t: jnp.where(
            t < n_first, first + t, jnp.where(t < n_first + n_second, second + t - n_first, NOTHING)
        )

    def square(t):
        at = 2 * square_pair(t)
        r0 = sr[at]
        return low(sl[at]), low(sl[at + 1]), low(r0), low(sr[at + 1]), r0 >> 12

    def cube(t):
        at = 2 * cube_pair(t)
        r1 = sr[at + 1]
        return sl[at] >> 12, sl[at + 1] >> 12, low(sr[at]), low(r1), r1 >> 12

    n_out, n_in, n_again = head_ref[H_OUT], head_ref[H_IN], head_ref[H_AGAIN]
    square_pair = span(0, n_out, LIST // 2, n_in)
    cube_pair = span(LIST // 2, n_in, LIST, n_again)
    phase((n_out + n_in + UNROLL - 1) // UNROLL, square, (ch, cl), (ch, cl), sa, UNROLL)

    @pl.loop(0, (head_ref[H_TURN] + MANY - 1) // MANY)
    def _(t):
        words = [turn_ref[MANY * t + u] for u in range(MANY)]
        done = [sa[w & (WORD - 1)].T for w in words]
        for u in range(MANY):
            sa[words[u] >> 12] = done[u]

    @pl.loop(0, (head_ref[H_SB] + MANY - 1) // MANY)
    def _(t):
        done = [split(sa[MANY * t + u]) for u in range(MANY)]
        for u in range(MANY):
            sh[MANY * t + u], slo[MANY * t + u] = done[u]

    phase((n_in + n_again + UNROLL - 1) // UNROLL, cube, (sh, slo), (ch, cl), da, UNROLL)

    @pl.loop(0, (head_ref[H_DB] + MANY - 1) // MANY)
    def _(t):
        done = [split(3.0 * sa[ds_ref[MANY * t + u]] - 2.0 * da[MANY * t + u]) for u in range(MANY)]
        for u in range(MANY):
            dh[MANY * t + u], dl[MANY * t + u] = done[u]

    phase(head_ref[H_E], plain(el, er), (dh, dl), (dh, dl), ea, UNROLL)

    @pl.loop(0, head_ref[H_EB])
    def _(t):
        eh[t], elo[t] = split(ea[t])

    phase(head_ref[H_F], plain(fl, fr), (eh, elo), (dh, dl), fa, FEW)
    for a in range(out_ref.shape[0] // BS):
        at = fin_ref[a]
        value = 3.0 * ea[jnp.maximum(at, 0)] - 2.0 * fa[a]
        out_ref[a * BS : (a + 1) * BS, :] = jnp.where(at >= 0, value.T, 0.0)


def linear(x, y, z, core):
    return (((x % 2) * NY + y) * (NZ * NC) + z * NC + core) * 2 + x // 2


def send(value, step):
    pairs = [
        (linear(x, y, z, core), linear(*step(x, y, z, core)))
        for x in range(NX)
        for y in range(NY)
        for z in range(NZ)
        for core in range(NC)
    ]
    return lax.ppermute(value, ("row", "col", "layer"), pairs)


def along_z(d):
    return lambda x, y, z, core: (x, y, (z + d) % NZ, core)


def inner(d):
    return lambda x, y, z, core: ((x + d) % NX, y, z, core) if core == 0 else (x, (y + d) % NY, z, core)


def outer(d):
    return lambda x, y, z, core: (x, (y + d) % NY, z, core) if core == 0 else ((x + d) % NX, y, z, core)


def other_core(x, y, z, core):
    return x, y, z, 1 - core


def list_blocks(plan):
    smem = pl.BlockSpec(memory_space=pltpu.SMEM)
    i32 = lambda *shape: jax.ShapeDtypeStruct(shape, jnp.int32)
    return pl.pallas_call(
        block_kernel,
        out_shape=i32(sum(BLOCK_SIZES)),
        in_specs=[smem],
        out_specs=smem,
        cost_estimate=pl.CostEstimate(flops=0, bytes_accessed=6_000_000, transcendentals=0),
        name="list_blocks",
    )(plan)


def list_products(plan):
    smem = pl.BlockSpec(memory_space=pltpu.SMEM)
    i32 = lambda *shape: jax.ShapeDtypeStruct(shape, jnp.int32)
    return pl.pallas_call(
        table_kernel,
        out_shape=i32(sum(LIST_SIZES)),
        in_specs=[smem],
        out_specs=smem,
        scratch_shapes=[
            pltpu.SMEM((NB, NB), jnp.int32),
            pltpu.SMEM((NB, NB), jnp.int32),
            pltpu.SMEM((NB,), jnp.int32),
        ],
        cost_estimate=pl.CostEstimate(flops=0, bytes_accessed=20_000_000, transcendentals=0),
        name="list_products",
    )(plan)


def plan_products(pattern, *owners):
    smem = pl.BlockSpec(memory_space=pltpu.SMEM)
    vmem = pl.BlockSpec(memory_space=pltpu.VMEM)
    i32 = lambda *shape: jax.ShapeDtypeStruct(shape, jnp.int32)
    return pl.pallas_call(
        plan_kernel,
        out_shape=(i32(WIDE, LANES), i32(1)),
        in_specs=[vmem] * 4,
        out_specs=(vmem, smem),
        cost_estimate=pl.CostEstimate(flops=0, bytes_accessed=10_000_000, transcendentals=0),
        name="plan_products",
    )(pattern, *owners)


def to_chips_along_z(shard):
    lines = [[z * NC + c for z in range(NZ)] for c in range(NC)]
    copies = jnp.broadcast_to(shard, (NZ, SHARD, BS))
    return lax.all_to_all(
        copies, "col", split_axis=0, concat_axis=0, tiled=True, axis_index_groups=lines
    ).reshape(UNIT, BS)


def gather_pieces(shard, pattern, owners):
    tie = lax.optimization_barrier
    swap = lambda value: send(value, other_core)
    own = to_chips_along_z(shard)
    own, owners = tie((own, owners))
    line = [own] + [send(own, inner(d)) for d in (1, -1, 2)]
    plan, ok = plan_products(pattern, *owners)
    blocks = list_blocks(plan)
    line, blocks = tie((line, blocks))

    low, high = jnp.concatenate(line[:2], axis=0), jnp.concatenate(line[2:], axis=0)
    low, high, plan = tie((low, high, plan))
    back_low, ahead_high = send(low, outer(1)), send(high, outer(-1))
    back_high, ahead_low = send(high, outer(1)), send(low, outer(-1))
    tables = list_products(plan)
    back_low, ahead_high, tables = tie((back_low, ahead_high, tables))
    far_low, far_high = send(back_low, outer(1)), send(ahead_high, outer(-1))
    panel = jnp.concatenate([low, high], axis=0)
    panel, back_low, ahead_high, back_high, ahead_low = tie((panel, back_low, ahead_high, back_high, ahead_low))
    first = jnp.concatenate([back_low, ahead_high], axis=0)
    second = jnp.concatenate([back_high, ahead_low], axis=0)
    far_low, far_high = tie((far_low, far_high))
    theirs = [swap(value) for value in (panel, first, second, far_low, far_high)]
    mine = [low, high, back_low, ahead_high, back_high, ahead_low, far_low, far_high]
    return ok, [blocks, tables], [*mine, *theirs]


def per_device(density, pattern):
    smem = pl.BlockSpec(memory_space=pltpu.SMEM)
    vmem = pl.BlockSpec(memory_space=pltpu.VMEM)

    square = jax.ShapeDtypeStruct((NB, NB), F32)
    packed, *owners = pl.pallas_call(
        pack_kernel,
        out_shape=(jax.ShapeDtypeStruct((CAP * BS, BS), F32), square, square, square),
        in_specs=[vmem, vmem],
        out_specs=[vmem] * 4,
        name="pack_blocks",
    )(pattern, density)

    rows = lax.axis_size("row")
    pieces = packed.reshape(rows, SHARD, BS)
    shard = jnp.sum(lax.all_to_all(pieces, "row", split_axis=0, concat_axis=0, tiled=True), axis=0)
    ok, tables, gathered = gather_pieces(shard, pattern, owners)

    def sparse(density, pattern, tables, gathered):
        block = lambda n, t: pltpu.VMEM((n, BS, BS), t)
        return pl.pallas_call(
            compute_kernel,
            out_shape=jax.ShapeDtypeStruct(density.shape, F32),
            in_specs=[smem] * len(tables) + [pl.BlockSpec(memory_space=pl.ANY)] * len(gathered),
            out_specs=vmem,
            scratch_shapes=[
                pltpu.VMEM((2 * RAW_HALF, BS), F32),
                block(ZERO + 2, BF16), block(ZERO + 2, BF16),
                block(S_CAP + 1, BF16), block(S_CAP + 1, BF16),
                block(D_CAP + 1, F32), block(D_CAP + 1, BF16), block(D_CAP + 1, BF16),
                block(E_CAP + 1, F32), block(E_CAP + 1, BF16), block(E_CAP + 1, BF16),
                block(NB // 8 + 1, F32),
                pltpu.SemaphoreType.DMA((len(gathered),)),
            ],
            compiler_params=pltpu.CompilerParams(vmem_limit_bytes=48 * 2**20),
            name="purify_column",
        )(*tables, *gathered)

    def dense(density, pattern, tables, gathered):
        return dense_plan(density, pattern)

    return lax.cond(ok[0] != 0, sparse, dense, density, pattern, tables, gathered)


def solution(mesh):
    return jax.shard_map(
        per_device,
        mesh=mesh,
        in_specs=(P("row", ("col", "layer")), P()),
        out_specs=P("row", ("col", "layer")),
        check_vma=False,
    )
```

```python
import jax
import jax.numpy as jnp
from jax import lax
from jax.experimental import pallas as pl
from jax.experimental.pallas import tpu as pltpu
from jax.sharding import PartitionSpec as P

BS = 128
ITERS = 2
NB = 32
CAP = 4
NS = NB * CAP
ROUNDS = 5
REPAIRS = 24
ZERO = 2 * NS
S_CAP = 104
D_CAP = 80
E_CAP = 16
PAIRS = 256
UNROLL = 8
FEW = 4
MANY = 4
LIST = 2 * PAIRS + 2 * UNROLL + 8
NZ, NC = 8, 2
NX, NY = 4, 4
SHARD = CAP * BS // 8
UNIT = NZ * SHARD
PANEL = 4 * UNIT
RAW_HALF = 4 * PANEL
WIDE = 40
WORD = 4096
HALF_WORD = 256
OK = WIDE - 1
LANES = 128
NEAR = WIDE
NEED = 2 * WIDE
SIZE = WIDE - 1
F32 = jnp.float32
BF16 = jnp.bfloat16


def panel_cols(tile, layers):
    row_count, shard_cols = tile.shape
    gathered = lax.all_gather(tile, "row", axis=0, tiled=True)
    pieces = gathered.reshape(
        gathered.shape[0] // (shard_cols * layers), layers, shard_cols, shard_cols
    )
    arranged = lax.all_to_all(pieces, "layer", split_axis=1, concat_axis=3, tiled=True)
    return arranged.reshape(-1, layers * shard_cols)


def multiply(left_tile, right_panel):
    partial_sum = jnp.dot(
        lax.all_gather(left_tile, "col", axis=1, tiled=True),
        right_panel,
        precision=lax.Precision.HIGHEST,
        preferred_element_type=jnp.float32,
    )
    return lax.psum_scatter(partial_sum, "layer", scatter_dimension=1, tiled=True)


def dense_plan(density, pattern):
    row_index = lax.axis_index("row")
    col_index = lax.axis_index("col")
    layer_index = lax.axis_index("layer")
    layers = lax.axis_size("layer")
    row_count, shard_cols = density.shape
    blocks = pattern.shape[0]
    block_line = jnp.arange(blocks, dtype=jnp.int32)
    row_ids = (row_index * row_count + jnp.arange(row_count, dtype=jnp.int32)) // BS
    col_ids = (
        (col_index * layers + layer_index) * shard_cols + jnp.arange(shard_cols, dtype=jnp.int32)
    ) // BS
    pick_rows = (row_ids[:, None] == block_line[None, :]).astype(jnp.float32)
    pick_cols = (col_ids[:, None] == block_line[None, :]).astype(jnp.float32)
    occupied = pattern.astype(jnp.float32)
    in_pattern = jnp.dot(
        jnp.dot(pick_rows, occupied, precision=lax.Precision.HIGHEST),
        pick_cols.T,
        precision=lax.Precision.HIGHEST,
    )
    current = in_pattern * density
    for iteration in range(ITERS):
        current_panel = panel_cols(current, layers)
        squared = in_pattern * multiply(current, current_panel)
        cube_term = in_pattern * multiply(current, panel_cols(squared, layers))
        current = 3.0 * squared - 2.0 * cube_term
    return current


def here():
    row = lax.axis_index("row").astype(jnp.int32)
    column = lax.axis_index("col") * lax.axis_size("layer") + lax.axis_index("layer")
    return row, column.astype(jnp.int32)


def ring_place(source, at):
    back = (at - source) & 3
    return jnp.where(back == 3, 2, jnp.where(back == 2, 3, back))


def raw_row(column, p, j, r):
    px = ring_place((column & 1) * 2 + (p >> 2), (j & 1) * 2 + (r >> 2))
    py = ring_place(p & 3, r & 3)
    core = (column >> 1) & 1
    near, far = jnp.where(core == 0, px, py), jnp.where(core == 0, py, px)
    other = jnp.where(((j >> 1) & 1) == core, 0, 1)
    high = near >> 1
    ring = 2 + jnp.where(far == 1, 2 * high, 3 - 2 * high)
    group = jnp.where(far == 0, high, jnp.where(far == 3, 6 + high, ring))
    return other * RAW_HALF + group * (PANEL // 2) + (near & 1) * UNIT + (column >> 2) * SHARD


def pack_kernel(pat_ref, tile_ref, packed_ref, own_ref, own_t_ref, rank_ref):
    r, j = here()
    K = (pat_ref[...] != 0).astype(F32)
    ii = lax.broadcasted_iota(jnp.int32, (NB, NB), 0)
    jj = lax.broadcasted_iota(jnp.int32, (NB, NB), 1)
    diag = (ii == jj).astype(F32)
    left = K * (1.0 - diag)
    own = diag
    own_t = diag
    after = (ii > jj).astype(F32)
    before = (ii < jj).astype(F32)
    for _ in range(ROUNDS):
        fc = (jnp.sum(left, axis=0, keepdims=True) <= CAP - 1).astype(F32)
        fr = (jnp.sum(left, axis=1, keepdims=True) <= CAP - 1).astype(F32)
        own = own + left * fc * ((1.0 - fr) + fr * after)
        own_t = own_t + left * fr * ((1.0 - fc) + fc * before)
        left = left * (1.0 - fc) * (1.0 - fr)
    own = own + left * after
    own_t = own_t + left * before

    number = ii * NB + jj
    number_t = jj * NB + ii

    def move(_, held):
        own, own_t = held
        load_row = jnp.sum(own, axis=0, keepdims=True)
        load_col = jnp.sum(own_t, axis=1, keepdims=True)
        source = own * (1.0 - diag) * (load_row > CAP).astype(F32)
        room = source * (load_col < CAP).astype(F32)
        onward = jnp.max(own_t * (1.0 - diag) * (load_row < CAP).astype(F32), axis=1, keepdims=True)
        through = source * onward * (load_col == CAP).astype(F32)
        none = jnp.max(room, axis=(0, 1), keepdims=True) == 0.0
        use = jnp.where(none, through, room)
        first = jnp.min(jnp.where(use > 0, number, NB * NB), axis=(0, 1), keepdims=True)
        flip = (number == first).astype(F32)
        flip_t = (number_t == first).astype(F32)
        return own - flip + flip_t, own_t - flip_t + flip

    crowded = jnp.max(jnp.sum(own, axis=0)) > CAP
    own, own_t = lax.fori_loop(0, jnp.where(crowded, REPAIRS, 0), move, (own, own_t))
    rank = jnp.dot(after, own, preferred_element_type=F32)
    own_ref[...] = own
    own_t_ref[...] = own_t
    rank_ref[...] = rank

    for s in range(CAP):
        total = jnp.zeros((BS, BS), F32)
        for a in range(tile_ref.shape[0] // BS):
            at = (ii == r * (tile_ref.shape[0] // BS) + a) & (jj == j)
            pick = at & (own > 0) & (rank == s)
            w = jnp.sum(jnp.where(pick, 1.0, 0.0), axis=(0, 1), keepdims=True)
            total = total + w * tile_ref[a * BS : (a + 1) * BS, :]
        packed_ref[s * BS : (s + 1) * BS, :] = total


def plan_kernel(
    pat_ref, own_ref, own_t_ref, rank_ref,
    plan_ref, ok_ref,
):
    r, j = here()
    K = (pat_ref[...] != 0).astype(F32)
    ii = lax.broadcasted_iota(jnp.int32, (NB, NB), 0)
    jj = lax.broadcasted_iota(jnp.int32, (NB, NB), 1)
    before = (ii < jj).astype(F32)
    own = own_ref[...]
    own_t = own_t_ref[...]
    rank = rank_ref[...]
    rank_t = jnp.dot(own_t, before, preferred_element_type=F32)
    slot = jj * CAP + rank.astype(jnp.int32)
    slot_t = ii * CAP + rank_t.astype(jnp.int32)
    cid = jnp.where(own > 0, slot, jnp.where(own_t > 0, NS + slot_t, ZERO))
    column = jnp.where(own > 0, jj, ii)
    turn = jnp.where(own > 0, rank, rank_t).astype(jnp.int32)
    first, second = [raw_row(column, 2 * turn + n, j, r) // SHARD for n in range(2)]
    blocks = cid + (first + second * HALF_WORD) * WORD

    common = jnp.dot(K, K, preferred_element_type=F32)
    pairs = K * jnp.floor((common + 1.0) * 0.5)
    s_blocks = jnp.max(jnp.sum(common, axis=1))
    d_blocks = jnp.max(jnp.sum(common * K, axis=1))
    spread = jnp.dot(K, pairs, preferred_element_type=F32)
    s_pairs = jnp.max(jnp.sum(spread, axis=1))
    fits = (
        (jnp.max(jnp.sum(own, axis=0)) <= CAP)
        & (s_blocks <= S_CAP)
        & (d_blocks <= D_CAP - MANY)
        & (s_pairs <= PAIRS)
        & (jnp.max(jnp.sum(K, axis=1)) <= E_CAP)
    )
    ok_ref[0] = fits.astype(jnp.int32)
    last = lax.broadcasted_iota(jnp.int32, (WIDE - NB, LANES), 0) == OK - NB
    plan_ref[NB:WIDE, :] = jnp.where(last, fits.astype(jnp.int32), ZERO)

    kj = jnp.sum(jnp.where(jj == j, K, 0.0), axis=1, keepdims=True)
    near = lax.dot_general(K * kj, K, (((0,), (0,)), ((), ())), preferred_element_type=F32)
    wanted = jnp.where((near > 0) & (K > 0), 1.0, 0.0)
    wide = lax.broadcasted_iota(jnp.int32, (NB, LANES), 1)
    out = jnp.where(wide < NEED, NB + ZERO * WORD, NB)
    for listed, value, at in ((K, jj + cid * WORD, NEAR), (wanted, jj, NEED)):
        place = jnp.dot(listed, before, preferred_element_type=F32).astype(jnp.int32)
        place = jnp.where(listed > 0, place, -1)
        size = jnp.sum(listed, axis=1, keepdims=True).astype(jnp.int32)
        out = jnp.where(wide == at + SIZE, size, out)
        for d in range(NB):
            entry = jnp.sum(jnp.where(place == d, value, 0), axis=1, keepdims=True)
            out = jnp.where((wide == at + d) & (size > d), entry, out)
    plan_ref[:NB, :] = out
    plan_ref[:NB, :NB] = blocks


H_OUT, H_IN, H_AGAIN, H_E, H_F, H_SB, H_DB, H_EB, H_TURN = range(9)


class Part:
    def __init__(self, ref, start):
        self.ref, self.start = ref, start

    def __getitem__(self, at):
        return self.ref[self.start + at]

    def __setitem__(self, at, value):
        self.ref[self.start + at] = value


def parts_of(ref, sizes):
    return [Part(ref, sum(sizes[:n])) for n in range(len(sizes))]


BLOCK_SIZES = [8, *[2 * NS + 8] * 4]
SHORT = 160
NOTHING = PAIRS + 4
FIRST_SIZES = [16, *[3 * LIST] * 2, D_CAP + MANY, D_CAP + MANY, NB * NB, NB * NB]
LIST_SIZES = [16, *[3 * LIST] * 2, D_CAP + MANY, D_CAP + MANY, *[SHORT] * 4, 8]


def block_kernel(plan, blocks_ref):
    head_ref, pn_ref, pt_ref, an_ref, at_ref = parts_of(blocks_ref, BLOCK_SIZES)
    ok = plan[OK, 0]

    def lines(i, carry):
        def entry(d, c):
            pn, pt = c
            word = plan[i, plan[i, NEED + d]]
            held = word & (WORD - 1)
            row = word >> 12
            flipped = (held >= NS).astype(jnp.int32)
            pn_ref[pn] = held
            pt_ref[pt] = held
            an_ref[pn] = row
            at_ref[pt] = row
            return pn + (1 - flipped), pt + flipped

        return lax.fori_loop(0, plan[i, NEED + SIZE] * ok, entry, carry)

    pn, pt = lax.fori_loop(0, NB, lines, (0, 0))
    for names, rows, n in ((pn_ref, an_ref, pn), (pt_ref, at_ref, pt)):
        for u in range(MANY - 1):
            names[n + u] = ZERO + 1
            rows[n + u] = 0
    head_ref[0] = pn
    head_ref[1] = pt


def list_rows(plan, j, rows, parts, sid, did, earlier, begin):
    head_ref, sl, sr, ds_ref, turn_ref = parts

    def cid(q, k):
        return plan[q, k] & (WORD - 1)

    def row(a, carry):
        m = plan[j, NEAR + a] & (WORD - 1)
        nm = plan[m, NEAR + SIZE]
        base = carry[3] * WORD

        def output(b, c):
            apart, inner_, again, count, dcount, turns = c
            k = plan[m, NEAR + b] & (WORD - 1)
            inside = cid(k, j) != ZERO
            turned = inside & (k < m)
            start = jnp.where(turned, again, jnp.where(inside, inner_, apart))
            outs = count * WORD
            outd = dcount * WORD

            def eight(g, p):
                at = g * 8
                words = [plan[m, NEAR + at + u] for u in range(8)]
                rs = [cid(w & (WORD - 1), k) for w in words]
                for u in range(8):
                    sl[p] = (words[u] >> 12) + (base + (at + u) * WORD)
                    sr[p] = rs[u] + jnp.where((p & 1) == 1, outd, outs)
                    p = p + (rs[u] != ZERO).astype(jnp.int32)
                return p

            p = lax.fori_loop(0, (nm + 7) >> 3, eight, start)
            sl[p] = ZERO + S_CAP * WORD
            sr[p] = ZERO + outd
            p = p + (p & 1)
            sid[m * NB + k] = count
            did[m * NB + k] = dcount
            ds_ref[dcount - begin[1]] = count
            turn_ref[turns] = jnp.where(turned, earlier(k * NB + m, k), 0) + outs
            return (
                jnp.where(inside, apart, p),
                jnp.where(inside & jnp.logical_not(turned), p, inner_),
                jnp.where(turned, p, again),
                count + 1,
                dcount + inside.astype(jnp.int32),
                turns + turned.astype(jnp.int32),
            )

        return lax.fori_loop(0, nm, output, carry)

    done = lax.fori_loop(*rows, row, (0, LIST, 2 * LIST, *begin, 0))
    apart, inner_, again, count, dcount, turns = done
    for t, out in enumerate((S_CAP, D_CAP)):
        sl[2 * NOTHING + t] = ZERO + S_CAP * WORD
        sr[2 * NOTHING + t] = ZERO + out * WORD
    for u in range(MANY - 1):
        ds_ref[dcount - begin[1] + u] = 0
        turn_ref[turns + u] = S_CAP * WORD
    head_ref[H_OUT] = apart >> 1
    head_ref[H_IN] = (inner_ - LIST) >> 1
    head_ref[H_AGAIN] = (again - 2 * LIST) >> 1
    head_ref[H_TURN] = turns
    head_ref[H_SB] = count
    head_ref[H_DB] = dcount


def first_kernel(plan, first_ref):
    *parts, sid, did = parts_of(first_ref, FIRST_SIZES)
    _, j = here()
    nj = plan[j, NEAR + SIZE] * plan[OK, 0]
    list_rows(plan, j, (0, nj >> 1), parts, sid, did, lambda at, k: sid[at], (0, 0))


def second_kernel(plan, first_ref, lists_ref, sid, did_late, eid):
    first_head, _, _, _, _, sid_early, did_early = parts_of(first_ref, FIRST_SIZES)
    *parts, el, er, fl, fr, fin_ref = parts_of(lists_ref, LIST_SIZES)
    head_ref = parts[0]
    r, j = here()
    ok = plan[OK, 0]
    nj = plan[j, NEAR + SIZE] * ok
    border = plan[j, NEAR + (nj >> 1)] & (WORD - 1)
    earlier = lambda at, k: jnp.where(k < border, sid_early[at], sid[at])
    carry = (first_head[H_SB], first_head[H_DB])
    list_rows(plan, j, (nj >> 1, nj), parts, sid, did_late, earlier, carry)

    def cid(q, k):
        return plan[q, k] & (WORD - 1)

    def did(m, k):
        at = m * NB + k
        return jnp.where(m < border, did_early[at], did_late[at])

    def finish(refs, pos, lz, dummy, many):
        L, R = refs
        for t in range(2 * many):
            L[pos + t] = lz
            R[pos + t] = D_CAP + dummy * WORD
        return ((pos >> 1) + many - 1) // many

    def gather(refs, pos, k, left, out, lz):
        L, R = refs

        def entry(c, p):
            m = plan[j, NEAR + c] & (WORD - 1)
            L[p] = left(m)
            R[p] = did(m, k) + out * WORD
            return p + (cid(m, k) != ZERO).astype(jnp.int32)

        p = lax.fori_loop(0, nj, entry, pos)
        L[p] = lz
        R[p] = D_CAP + out * WORD
        return p + (p & 1)

    def e_out(b, pos):
        k = plan[j, NEAR + b] & (WORD - 1)
        eid[k] = b
        return gather((el, er), pos, k, lambda m: did(j, m), b, D_CAP)

    pos = lax.fori_loop(0, nj, e_out, 0)
    head_ref[H_E] = finish((el, er), pos, D_CAP, E_CAP, UNROLL)
    head_ref[H_EB] = nj

    per = NB // 8

    def f_out(a, pos):
        i = r * per + a

        def stored(pos):
            fin_ref[a] = eid[i]
            return gather((fl, fr), pos, i, lambda k: eid[k], a, E_CAP)

        def absent(pos):
            fin_ref[a] = -1
            return pos

        return lax.cond((cid(i, j) != ZERO) & (ok != 0), stored, absent, pos)

    pos = lax.fori_loop(0, per, f_out, 0)
    head_ref[H_F] = finish((fl, fr), pos, E_CAP, per, FEW)


class Blocks:
    def __init__(self, ref):
        self.ref = ref

    def rows(self, at):
        return pl.ds(pl.multiple_of(at * BS, BS), BS)

    def __getitem__(self, at):
        return self.ref[self.rows(at), :]

    def __setitem__(self, at, value):
        self.ref[self.rows(at), :] = value


def split(x):
    hi = x.astype(BF16)
    return hi, (x - hi.astype(F32)).astype(BF16)


def compute_kernel(
    blocks_in, first_in, lists_in,
    *rest,
):
    blocks_ref, pn_ref, pt_ref, an_ref, at_ref = parts_of(blocks_in, BLOCK_SIZES)
    *first_half, _, _ = parts_of(first_in, FIRST_SIZES)
    *second_half, el, er, fl, fr, fin_ref = parts_of(lists_in, LIST_SIZES)
    listed = first_half, second_half
    head_ref = second_half[0]
    pieces, rest = rest[:-14], rest[-14:]
    out_ref, raw, ch, cl, sh, slo, da, dh, dl, ea, eh, elo, fa, sem = rest
    sa = Blocks(raw)
    copies = []
    row = 0
    for n, piece in enumerate(pieces):
        height = piece.shape[0]
        copies.append(pltpu.make_async_copy(piece, raw.at[pl.ds(row, height)], sem.at[n]))
        row += height
    for c in copies:
        c.start()
    zero = jnp.zeros((BS, BS), BF16)
    for hi, lo, at in ((ch, cl, ZERO), (sh, slo, S_CAP), (dh, dl, D_CAP), (eh, elo, E_CAP)):
        hi[at] = zero
        lo[at] = zero

    def clear(ref, n):
        @pl.loop(0, (n + MANY - 1) // MANY)
        def _(t):
            for u in range(MANY):
                ref[MANY * t + u] = jnp.zeros((BS, BS), F32)

    clear(da, head_ref[H_DB])
    clear(ea, head_ref[H_EB])
    clear(fa, NB // 8)
    for c in copies:
        c.wait()

    def prepare(n, names, rows, turn):
        @pl.loop(0, (n + MANY - 1) // MANY)
        def _(t):
            ids = [names[MANY * t + u] for u in range(MANY)]
            xs = []
            for u in range(MANY):
                word = rows[MANY * t + u]
                parts = [
                    raw[pl.ds(pl.multiple_of(at * SHARD, SHARD), SHARD), :] for at in (word & (HALF_WORD - 1), word >> 8)
                ]
                xs.append(split(turn(jnp.concatenate(parts, axis=0))))
            for a, (hi, lo) in zip(ids, xs):
                ch[a] = hi
                cl[a] = lo

    prepare(blocks_ref[0], pn_ref, an_ref, lambda v: v)
    prepare(blocks_ref[1], pt_ref, at_ref, lambda v: v.T)
    clear(sa, head_ref[H_SB])

    def phase(n, task, left, right, acc, many):
        lh, ll = left
        rh, rl = right

        @pl.loop(0, n)
        def _(t):
            for u in range(many):
                a0, a1, b0, b1, out = task(t * many + u)
                lhs = jnp.concatenate(
                    [
                        jnp.concatenate([lh[a0], lh[a1]], axis=1),
                        jnp.concatenate([ll[a0], ll[a1]], axis=1),
                    ],
                    axis=0,
                )
                rhs = jnp.concatenate(
                    [
                        jnp.concatenate([rh[b0], rl[b0]], axis=1),
                        jnp.concatenate([rh[b1], rl[b1]], axis=1),
                    ],
                    axis=0,
                )
                both = jnp.dot(lhs, rhs, preferred_element_type=F32)
                acc[out] = acc[out] + (both[:BS, :BS] + (both[:BS, BS:] + both[BS:, :BS]))

    low = lambda w: w & (WORD - 1)

    def plain(L, R):
        def task(t):
            r0 = R[2 * t]
            return low(L[2 * t]), low(L[2 * t + 1]), low(r0), low(R[2 * t + 1]), r0 >> 12

        return task

    def span(first, n_first, second, n_second):
        return lambda t: jnp.where(
            t < n_first, first + t, jnp.where(t < n_first + n_second, second + t - n_first, NOTHING)
        )

    for head, sl, sr, _, _ in listed:
        n_out, n_in = head[H_OUT], head[H_IN]
        pair = span(0, n_out, LIST // 2, n_in)

        def square(t, sl=sl, sr=sr, pair=pair):
            at = 2 * pair(t)
            r0 = sr[at]
            return low(sl[at]), low(sl[at + 1]), low(r0), low(sr[at + 1]), r0 >> 12

        phase((n_out + n_in + UNROLL - 1) // UNROLL, square, (ch, cl), (ch, cl), sa, UNROLL)

    for head, _, _, _, turn_ref in listed:

        @pl.loop(0, (head[H_TURN] + MANY - 1) // MANY)
        def _(t, turn_ref=turn_ref):
            words = [turn_ref[MANY * t + u] for u in range(MANY)]
            done = [sa[low(w)].T for w in words]
            for u in range(MANY):
                sa[words[u] >> 12] = done[u]

    @pl.loop(0, (head_ref[H_SB] + MANY - 1) // MANY)
    def _(t):
        done = [split(sa[MANY * t + u]) for u in range(MANY)]
        for u in range(MANY):
            sh[MANY * t + u], slo[MANY * t + u] = done[u]

    for head, sl, sr, _, _ in listed:
        n_in, n_again = head[H_IN], head[H_AGAIN]
        pair = span(LIST // 2, n_in, LIST, n_again)

        def cube(t, sl=sl, sr=sr, pair=pair):
            at = 2 * pair(t)
            r1 = sr[at + 1]
            return sl[at] >> 12, sl[at + 1] >> 12, low(sr[at]), low(r1), r1 >> 12

        phase((n_in + n_again + UNROLL - 1) // UNROLL, cube, (sh, slo), (ch, cl), da, UNROLL)

    start = 0
    for head, _, _, ds_ref, _ in listed:

        @pl.loop(0, (head[H_DB] - start + MANY - 1) // MANY)
        def _(t, ds_ref=ds_ref, start=start):
            at = MANY * t
            done = [split(3.0 * sa[ds_ref[at + u]] - 2.0 * da[start + at + u]) for u in range(MANY)]
            for u in range(MANY):
                dh[start + at + u], dl[start + at + u] = done[u]

        start = head[H_DB]

    phase(head_ref[H_E], plain(el, er), (dh, dl), (dh, dl), ea, UNROLL)

    @pl.loop(0, head_ref[H_EB])
    def _(t):
        eh[t], elo[t] = split(ea[t])

    phase(head_ref[H_F], plain(fl, fr), (eh, elo), (dh, dl), fa, FEW)
    for a in range(out_ref.shape[0] // BS):
        at = fin_ref[a]
        value = 3.0 * ea[jnp.maximum(at, 0)] - 2.0 * fa[a]
        out_ref[a * BS : (a + 1) * BS, :] = jnp.where(at >= 0, value.T, 0.0)


def linear(x, y, z, core):
    return (((x % 2) * NY + y) * (NZ * NC) + z * NC + core) * 2 + x // 2


def send(value, step):
    pairs = [
        (linear(x, y, z, core), linear(*step(x, y, z, core)))
        for x in range(NX)
        for y in range(NY)
        for z in range(NZ)
        for core in range(NC)
    ]
    return lax.ppermute(value, ("row", "col", "layer"), pairs)


def along_z(d):
    return lambda x, y, z, core: (x, y, (z + d) % NZ, core)


def inner(d):
    return lambda x, y, z, core: ((x + d) % NX, y, z, core) if core == 0 else (x, (y + d) % NY, z, core)


def outer(d):
    return lambda x, y, z, core: (x, (y + d) % NY, z, core) if core == 0 else ((x + d) % NX, y, z, core)


def other_core(x, y, z, core):
    return x, y, z, 1 - core


def list_blocks(plan):
    smem = pl.BlockSpec(memory_space=pltpu.SMEM)
    i32 = lambda *shape: jax.ShapeDtypeStruct(shape, jnp.int32)
    return pl.pallas_call(
        block_kernel,
        out_shape=i32(sum(BLOCK_SIZES)),
        in_specs=[smem],
        out_specs=smem,
        cost_estimate=pl.CostEstimate(flops=0, bytes_accessed=6_000_000, transcendentals=0),
        name="list_blocks",
    )(plan)


def list_first(plan):
    smem = pl.BlockSpec(memory_space=pltpu.SMEM)
    return pl.pallas_call(
        first_kernel,
        out_shape=jax.ShapeDtypeStruct((sum(FIRST_SIZES),), jnp.int32),
        in_specs=[smem],
        out_specs=smem,
        cost_estimate=pl.CostEstimate(flops=0, bytes_accessed=16_000_000, transcendentals=0),
        name="list_first",
    )(plan)


def list_second(plan, first):
    smem = pl.BlockSpec(memory_space=pltpu.SMEM)
    return pl.pallas_call(
        second_kernel,
        out_shape=jax.ShapeDtypeStruct((sum(LIST_SIZES),), jnp.int32),
        in_specs=[smem, smem],
        out_specs=smem,
        scratch_shapes=[
            pltpu.SMEM((NB * NB,), jnp.int32),
            pltpu.SMEM((NB * NB,), jnp.int32),
            pltpu.SMEM((NB,), jnp.int32),
        ],
        cost_estimate=pl.CostEstimate(flops=0, bytes_accessed=16_000_000, transcendentals=0),
        name="list_second",
    )(plan, first)


def plan_products(pattern, *owners):
    smem = pl.BlockSpec(memory_space=pltpu.SMEM)
    vmem = pl.BlockSpec(memory_space=pltpu.VMEM)
    i32 = lambda *shape: jax.ShapeDtypeStruct(shape, jnp.int32)
    return pl.pallas_call(
        plan_kernel,
        out_shape=(i32(WIDE, LANES), i32(1)),
        in_specs=[vmem] * 4,
        out_specs=(vmem, smem),
        cost_estimate=pl.CostEstimate(flops=0, bytes_accessed=10_000_000, transcendentals=0),
        name="plan_products",
    )(pattern, *owners)


def to_chips_along_z(shard):
    lines = [[z * NC + c for z in range(NZ)] for c in range(NC)]
    copies = jnp.broadcast_to(shard, (NZ, SHARD, BS))
    return lax.all_to_all(
        copies, "col", split_axis=0, concat_axis=0, tiled=True, axis_index_groups=lines
    ).reshape(UNIT, BS)


def gather_pieces(shard, pattern, owners):
    tie = lax.optimization_barrier
    swap = lambda value: send(value, other_core)
    own = to_chips_along_z(shard)
    own, owners = tie((own, owners))
    line = [own] + [send(own, inner(d)) for d in (1, -1, 2)]
    plan, ok = plan_products(pattern, *owners)
    blocks = list_blocks(plan)
    line, blocks = tie((line, blocks))

    low, high = jnp.concatenate(line[:2], axis=0), jnp.concatenate(line[2:], axis=0)
    low, high, plan = tie((low, high, plan))
    back_low, ahead_high = send(low, outer(1)), send(high, outer(-1))
    back_high, ahead_low = send(high, outer(1)), send(low, outer(-1))
    first_lists = list_first(plan)
    back_low, ahead_high, first_lists = tie((back_low, ahead_high, first_lists))
    far_low, far_high = send(back_low, outer(1)), send(ahead_high, outer(-1))
    panel = jnp.concatenate([low, high], axis=0)
    panel, back_low, ahead_high, back_high, ahead_low, first_lists = tie(
        (panel, back_low, ahead_high, back_high, ahead_low, first_lists)
    )
    second_lists = list_second(plan, first_lists)
    first = jnp.concatenate([back_low, ahead_high], axis=0)
    second = jnp.concatenate([back_high, ahead_low], axis=0)
    far_low, far_high, second_lists = tie((far_low, far_high, second_lists))
    theirs = [swap(value) for value in (panel, first, second, far_low, far_high)]
    mine = [low, high, back_low, ahead_high, back_high, ahead_low, far_low, far_high]
    return ok, [blocks, first_lists, second_lists], [*mine, *theirs]


def per_device(density, pattern):
    smem = pl.BlockSpec(memory_space=pltpu.SMEM)
    vmem = pl.BlockSpec(memory_space=pltpu.VMEM)

    square = jax.ShapeDtypeStruct((NB, NB), F32)
    packed, *owners = pl.pallas_call(
        pack_kernel,
        out_shape=(jax.ShapeDtypeStruct((CAP * BS, BS), F32), square, square, square),
        in_specs=[vmem, vmem],
        out_specs=[vmem] * 4,
        name="pack_blocks",
    )(pattern, density)

    rows = lax.axis_size("row")
    pieces = packed.reshape(rows, SHARD, BS)
    shard = jnp.sum(lax.all_to_all(pieces, "row", split_axis=0, concat_axis=0, tiled=True), axis=0)
    ok, tables, gathered = gather_pieces(shard, pattern, owners)

    def sparse(density, pattern, tables, gathered):
        block = lambda n, t: pltpu.VMEM((n, BS, BS), t)
        return pl.pallas_call(
            compute_kernel,
            out_shape=jax.ShapeDtypeStruct(density.shape, F32),
            in_specs=[smem] * len(tables) + [pl.BlockSpec(memory_space=pl.ANY)] * len(gathered),
            out_specs=vmem,
            scratch_shapes=[
                pltpu.VMEM((2 * RAW_HALF, BS), F32),
                block(ZERO + 2, BF16), block(ZERO + 2, BF16),
                block(S_CAP + 1, BF16), block(S_CAP + 1, BF16),
                block(D_CAP + 1, F32), block(D_CAP + 1, BF16), block(D_CAP + 1, BF16),
                block(E_CAP + 1, F32), block(E_CAP + 1, BF16), block(E_CAP + 1, BF16),
                block(NB // 8 + 1, F32),
                pltpu.SemaphoreType.DMA((len(gathered),)),
            ],
            compiler_params=pltpu.CompilerParams(vmem_limit_bytes=48 * 2**20),
            name="purify_column",
        )(*tables, *gathered)

    def dense(density, pattern, tables, gathered):
        return dense_plan(density, pattern)

    return lax.cond(ok[0] != 0, sparse, dense, density, pattern, tables, gathered)


def solution(mesh):
    return jax.shard_map(
        per_device,
        mesh=mesh,
        in_specs=(P("row", ("col", "layer")), P()),
        out_specs=P("row", ("col", "layer")),
        check_vma=False,
    )
```
